32 devices in a mesh: section: 4 (over z), head: 8 (over y, x, core).
Axes of the slice: x: 2, y: 2, z: 4, core: 2. Of those that a mesh axis runs over, the one named last changes fastest.
Arguments:
- hidden_in: bfloat16 [12288, 2048], P(('section', 'head')), may hold values from -3 to 3
- norm_gain: float32 [2048], replicated, may hold values from 0.1 to 1.9
- w_qkv: bfloat16 [2048, 3, 2048], P(None, None, 'head'), may hold values from -0.5 to 0.5
- w_out: bfloat16 [2048, 2048], P('head'), may hold values from -0.375 to 0.375
- block_lists: int32 [24, 12], P('section'), may hold values from -1 to 23, as said below
Outputs:
- mixed: bfloat16 [12288, 2048], P(('section', 'head'))
The draws below stay inside these ranges and needn't reach their ends.
Inputs may be any that keep to these rules, and one draw needn't show every extreme that they name: `block_lists`: row b starts with b itself, then holds 1 + b * 11 // 23 - 1 further distinct blocks below b, then -1 in every remaining slot.
All inputs are finite; a program needn't handle non-finite values.
Results may differ from the reference program's by a relative error of at most 0.015.
Values may be sent and summed in bfloat16 or wider, within the bound.
No kernel may reach another device: no remote copies, remote signals or barrier semaphores. Data moves between devices by JAX's collectives and lax.ppermute only.
A program may use at most 128 MiB of HBM per device.

```python
import math
import jax
import jax.numpy as jnp
from jax import lax

D = 2048
HEADS = 16
HD = 128
BLK = 512
KSEL = 12
NBLK = 24
SEQ = 12288


def draw_hidden_in(key, part):
    base = 0.5 * jax.random.normal(key, (SEQ, D), jnp.float32)
    return jnp.clip(base, -3.0, 3.0).astype(jnp.bfloat16)


def draw_w_qkv(key, part):
    scale = D ** (-0.5)
    base = jax.random.normal(key, (D, 3, HEADS * HD), jnp.float32) * scale
    return jnp.clip(base, -0.5, 0.5).astype(jnp.bfloat16)


def draw_block_lists(key, part):
    blocks = jnp.arange(NBLK, dtype=jnp.int32)
    counts = 1 + blocks * (KSEL - 1) // (NBLK - 1)
    scores = jax.random.randint(key, (NBLK, NBLK), 0, 2 ** 20, dtype=jnp.int32) * NBLK + blocks[None, :]
    scores = jnp.where(blocks[None, :] < blocks[:, None], scores, -1 - blocks[None, :])
    _, picks = lax.top_k(scores, KSEL - 1)
    entries = jnp.concatenate([blocks[:, None], picks.astype(jnp.int32)], axis=1)
    slots = jnp.arange(KSEL, dtype=jnp.int32)
    return jnp.where(slots[None, :] < counts[:, None], entries, -1).astype(jnp.int32)


def level_of(rng, shape, pieces, smallest, top_value):
    def one(position, parts):
        heights = jax.random.uniform(jax.random.fold_in(jax.random.fold_in(rng, 6), position), (parts,), jnp.float32, smallest / len(pieces), top_value / len(pieces))
        return jnp.repeat(jnp.exp(heights), shape[position] // parts).reshape((-1,) + (1,) * (len(shape) - position - 1))

    loudness = one(*pieces[0])
    for cut in pieces[1:]:
        loudness = loudness * one(*cut)
    return loudness


def scatter_about(key, extent, width, most, pieces=(), kind=jnp.bfloat16):
    loudness = level_of(key, extent, pieces, -0.22, 0.18) if pieces else 1.0
    values = jax.random.normal(key, extent, jnp.float32) * width * loudness
    return jnp.minimum(jnp.maximum(values, -most), most).astype(kind)


def setup_inputs(seed: int = 0) -> dict:
    seeds = jax.random.split(jax.random.key(seed), 6)
    hidden_in = draw_hidden_in(jax.random.fold_in(seeds[5], 71), 0)
    norm_gain = jnp.clip(1.0 + 0.18 * jax.random.normal(seeds[1], (D,), jnp.float32), 0.1, 1.9)
    w_qkv = draw_w_qkv(jax.random.fold_in(seeds[5], 71), 0)
    w_out = scatter_about(seeds[3], (HEADS * HD, D), (HEADS * HD // 9) ** -0.5, 0.375, ((0, 8),))
    block_lists = draw_block_lists(jax.random.fold_in(seeds[5], 71), 0)
    return {"hidden_in": hidden_in, "norm_gain": norm_gain, "w_qkv": w_qkv, "w_out": w_out, "block_lists": block_lists}


EPS = 1e-05
THETA = 10000.0

def rope_tables(positions):
    half = HD // 2
    frequency = THETA ** (-(2.0 * jnp.arange(half, dtype=jnp.float32)) / HD)
    angle = positions.astype(jnp.float32)[:, None] * frequency[None, :]
    return (jnp.cos(angle)[:, None, :], jnp.sin(angle)[:, None, :])

def rotate(vectors, cosine, sine):
    half = vectors.shape[-1] // 2
    first = vectors[..., :half]
    second = vectors[..., half:]
    return jnp.concatenate([first * cosine - second * sine, second * cosine + first * sine], axis=-1)

def reference(hidden_in, norm_gain, w_qkv, w_out, block_lists):
    resid = hidden_in.astype(jnp.float32)
    normed = (resid * lax.rsqrt(lax.optimization_barrier(jnp.mean(resid * resid, axis=-1, keepdims=True)) + EPS) * norm_gain).astype(jnp.bfloat16)
    projected = jnp.dot(normed, w_qkv.reshape(D, 3 * HEADS * HD), preferred_element_type=jnp.float32)
    projected = projected.reshape(SEQ, 3, HEADS, HD)
    cosine, sine = rope_tables(jnp.arange(SEQ, dtype=jnp.int32))
    query = rotate(projected[:, 0], cosine, sine).astype(jnp.bfloat16)
    keys = rotate(projected[:, 1], cosine, sine).astype(jnp.bfloat16)
    values = projected[:, 2].astype(jnp.bfloat16)
    scale = 1.0 / math.sqrt(HD)

    def one_block(block):
        query_rows = lax.dynamic_slice_in_dim(query, block * BLK, BLK, 0).astype(jnp.float32)
        block_row = lax.dynamic_index_in_dim(block_lists, block, 0, keepdims=False)
        safe = jnp.maximum(block_row, 0)
        key_positions = (safe[:, None] * BLK + jnp.arange(BLK, dtype=jnp.int32)[None, :]).reshape(-1).astype(jnp.int32)
        key_rows = keys[key_positions].astype(jnp.float32)
        value_rows = values[key_positions].astype(jnp.float32)
        scores = jnp.einsum('qhd,khd->hqk', query_rows, key_rows) * scale
        query_positions = block * BLK + jnp.arange(BLK, dtype=jnp.int32)
        live = jnp.repeat(block_row >= 0, BLK)
        allowed = live[None, :] & (key_positions[None, :] <= query_positions[:, None])
        scores = jnp.where(allowed[None], scores, -jnp.inf)
        highest = lax.optimization_barrier(jnp.max(scores, axis=-1, keepdims=True))
        weights = jnp.exp(scores - highest)
        total = lax.optimization_barrier(jnp.sum(weights, axis=-1, keepdims=True))
        rounded = lax.optimization_barrier(weights.astype(jnp.bfloat16)).astype(jnp.float32)
        summed = jnp.einsum('hqk,khd->hqd', rounded, value_rows) / total
        return jnp.transpose(summed, (1, 0, 2)).reshape(BLK, HEADS * HD).astype(jnp.bfloat16)
    attended = lax.map(one_block, jnp.arange(NBLK, dtype=jnp.int32)).reshape(SEQ, HEADS * HD)
    output = resid + jnp.dot(attended, w_out, preferred_element_type=jnp.float32)
    return output.astype(jnp.bfloat16)
```

```python
import functools
import math

import jax
import jax.numpy as jnp
from jax import lax
from jax.experimental import pallas as pl
from jax.experimental.pallas import tpu as pltpu
from jax.sharding import PartitionSpec as P

D = 2048
HD = 128
BLK = 512
TILE = 128


EPS = 1e-05
THETA = 10000.0
VMEM_LIMIT = 56 * 1024 * 1024


def rotate(vectors, cosine, sine):
    half = vectors.shape[-1] // 2
    first = vectors[..., :half]
    second = vectors[..., half:]
    return jnp.concatenate(
        [first * cosine - second * sine, second * cosine + first * sine], axis=-1
    )


def general(hidden_in, norm_gain, w_qkv, w_out, block_lists):
    section_id = lax.axis_index("section")
    width = w_qkv.shape[2]
    heads_here = width // HD
    blocks_here = block_lists.shape[0]
    tok_dev = blocks_here * BLK
    scale = 1.0 / math.sqrt(HD)
    resid = hidden_in.astype(jnp.float32)
    normed = (
        resid * lax.rsqrt(jnp.mean(resid * resid, axis=-1, keepdims=True) + EPS) * norm_gain
    ).astype(jnp.bfloat16)
    flat_weight = w_qkv.reshape(D, 3 * width)
    frequency = THETA ** (-(2.0 * jnp.arange(HD // 2, dtype=jnp.float32)) / HD)
    piece = lax.all_gather(normed, "head", axis=0, tiled=True)
    count = piece.shape[0]
    mixed_rows = jnp.dot(piece, flat_weight, preferred_element_type=jnp.float32).reshape(
        count, 3, heads_here, HD
    )
    positions = (section_id * tok_dev + jnp.arange(count, dtype=jnp.int32)).astype(jnp.float32)
    angle = positions[:, None] * frequency[None, :]
    cosine = jnp.cos(angle)[:, None, :]
    sine = jnp.sin(angle)[:, None, :]
    query = rotate(mixed_rows[:, 0], cosine, sine).astype(jnp.bfloat16).reshape(count, width)
    keys = rotate(mixed_rows[:, 1], cosine, sine).astype(jnp.bfloat16).reshape(count, width)
    values = mixed_rows[:, 2].astype(jnp.bfloat16).reshape(count, width)
    keys_all, values_all = (
        lax.all_gather(keys, "section", axis=0, tiled=True),
        lax.all_gather(values, "section", axis=0, tiled=True),
    )
    count_blocks = block_lists.shape[0]
    query_blocks = query.reshape(count_blocks, BLK, heads_here, HD)
    block_ids = section_id * blocks_here + jnp.arange(count_blocks, dtype=jnp.int32)

    def one_block(carry, item):
        query_block, block_row, block_id = item
        live_slots = jnp.sum((block_row >= 0).astype(jnp.int32))
        query_positions = block_id * BLK + jnp.arange(BLK, dtype=jnp.int32)

        def one_slot(slot, state):
            highest, total, weighted = state
            source = block_row[slot]
            key_block = lax.dynamic_slice_in_dim(keys_all, source * BLK, BLK, 0).reshape(
                BLK, heads_here, HD
            )
            value_block = lax.dynamic_slice_in_dim(values_all, source * BLK, BLK, 0).reshape(
                BLK, heads_here, HD
            )
            scores = (
                jnp.einsum(
                    "qhd,khd->hqk", query_block, key_block, preferred_element_type=jnp.float32
                )
                * scale
            )
            key_positions = source * BLK + jnp.arange(BLK, dtype=jnp.int32)
            scores = jnp.where(
                key_positions[None, None, :] <= query_positions[None, :, None], scores, -jnp.inf
            )
            new_highest = jnp.maximum(highest, jnp.max(scores, axis=-1))
            factor = jnp.exp(highest - new_highest)
            weights = jnp.exp(scores - new_highest[..., None])
            total = total * factor + jnp.sum(weights, axis=-1)
            update = jnp.einsum(
                "hqk,khd->hqd",
                weights.astype(jnp.bfloat16),
                value_block,
                preferred_element_type=jnp.float32,
            )
            weighted = weighted * factor[..., None] + update
            return (new_highest, total, weighted)

        start_state = (
            jnp.full((heads_here, BLK), -jnp.inf, jnp.float32),
            jnp.zeros((heads_here, BLK), jnp.float32),
            jnp.zeros((heads_here, BLK, HD), jnp.float32),
        )
        highest, total, weighted = lax.fori_loop(0, live_slots, one_slot, start_state)
        result = (
            (weighted / total[..., None])
            .transpose(1, 0, 2)
            .reshape(BLK, width)
            .astype(jnp.bfloat16)
        )
        return (carry, result)

    _, results = lax.scan(
        one_block, jnp.zeros((), jnp.int32), (query_blocks, block_lists, block_ids)
    )
    attended = results.reshape(count_blocks * BLK, width)
    regrouped = lax.all_to_all(attended, "head", split_axis=0, concat_axis=1, tiled=True)
    summed = jnp.dot(
        regrouped,
        lax.all_gather(w_out, "head", axis=0, tiled=True),
        preferred_element_type=jnp.float32,
    )
    return (resid + summed).astype(jnp.bfloat16)


def project_kernel(place, first, second, own, other, cosine, sine, *rest):
    outs, (rows, weights, results, row_sems, weight_sems, out_sems) = rest[:4], rest[4:]
    half = first.shape[0]
    width = own.shape[1] // 3
    row_copies = [
        pltpu.make_async_copy(ref, rows.at[pl.ds(i * half, half)], row_sems.at[i])
        for i, ref in enumerate((first, second))
    ]
    weight_copies = [
        pltpu.make_async_copy(
            ref.at[:, pl.ds(part * width, width)],
            weights.at[w * 3 + part],
            weight_sems.at[w * 3 + part],
        )
        for w, ref in enumerate((own, other))
        for part in range(3)
    ]
    for copy in row_copies + weight_copies:
        copy.start()
    for copy in row_copies:
        copy.wait()
    query_scale = math.log2(math.e) / math.sqrt(HD)
    for w in range(2):
        for part in range(3):
            weight_copies[w * 3 + part].wait()
            product = jnp.dot(
                rows[...], weights[w * 3 + part], preferred_element_type=jnp.float32
            )
            for h in range(2):
                vector = product[:, h * HD : (h + 1) * HD]
                if part < 2:
                    vector = vector * cosine[...] + pltpu.roll(vector, HD // 2, 1) * sine[...]
                if part == 0:
                    vector = vector * query_scale
                results[w * 2 + h, :, part * HD : (part + 1) * HD] = vector.astype(jnp.bfloat16)
    copies = [
        pltpu.make_async_copy(results.at[place[shift]], outs[shift], out_sems.at[shift])
        for shift in range(4)
    ]
    for copy in copies:
        copy.start()
    for copy in copies:
        copy.wait()


def project(place, first, second, own, other, cosine, sine):
    half = first.shape[0]
    count = 2 * half
    width = own.shape[1] // 3
    any_space = pl.BlockSpec(memory_space=pl.ANY)
    vmem = pl.BlockSpec(memory_space=pltpu.VMEM)
    return pl.pallas_call(
        project_kernel,
        out_shape=[jax.ShapeDtypeStruct((count, 3 * HD), jnp.bfloat16)] * 4,
        in_specs=[pl.BlockSpec(memory_space=pltpu.SMEM)] + [any_space] * 4 + [vmem] * 2,
        out_specs=[any_space] * 4,
        scratch_shapes=[
            pltpu.VMEM((count, D), jnp.bfloat16),
            pltpu.VMEM((6, D, width), jnp.bfloat16),
            pltpu.VMEM((4, count, 3 * HD), jnp.bfloat16),
            pltpu.SemaphoreType.DMA((2,)),
            pltpu.SemaphoreType.DMA((6,)),
            pltpu.SemaphoreType.DMA((4,)),
        ],
        compiler_params=pltpu.CompilerParams(vmem_limit_bytes=VMEM_LIMIT),
        cost_estimate=pl.CostEstimate(
            flops=2 * count * D * 6 * width, bytes_accessed=2 * 6 * D * width, transcendentals=0
        ),
        name="project_and_rotate",
    )(place, first, second, own, other, cosine, sine)


def attend_kernel(blocks_here, place, *rest):
    lists, pieces, out = rest[:4], rest[4:36], rest[36]
    rows, values_t, sems = rest[37:]
    section, chip, core = place[0], place[1], place[2]
    half = pieces[0].shape[0] // 2
    tok = blocks_here * BLK
    total_blocks = 4 * blocks_here
    copies = []
    for chunk in range(4):
        for shift in range(4):
            for far in range(2):
                number = (chunk * 4 + shift) * 2 + far
                source = lax.rem(section - shift + 4, 4)
                side = core if far == 0 else 1 - core
                for part in range(2):
                    if chunk == 0:
                        relative, which = 0, part
                    elif chunk == 3:
                        relative, which = 3, part
                    else:
                        relative, which = 1 + part, chunk - 1
                    owner = chip ^ relative
                    start = source * tok + owner * (4 * half) + side * (2 * half) + which * half
                    copies.append(
                        pltpu.make_async_copy(
                            pieces[number].at[pl.ds(part * half, half)],
                            rows.at[pl.ds(pl.multiple_of(start, half), half)],
                            sems.at[number * 2 + part],
                        )
                    )
    for copy in copies:
        copy.start()
    for copy in copies:
        copy.wait()

    def turn(i, carry):
        at = pl.multiple_of(i * BLK, BLK)
        values_t[:, pl.ds(at, BLK)] = rows[pl.ds(at, BLK), 2 * HD : 3 * HD].T
        return carry

    lax.fori_loop(0, total_blocks, turn, 0)

    lane = lax.broadcasted_iota(jnp.int32, (BLK, 2 * TILE), 1)
    key_at = lax.broadcasted_iota(jnp.int32, (BLK, 2 * TILE), 0)

    for shift in range(4):
        target = lax.rem(section + shift, 4)
        block_list = lists[(4 - shift) % 4]

        def one_block(local, carry, shift=shift, target=target, block_list=block_list):
            block = target * blocks_here + local
            middle = lax.rem(local, 3) == 1
            offset = jnp.where(middle, core * TILE, core * 2 * TILE)
            gap = jnp.where(middle, TILE, 0)
            start = pl.multiple_of(block * BLK + offset, TILE)
            later = pl.multiple_of(start + TILE + gap, TILE)
            query = jnp.concatenate(
                [rows[pl.ds(start, TILE), 0:HD], rows[pl.ds(later, TILE), 0:HD]], axis=0
            )
            live = jnp.int32(0)
            for slot in range(block_list.shape[1]):
                live = live + (block_list[local, slot] >= 0).astype(jnp.int32)

            def scores_of(source):
                at = pl.multiple_of(source * BLK, BLK)
                return lax.dot_general(
                    rows[pl.ds(at, BLK), HD : 2 * HD],
                    query,
                    (((1,), (1,)), ((), ())),
                    preferred_element_type=jnp.float32,
                )

            def weigh(source, weights):
                at = pl.multiple_of(source * BLK, BLK)
                return jnp.dot(
                    values_t[:, pl.ds(at, BLK)],
                    weights.astype(jnp.bfloat16),
                    preferred_element_type=jnp.float32,
                )

            query_at = offset + lane + jnp.where(lane >= TILE, gap, 0)
            scores = jnp.where(key_at <= query_at, scores_of(block), -jnp.inf)
            highest = jnp.max(scores, axis=0, keepdims=True)
            weights = jnp.exp2(scores - highest)
            total = jnp.sum(weights, axis=0, keepdims=True)
            weighted = weigh(block, weights)

            def one_slot(slot, state):
                highest, total, weighted = state
                source = block_list[local, slot]
                scores = scores_of(source)
                new_highest = jnp.maximum(highest, jnp.max(scores, axis=0, keepdims=True))
                factor = jnp.exp2(highest - new_highest)
                weights = jnp.exp2(scores - new_highest)
                total = total * factor + jnp.sum(weights, axis=0, keepdims=True)
                weighted = weighted * factor + weigh(source, weights)
                return (new_highest, total, weighted)

            _, total, weighted = lax.fori_loop(1, live, one_slot, (highest, total, weighted))
            result = (weighted / total).T.astype(jnp.bfloat16)
            for part in range(2):
                tile = 2 * local + part
                owner = tile // 3
                where = (owner ^ chip) * 3 + lax.rem(tile, 3)
                out[shift, where] = result[part * TILE : (part + 1) * TILE]
            return carry

        lax.fori_loop(0, blocks_here, one_block, 0)


def attend(place, lists, pieces):
    blocks_here = lists[0].shape[0]
    tokens = 4 * blocks_here * BLK
    tiles = blocks_here * 2
    smem = pl.BlockSpec(memory_space=pltpu.SMEM)
    pairs = tokens // BLK * lists[0].shape[1] // 2
    return pl.pallas_call(
        functools.partial(attend_kernel, blocks_here),
        out_shape=jax.ShapeDtypeStruct((4, tiles, TILE, HD), jnp.bfloat16),
        in_specs=[smem] * 5 + [pl.BlockSpec(memory_space=pl.ANY)] * 32,
        out_specs=pl.BlockSpec(memory_space=pltpu.VMEM),
        scratch_shapes=[
            pltpu.VMEM((tokens, 3 * HD), jnp.bfloat16),
            pltpu.VMEM((HD, tokens), jnp.bfloat16),
            pltpu.SemaphoreType.DMA((64,)),
        ],
        compiler_params=pltpu.CompilerParams(vmem_limit_bytes=VMEM_LIMIT),
        cost_estimate=pl.CostEstimate(
            flops=pairs * 4 * BLK * 2 * TILE * HD,
            bytes_accessed=tokens * 10 * HD,
            transcendentals=pairs * BLK * 2 * TILE,
        ),
        name="attend_one_head",
    )(place, *lists, *pieces)


def finish_kernel(place, *rest):
    parts, swapped, w_out, hidden, out = rest[:4], rest[4], rest[5], rest[6], rest[7]
    attended, sems, swap_sems = rest[8:]
    section, chip, core = place[0], place[1], place[2]
    odd = lax.rem(chip, 2)

    @pl.when(pl.program_id(0) == 0)
    def _():
        copies = []
        for relative in range(4):
            for shift in range(4):
                head = (chip ^ relative) * 4 + lax.rem(section - shift + 4, 4)
                column = pl.ds(pl.multiple_of(head * HD, HD), HD)
                number = relative * 4 + shift
                for kept in range(2):
                    tile = kept + core
                    to = jnp.where(
                        core == 0, kept * (1 + odd), jnp.where(kept == 0, odd, 2)
                    )
                    copies.append(
                        pltpu.make_async_copy(
                            parts[relative].at[shift, tile],
                            attended.at[pl.ds(pl.multiple_of(to * TILE, TILE), TILE), column],
                            sems.at[number * 2 + kept],
                        )
                    )
                to = jnp.where(core == 0, 2 - odd, 1 - odd)
                copies.append(
                    pltpu.make_async_copy(
                        swapped.at[relative, shift],
                        attended.at[pl.ds(pl.multiple_of(to * TILE, TILE), TILE), column],
                        swap_sems.at[number],
                    )
                )
        for copy in copies:
            copy.start()
        for copy in copies:
            copy.wait()

    summed = jnp.dot(attended[...], w_out[...], preferred_element_type=jnp.float32)
    out[...] = (hidden[...].astype(jnp.float32) + summed).astype(jnp.bfloat16)


def finish(place, parts, swapped, w_out, hidden):
    count = hidden.shape[0]
    step = 256
    any_space = pl.BlockSpec(memory_space=pl.ANY)
    return pl.pallas_call(
        finish_kernel,
        out_shape=jax.ShapeDtypeStruct((count, D), jnp.bfloat16),
        grid=(D // step,),
        in_specs=[pl.BlockSpec(memory_space=pltpu.SMEM)]
        + [any_space] * 5
        + [
            pl.BlockSpec((D, step), lambda i: (0, i)),
            pl.BlockSpec((count, step), lambda i: (0, i)),
        ],
        out_specs=pl.BlockSpec((count, step), lambda i: (0, i)),
        scratch_shapes=[
            pltpu.VMEM((count, D), jnp.bfloat16),
            pltpu.SemaphoreType.DMA((32,)),
            pltpu.SemaphoreType.DMA((16,)),
        ],
        compiler_params=pltpu.CompilerParams(
            vmem_limit_bytes=VMEM_LIMIT, dimension_semantics=("arbitrary",)
        ),
        cost_estimate=pl.CostEstimate(
            flops=2 * count * D * D, bytes_accessed=2 * D * D, transcendentals=0
        ),
        name="project_out",
    )(place, *parts, swapped, w_out, hidden)


def by_head(hidden_in, norm_gain, w_qkv, w_out, block_lists):
    section = lax.axis_index("section")
    device = lax.axis_index("head")
    chip, core = device // 2, device % 2
    width = w_qkv.shape[2]
    blocks_here = block_lists.shape[0]
    tok = blocks_here * BLK
    rows = hidden_in.shape[0]
    half = rows // 2

    other_core = [(i, i ^ 1) for i in range(8)]
    along_x = [(i, i ^ 2) for i in range(8)]
    along_y = [(i, i ^ 4) for i in range(8)]
    diagonal = [(i, i ^ 6) for i in range(8)]

    def to_section(array, shift):
        return lax.ppermute(array, "section", [(i, (i + shift) % 4) for i in range(4)])

    place = jnp.stack([section, chip, core]).astype(jnp.int32)
    shifts = jnp.arange(4, dtype=jnp.int32)
    chosen = (section + shifts - 2 * core + 4) % 4

    own = w_qkv.reshape(D, 3 * width)
    other = lax.ppermute(own, "head", other_core)
    lists = [block_lists] + [to_section(block_lists, shift) for shift in range(1, 4)]

    resid = hidden_in.astype(jnp.float32)
    normed = (
        resid * lax.rsqrt(jnp.mean(resid * resid, axis=-1, keepdims=True) + EPS) * norm_gain
    ).astype(jnp.bfloat16)
    low, high = normed[:half], normed[half:]
    x_low = lax.ppermute(low, "head", along_x)
    y_low = lax.ppermute(low, "head", along_y)
    x_high = lax.ppermute(high, "head", along_x)
    y_high = lax.ppermute(high, "head", along_y)
    d_low = lax.ppermute(y_low, "head", along_x)
    d_high = lax.ppermute(x_high, "head", along_y)
    chunks = [(low, high), (x_low, y_low), (x_high, y_high), (d_low, d_high)]
    origins = [
        ((0, 0), (0, 1)),
        ((1, 0), (2, 0)),
        ((1, 1), (2, 1)),
        ((3, 0), (3, 1)),
    ]

    frequency = THETA ** (-(2.0 * jnp.arange(HD // 2, dtype=jnp.float32)) / HD)
    starts = jnp.stack(
        [
            section * tok + (chip ^ relative) * (2 * rows) + core * rows + which * half
            for chunk in origins
            for relative, which in chunk
        ]
    )
    positions = (starts[:, None] + jnp.arange(half, dtype=jnp.int32)[None, :]).reshape(4, rows)
    angle = positions.astype(jnp.float32)[:, :, None] * frequency
    cosine, sine = jnp.cos(angle), jnp.sin(angle)
    cosine = jnp.concatenate([cosine, cosine], axis=-1)
    sine = jnp.concatenate([-sine, sine], axis=-1)

    pieces = []
    for number, (first, second) in enumerate(chunks):
        outs = project(chosen, first, second, own, other, cosine[number], sine[number])
        for shift in range(4):
            arrived = outs[shift] if shift == 0 else to_section(outs[shift], shift)
            pieces += [arrived, lax.ppermute(arrived, "head", other_core)]

    late_w_out, _, _ = lax.optimization_barrier((w_out, d_low, d_high))
    w_out_all = lax.all_gather(late_w_out, "head", axis=0, tiled=True)

    attended = attend(place, lists, pieces)
    back = [attended[0]] + [to_section(attended[shift], shift) for shift in range(1, 4)]
    back = jnp.stack(back).reshape(4, 4, 3, TILE, HD)
    parts = [back[:, 0]] + [
        lax.ppermute(back[:, relative], "head", perm)
        for relative, perm in ((1, along_x), (2, along_y), (3, diagonal))
    ]
    given = jnp.where(core == 0, 2, 0)
    swapped = lax.ppermute(
        jnp.stack([lax.dynamic_index_in_dim(part, given, 1, keepdims=False) for part in parts]),
        "head",
        other_core,
    )
    return finish(place, parts, swapped, w_out_all, hidden_in)


def solution(mesh):
    placed = (
        P(("section", "head"), None),
        P(),
        P(None, None, "head"),
        P("head", None),
        P("section", None),
    )

    def local(hidden_in, norm_gain, w_qkv, w_out, block_lists):
        fits = (
            mesh.shape["section"] == 4
            and mesh.shape["head"] == 8
            and w_qkv.shape[2] == 2 * HD
            and block_lists.shape[0] % 6 == 0
        )
        form = by_head if fits else general
        return form(hidden_in, norm_gain, w_qkv, w_out, block_lists)

    return jax.shard_map(
        local, mesh=mesh, in_specs=placed, out_specs=P(("section", "head"), None), check_vma=False
    )
```

```python
import functools
import math

import jax
import jax.numpy as jnp
from jax import lax
from jax.experimental import pallas as pl
from jax.experimental.pallas import tpu as pltpu
from jax.sharding import PartitionSpec as P

D = 2048
HD = 128
BLK = 512
TILE = 128
STEP = 12


EPS = 1e-05
THETA = 10000.0
VMEM_LIMIT = 56 * 1024 * 1024


def rotate(vectors, cosine, sine):
    half = vectors.shape[-1] // 2
    first = vectors[..., :half]
    second = vectors[..., half:]
    return jnp.concatenate(
        [first * cosine - second * sine, second * cosine + first * sine], axis=-1
    )


def general(hidden_in, norm_gain, w_qkv, w_out, block_lists):
    section_id = lax.axis_index("section")
    width = w_qkv.shape[2]
    heads_here = width // HD
    blocks_here = block_lists.shape[0]
    tok_dev = blocks_here * BLK
    scale = 1.0 / math.sqrt(HD)
    resid = hidden_in.astype(jnp.float32)
    normed = (
        resid * lax.rsqrt(jnp.mean(resid * resid, axis=-1, keepdims=True) + EPS) * norm_gain
    ).astype(jnp.bfloat16)
    flat_weight = w_qkv.reshape(D, 3 * width)
    frequency = THETA ** (-(2.0 * jnp.arange(HD // 2, dtype=jnp.float32)) / HD)
    piece = lax.all_gather(normed, "head", axis=0, tiled=True)
    count = piece.shape[0]
    mixed_rows = jnp.dot(piece, flat_weight, preferred_element_type=jnp.float32).reshape(
        count, 3, heads_here, HD
    )
    positions = (section_id * tok_dev + jnp.arange(count, dtype=jnp.int32)).astype(jnp.float32)
    angle = positions[:, None] * frequency[None, :]
    cosine = jnp.cos(angle)[:, None, :]
    sine = jnp.sin(angle)[:, None, :]
    query = rotate(mixed_rows[:, 0], cosine, sine).astype(jnp.bfloat16).reshape(count, width)
    keys = rotate(mixed_rows[:, 1], cosine, sine).astype(jnp.bfloat16).reshape(count, width)
    values = mixed_rows[:, 2].astype(jnp.bfloat16).reshape(count, width)
    keys_all, values_all = (
        lax.all_gather(keys, "section", axis=0, tiled=True),
        lax.all_gather(values, "section", axis=0, tiled=True),
    )
    count_blocks = block_lists.shape[0]
    query_blocks = query.reshape(count_blocks, BLK, heads_here, HD)
    block_ids = section_id * blocks_here + jnp.arange(count_blocks, dtype=jnp.int32)

    def one_block(carry, item):
        query_block, block_row, block_id = item
        live_slots = jnp.sum((block_row >= 0).astype(jnp.int32))
        query_positions = block_id * BLK + jnp.arange(BLK, dtype=jnp.int32)

        def one_slot(slot, state):
            highest, total, weighted = state
            source = block_row[slot]
            key_block = lax.dynamic_slice_in_dim(keys_all, source * BLK, BLK, 0).reshape(
                BLK, heads_here, HD
            )
            value_block = lax.dynamic_slice_in_dim(values_all, source * BLK, BLK, 0).reshape(
                BLK, heads_here, HD
            )
            scores = (
                jnp.einsum(
                    "qhd,khd->hqk", query_block, key_block, preferred_element_type=jnp.float32
                )
                * scale
            )
            key_positions = source * BLK + jnp.arange(BLK, dtype=jnp.int32)
            scores = jnp.where(
                key_positions[None, None, :] <= query_positions[None, :, None], scores, -jnp.inf
            )
            new_highest = jnp.maximum(highest, jnp.max(scores, axis=-1))
            factor = jnp.exp(highest - new_highest)
            weights = jnp.exp(scores - new_highest[..., None])
            total = total * factor + jnp.sum(weights, axis=-1)
            update = jnp.einsum(
                "hqk,khd->hqd",
                weights.astype(jnp.bfloat16),
                value_block,
                preferred_element_type=jnp.float32,
            )
            weighted = weighted * factor[..., None] + update
            return (new_highest, total, weighted)

        start_state = (
            jnp.full((heads_here, BLK), -jnp.inf, jnp.float32),
            jnp.zeros((heads_here, BLK), jnp.float32),
            jnp.zeros((heads_here, BLK, HD), jnp.float32),
        )
        highest, total, weighted = lax.fori_loop(0, live_slots, one_slot, start_state)
        result = (
            (weighted / total[..., None])
            .transpose(1, 0, 2)
            .reshape(BLK, width)
            .astype(jnp.bfloat16)
        )
        return (carry, result)

    _, results = lax.scan(
        one_block, jnp.zeros((), jnp.int32), (query_blocks, block_lists, block_ids)
    )
    attended = results.reshape(count_blocks * BLK, width)
    regrouped = lax.all_to_all(attended, "head", split_axis=0, concat_axis=1, tiled=True)
    summed = jnp.dot(
        regrouped,
        lax.all_gather(w_out, "head", axis=0, tiled=True),
        preferred_element_type=jnp.float32,
    )
    return (resid + summed).astype(jnp.bfloat16)


def project_kernel(place, first, second, own, other, cosine, sine, *rest):
    outs, (rows, weights, results, row_sems, weight_sems, out_sems) = rest[:4], rest[4:]
    half = first.shape[0]
    count = rows.shape[0]
    row_copies = [
        pltpu.make_async_copy(ref, rows.at[pl.ds(i * half, half)], row_sems.at[i])
        for i, ref in enumerate((first, second))
    ]
    weight_copies = [
        pltpu.make_async_copy(
            ref.at[part],
            weights.at[w * 3 + part],
            weight_sems.at[w * 3 + part],
        )
        for w, ref in enumerate((own, other))
        for part in range(3)
    ]
    for copy in row_copies + weight_copies:
        copy.start()
    for copy in row_copies:
        copy.wait()
    query_scale = math.log2(math.e) / math.sqrt(HD)
    for w in range(2):
        for part in range(3):
            weight_copies[w * 3 + part].wait()
            for at in range(0, count, half):
                piece = slice(at, at + half)
                product = jnp.dot(
                    rows[piece], weights[w * 3 + part], preferred_element_type=jnp.float32
                )
                for h in range(2):
                    vector = product[:, h * HD : (h + 1) * HD]
                    if part < 2:
                        turned = pltpu.roll(vector, HD // 2, 1)
                        vector = vector * cosine[piece] + turned * sine[piece]
                    if part == 0:
                        vector = vector * query_scale
                    column = slice(part * HD, (part + 1) * HD)
                    results[w * 2 + h, piece, column] = vector.astype(jnp.bfloat16)
    copies = [
        pltpu.make_async_copy(results.at[place[shift]], outs[shift], out_sems.at[shift])
        for shift in range(4)
    ]
    for copy in copies:
        copy.start()
    for copy in copies:
        copy.wait()


def project(place, first, second, own, other, cosine, sine):
    half = first.shape[0]
    count = 2 * half
    width = own.shape[2]
    any_space = pl.BlockSpec(memory_space=pl.ANY)
    vmem = pl.BlockSpec(memory_space=pltpu.VMEM)
    return pl.pallas_call(
        project_kernel,
        out_shape=[jax.ShapeDtypeStruct((count, 3 * HD), jnp.bfloat16)] * 4,
        in_specs=[pl.BlockSpec(memory_space=pltpu.SMEM)] + [any_space] * 4 + [vmem] * 2,
        out_specs=[any_space] * 4,
        scratch_shapes=[
            pltpu.VMEM((count, D), jnp.bfloat16),
            pltpu.VMEM((6, D, width), jnp.bfloat16),
            pltpu.VMEM((4, count, 3 * HD), jnp.bfloat16),
            pltpu.SemaphoreType.DMA((2,)),
            pltpu.SemaphoreType.DMA((6,)),
            pltpu.SemaphoreType.DMA((4,)),
        ],
        compiler_params=pltpu.CompilerParams(vmem_limit_bytes=VMEM_LIMIT),
        cost_estimate=pl.CostEstimate(
            flops=2 * count * D * 6 * width, bytes_accessed=2 * 6 * D * width, transcendentals=0
        ),
        name="project_and_rotate",
    )(place, first, second, own, other, cosine, sine)


def attend_kernel(blocks_here, place, *rest):
    lists, pieces, out = rest[:4], rest[4:36], rest[36]
    rows, values_t, queries, tops, sums, item_q, item_k, sems = rest[37:]
    section, chip, core = place[0], place[1], place[2]
    half = pieces[0].shape[0] // 2
    tok = blocks_here * BLK
    total_blocks = 4 * blocks_here
    slots = lists[0].shape[1]
    wide = 2 * TILE
    copies = []
    for chunk in range(4):
        for shift in range(4):
            for far in range(2):
                number = (chunk * 4 + shift) * 2 + far
                source = lax.rem(section - shift + 4, 4)
                side = core if far == 0 else 1 - core
                for part in range(2):
                    if chunk == 0:
                        relative, which = 0, part
                    elif chunk == 3:
                        relative, which = 3, part
                    else:
                        relative, which = 1 + part, chunk - 1
                    owner = chip ^ relative
                    start = source * tok + owner * (4 * half) + side * (2 * half) + which * half
                    copies.append(
                        pltpu.make_async_copy(
                            pieces[number].at[pl.ds(part * half, half)],
                            rows.at[pl.ds(pl.multiple_of(start, half), half)],
                            sems.at[number * 2 + part],
                        )
                    )
    for copy in copies:
        copy.start()

    count = jnp.int32(0)
    for shift in range(4):
        block_list = lists[(4 - shift) % 4]
        first_block = lax.rem(section + shift, 4) * blocks_here

        def note(local, count, block_list=block_list, first_block=first_block):
            for slot in range(1, slots):
                source = block_list[local, slot]
                item_q[count] = first_block + local
                item_k[count] = source
                count = count + (source >= 0).astype(jnp.int32)
            return count

        count = lax.fori_loop(0, blocks_here, note, count)
    for extra in range(STEP):
        item_q[count + extra] = total_blocks
        item_k[count + extra] = 0

    values_t[HD:, :] = jnp.ones((values_t.shape[0] - HD, values_t.shape[1]), jnp.bfloat16)
    queries[total_blocks] = jnp.zeros((wide, HD), jnp.bfloat16)
    tops[total_blocks] = jnp.zeros((8, wide), jnp.float32)
    sums[total_blocks] = jnp.zeros(sums.shape[1:], jnp.float32)
    for copy in copies:
        copy.wait()

    lane = lax.broadcasted_iota(jnp.int32, (BLK, wide), 1)
    key_at = lax.broadcasted_iota(jnp.int32, (BLK, wide), 0)

    def query_place(local):
        middle = lax.rem(local, 3) == 1
        offset = jnp.where(middle, core * TILE, core * wide)
        return offset, jnp.where(middle, TILE, 0)

    def scores_of(source, query):
        at = pl.multiple_of(source * BLK, BLK)
        return lax.dot_general(
            rows[pl.ds(at, BLK), HD : 2 * HD],
            query,
            (((1,), (1,)), ((), ())),
            preferred_element_type=jnp.float32,
        )

    def weigh(source, weights):
        at = pl.multiple_of(source * BLK, BLK)
        return jnp.dot(
            values_t[:, pl.ds(at, BLK)],
            weights.astype(jnp.bfloat16),
            preferred_element_type=jnp.float32,
        )

    def masked(local, scores):
        offset, gap = query_place(local)
        query_at = offset + lane + jnp.where(lane >= TILE, gap, 0)
        return jnp.where(key_at <= query_at, scores, -jnp.inf)

    def diagonal(step, carry):
        blocks = [step * 4 + i for i in range(4)]
        scores = []
        for block in blocks:
            local = lax.rem(block, blocks_here)
            at = pl.multiple_of(block * BLK, BLK)
            values_t[:HD, pl.ds(at, BLK)] = rows[pl.ds(at, BLK), 2 * HD : 3 * HD].T
            offset, gap = query_place(local)
            start = pl.multiple_of(block * BLK + offset, TILE)
            later = pl.multiple_of(start + TILE + gap, TILE)
            query = jnp.concatenate(
                [rows[pl.ds(start, TILE), 0:HD], rows[pl.ds(later, TILE), 0:HD]], axis=0
            )
            queries[block] = query
            scores.append(scores_of(block, query))
        for block, score in zip(blocks, scores):
            score = masked(lax.rem(block, blocks_here), score)
            top = jnp.max(score, axis=0, keepdims=True)
            tops[block] = jnp.broadcast_to(top, (8, wide))
            sums[block] = weigh(block, jnp.exp2(score - top))
        return carry

    lax.fori_loop(0, total_blocks // 4, diagonal, 0)

    def below(step, carry):
        items = [step * STEP + i for i in range(STEP)]
        scores = scores_of(item_k[items[0]], queries[item_q[items[0]]])
        held = None
        for i, item in enumerate(items):
            if i + 1 < STEP:
                ahead = scores_of(item_k[items[i + 1]], queries[item_q[items[i + 1]]])
            weights = jnp.exp2(scores - tops[item_q[item], 0:1]).astype(jnp.bfloat16)
            if held is not None:
                sums[item_q[items[i - 1]]] += weigh(item_k[items[i - 1]], held)
            held, scores = weights, ahead
        sums[item_q[items[-1]]] += weigh(item_k[items[-1]], held)
        return carry

    lax.fori_loop(0, (count + STEP - 1) // STEP, below, 0)

    def store(block, result):
        local = lax.rem(block, blocks_here)
        shift = lax.rem(block // blocks_here - section + 4, 4)
        for part in range(2):
            tile = 2 * local + part
            where = ((tile // 3) ^ chip) * 3 + lax.rem(tile, 3)
            out[shift, where] = result[part * TILE : (part + 1) * TILE]

    def leave(step, over):
        for i in range(4):
            block = step * 4 + i
            total = sums[block, HD : HD + 1]
            over = jnp.maximum(over, jnp.where(total < 2.0**100, 0.0, 1.0))
            store(block, (sums[block, 0:HD] / total).T.astype(jnp.bfloat16))
        return over

    over = lax.fori_loop(0, total_blocks // 4, leave, jnp.zeros((1, wide), jnp.float32))

    @pl.when(jnp.max(over) > 0)
    def _():
        for shift in range(4):
            block_list = lists[(4 - shift) % 4]
            first_block = lax.rem(section + shift, 4) * blocks_here

            def one_block(local, carry, block_list=block_list, first_block=first_block):
                block = first_block + local
                query = queries[block]
                live = jnp.int32(0)
                for slot in range(slots):
                    live = live + (block_list[local, slot] >= 0).astype(jnp.int32)
                scores = masked(local, scores_of(block, query))
                highest = jnp.max(scores, axis=0, keepdims=True)
                weighted = weigh(block, jnp.exp2(scores - highest))

                def one_slot(slot, state):
                    highest, weighted = state
                    source = block_list[local, slot]
                    scores = scores_of(source, query)
                    new_highest = jnp.maximum(highest, jnp.max(scores, axis=0, keepdims=True))
                    weights = jnp.exp2(scores - new_highest)
                    weighted = weighted * jnp.exp2(highest - new_highest) + weigh(source, weights)
                    return (new_highest, weighted)

                _, weighted = lax.fori_loop(1, live, one_slot, (highest, weighted))
                result = weighted[0:HD] / weighted[HD : HD + 1]
                store(block, result.T.astype(jnp.bfloat16))
                return carry

            lax.fori_loop(0, blocks_here, one_block, 0)


def attend(place, lists, pieces):
    blocks_here, slots = lists[0].shape
    total_blocks = 4 * blocks_here
    tokens = total_blocks * BLK
    tiles = blocks_here * 2
    room = total_blocks * slots + STEP
    pairs = total_blocks * slots // 2
    return pl.pallas_call(
        functools.partial(attend_kernel, blocks_here),
        out_shape=jax.ShapeDtypeStruct((4, tiles, TILE, HD), jnp.bfloat16),
        in_specs=[pl.BlockSpec(memory_space=pltpu.SMEM)] * 5
        + [pl.BlockSpec(memory_space=pl.ANY)] * 32,
        out_specs=pl.BlockSpec(memory_space=pltpu.VMEM),
        scratch_shapes=[
            pltpu.VMEM((tokens, 3 * HD), jnp.bfloat16),
            pltpu.VMEM((HD + 16, tokens), jnp.bfloat16),
            pltpu.VMEM((total_blocks + 1, 2 * TILE, HD), jnp.bfloat16),
            pltpu.VMEM((total_blocks + 1, 8, 2 * TILE), jnp.float32),
            pltpu.VMEM((total_blocks + 1, HD + 16, 2 * TILE), jnp.float32),
            pltpu.SMEM((room,), jnp.int32),
            pltpu.SMEM((room,), jnp.int32),
            pltpu.SemaphoreType.DMA((64,)),
        ],
        compiler_params=pltpu.CompilerParams(vmem_limit_bytes=VMEM_LIMIT),
        cost_estimate=pl.CostEstimate(
            flops=pairs * 4 * BLK * 2 * TILE * HD,
            bytes_accessed=tokens * 10 * HD,
            transcendentals=pairs * BLK * 2 * TILE,
        ),
        name="attend_one_head",
    )(place, *lists, *pieces)


def finish_kernel(place, *rest):
    parts, swapped, w_out, hidden, out = rest[:4], rest[4], rest[5], rest[6], rest[7]
    attended, sems, swap_sems = rest[8:]
    section, chip, core = place[0], place[1], place[2]
    odd = lax.rem(chip, 2)

    @pl.when(pl.program_id(0) == 0)
    def _():
        copies = []
        for relative in range(4):
            for shift in range(4):
                head = (chip ^ relative) * 4 + lax.rem(section - shift + 4, 4)
                column = pl.ds(pl.multiple_of(head * HD, HD), HD)
                number = relative * 4 + shift
                for kept in range(2):
                    tile = kept + core
                    to = jnp.where(
                        core == 0, kept * (1 + odd), jnp.where(kept == 0, odd, 2)
                    )
                    copies.append(
                        pltpu.make_async_copy(
                            parts[relative].at[shift, tile],
                            attended.at[pl.ds(pl.multiple_of(to * TILE, TILE), TILE), column],
                            sems.at[number * 2 + kept],
                        )
                    )
                to = jnp.where(core == 0, 2 - odd, 1 - odd)
                copies.append(
                    pltpu.make_async_copy(
                        swapped.at[relative, shift],
                        attended.at[pl.ds(pl.multiple_of(to * TILE, TILE), TILE), column],
                        swap_sems.at[number],
                    )
                )
        for copy in copies:
            copy.start()
        for copy in copies:
            copy.wait()

    summed = jnp.dot(attended[...], w_out[...], preferred_element_type=jnp.float32)
    out[...] = (hidden[...].astype(jnp.float32) + summed).astype(jnp.bfloat16)


def finish(place, parts, swapped, w_out, hidden):
    count = hidden.shape[0]
    step = 256
    any_space = pl.BlockSpec(memory_space=pl.ANY)
    return pl.pallas_call(
        finish_kernel,
        out_shape=jax.ShapeDtypeStruct((count, D), jnp.bfloat16),
        grid=(D // step,),
        in_specs=[pl.BlockSpec(memory_space=pltpu.SMEM)]
        + [any_space] * 5
        + [
            pl.BlockSpec((D, step), lambda i: (0, i)),
            pl.BlockSpec((count, step), lambda i: (0, i)),
        ],
        out_specs=pl.BlockSpec((count, step), lambda i: (0, i)),
        scratch_shapes=[
            pltpu.VMEM((count, D), jnp.bfloat16),
            pltpu.SemaphoreType.DMA((32,)),
            pltpu.SemaphoreType.DMA((16,)),
        ],
        compiler_params=pltpu.CompilerParams(
            vmem_limit_bytes=VMEM_LIMIT, dimension_semantics=("arbitrary",)
        ),
        cost_estimate=pl.CostEstimate(
            flops=2 * count * D * D, bytes_accessed=2 * D * D, transcendentals=0
        ),
        name="project_out",
    )(place, *parts, swapped, w_out, hidden)


def by_head(hidden_in, norm_gain, w_qkv, w_out, block_lists):
    section = lax.axis_index("section")
    device = lax.axis_index("head")
    chip, core = device // 2, device % 2
    blocks_here = block_lists.shape[0]
    tok = blocks_here * BLK
    rows = hidden_in.shape[0]
    half = rows // 2

    other_core = [(i, i ^ 1) for i in range(8)]
    along_x = [(i, i ^ 2) for i in range(8)]
    along_y = [(i, i ^ 4) for i in range(8)]
    diagonal = [(i, i ^ 6) for i in range(8)]

    def to_section(array, shift):
        return lax.ppermute(array, "section", [(i, (i + shift) % 4) for i in range(4)])

    place = jnp.stack([section, chip, core]).astype(jnp.int32)
    shifts = jnp.arange(4, dtype=jnp.int32)
    chosen = (section + shifts - 2 * core + 4) % 4

    own = jnp.transpose(w_qkv, (1, 0, 2))
    other = lax.ppermute(own, "head", other_core)
    hidden_in, own = lax.optimization_barrier((hidden_in, own))
    lists = [block_lists] + [to_section(block_lists, shift) for shift in range(1, 4)]

    resid = hidden_in.astype(jnp.float32)
    normed = (
        resid * lax.rsqrt(jnp.mean(resid * resid, axis=-1, keepdims=True) + EPS) * norm_gain
    ).astype(jnp.bfloat16)
    low, high = normed[:half], normed[half:]
    x_low = lax.ppermute(low, "head", along_x)
    y_low = lax.ppermute(low, "head", along_y)
    x_high = lax.ppermute(high, "head", along_x)
    y_high = lax.ppermute(high, "head", along_y)
    origins = [
        ((0, 0), (0, 1)),
        ((1, 0), (2, 0)),
        ((1, 1), (2, 1)),
        ((3, 0), (3, 1)),
    ]

    frequency = THETA ** (-(2.0 * jnp.arange(HD // 2, dtype=jnp.float32)) / HD)
    starts = jnp.stack(
        [
            section * tok + (chip ^ relative) * (2 * rows) + core * rows + which * half
            for chunk in origins
            for relative, which in chunk
        ]
    )
    positions = (starts[:, None] + jnp.arange(half, dtype=jnp.int32)[None, :]).reshape(4, rows)
    angle = positions.astype(jnp.float32)[:, :, None] * frequency
    cosine, sine = jnp.cos(angle), jnp.sin(angle)
    cosine = jnp.concatenate([cosine, cosine], axis=-1)
    sine = jnp.concatenate([-sine, sine], axis=-1)

    pieces = []

    def send(number, first, second):
        outs = project(chosen, first, second, own, other, cosine[number], sine[number])
        for shift in range(4):
            arrived = outs[shift] if shift == 0 else to_section(outs[shift], shift)
            pieces.extend([arrived, lax.ppermute(arrived, "head", other_core)])
        return outs[0]

    mark = send(0, low, high)
    x_high, y_high, x_low, y_low, mark = lax.optimization_barrier(
        (x_high, y_high, x_low, y_low, mark)
    )
    d_low = lax.ppermute(y_low, "head", along_x)
    d_high = lax.ppermute(x_high, "head", along_y)
    send(1, x_low, y_low)
    send(2, x_high, y_high)
    send(3, d_low, d_high)

    late_w_out, _, _ = lax.optimization_barrier((w_out, d_low, d_high))
    w_out_all = lax.all_gather(late_w_out, "head", axis=0, tiled=True)

    attended = attend(place, lists, pieces)
    back = [attended[0]] + [to_section(attended[shift], shift) for shift in range(1, 4)]
    back = jnp.stack(back).reshape(4, 4, 3, TILE, HD)
    parts = [back[:, 0]] + [
        lax.ppermute(back[:, relative], "head", perm)
        for relative, perm in ((1, along_x), (2, along_y), (3, diagonal))
    ]
    given = jnp.where(core == 0, 2, 0)
    swapped = lax.ppermute(
        jnp.stack([lax.dynamic_index_in_dim(part, given, 1, keepdims=False) for part in parts]),
        "head",
        other_core,
    )
    return finish(place, parts, swapped, w_out_all, hidden_in)


def solution(mesh):
    placed = (
        P(("section", "head"), None),
        P(),
        P(None, None, "head"),
        P("head", None),
        P("section", None),
    )

    def local(hidden_in, norm_gain, w_qkv, w_out, block_lists):
        fits = (
            mesh.shape["section"] == 4
            and mesh.shape["head"] == 8
            and w_qkv.shape[2] == 2 * HD
            and block_lists.shape[0] % 6 == 0
        )
        form = by_head if fits else general
        return form(hidden_in, norm_gain, w_qkv, w_out, block_lists)

    return jax.shard_map(
        local, mesh=mesh, in_specs=placed, out_specs=P(("section", "head"), None), check_vma=False
    )
```

```python
import functools
import math

import jax
import jax.numpy as jnp
from jax import lax
from jax.experimental import pallas as pl
from jax.experimental.pallas import tpu as pltpu
from jax.sharding import PartitionSpec as P

D = 2048
HD = 128
BLK = 512
TILE = 128
STEP = 12


EPS = 1e-05
THETA = 10000.0
VMEM_LIMIT = 56 * 1024 * 1024


def rotate(vectors, cosine, sine):
    half = vectors.shape[-1] // 2
    first = vectors[..., :half]
    second = vectors[..., half:]
    return jnp.concatenate(
        [first * cosine - second * sine, second * cosine + first * sine], axis=-1
    )


def general(hidden_in, norm_gain, w_qkv, w_out, block_lists):
    section_id = lax.axis_index("section")
    width = w_qkv.shape[2]
    heads_here = width // HD
    blocks_here = block_lists.shape[0]
    tok_dev = blocks_here * BLK
    scale = 1.0 / math.sqrt(HD)
    resid = hidden_in.astype(jnp.float32)
    normed = (
        resid * lax.rsqrt(jnp.mean(resid * resid, axis=-1, keepdims=True) + EPS) * norm_gain
    ).astype(jnp.bfloat16)
    flat_weight = w_qkv.reshape(D, 3 * width)
    frequency = THETA ** (-(2.0 * jnp.arange(HD // 2, dtype=jnp.float32)) / HD)
    piece = lax.all_gather(normed, "head", axis=0, tiled=True)
    count = piece.shape[0]
    mixed_rows = jnp.dot(piece, flat_weight, preferred_element_type=jnp.float32).reshape(
        count, 3, heads_here, HD
    )
    positions = (section_id * tok_dev + jnp.arange(count, dtype=jnp.int32)).astype(jnp.float32)
    angle = positions[:, None] * frequency[None, :]
    cosine = jnp.cos(angle)[:, None, :]
    sine = jnp.sin(angle)[:, None, :]
    query = rotate(mixed_rows[:, 0], cosine, sine).astype(jnp.bfloat16).reshape(count, width)
    keys = rotate(mixed_rows[:, 1], cosine, sine).astype(jnp.bfloat16).reshape(count, width)
    values = mixed_rows[:, 2].astype(jnp.bfloat16).reshape(count, width)
    keys_all, values_all = (
        lax.all_gather(keys, "section", axis=0, tiled=True),
        lax.all_gather(values, "section", axis=0, tiled=True),
    )
    count_blocks = block_lists.shape[0]
    query_blocks = query.reshape(count_blocks, BLK, heads_here, HD)
    block_ids = section_id * blocks_here + jnp.arange(count_blocks, dtype=jnp.int32)

    def one_block(carry, item):
        query_block, block_row, block_id = item
        live_slots = jnp.sum((block_row >= 0).astype(jnp.int32))
        query_positions = block_id * BLK + jnp.arange(BLK, dtype=jnp.int32)

        def one_slot(slot, state):
            highest, total, weighted = state
            source = block_row[slot]
            key_block = lax.dynamic_slice_in_dim(keys_all, source * BLK, BLK, 0).reshape(
                BLK, heads_here, HD
            )
            value_block = lax.dynamic_slice_in_dim(values_all, source * BLK, BLK, 0).reshape(
                BLK, heads_here, HD
            )
            scores = (
                jnp.einsum(
                    "qhd,khd->hqk", query_block, key_block, preferred_element_type=jnp.float32
                )
                * scale
            )
            key_positions = source * BLK + jnp.arange(BLK, dtype=jnp.int32)
            scores = jnp.where(
                key_positions[None, None, :] <= query_positions[None, :, None], scores, -jnp.inf
            )
            new_highest = jnp.maximum(highest, jnp.max(scores, axis=-1))
            factor = jnp.exp(highest - new_highest)
            weights = jnp.exp(scores - new_highest[..., None])
            total = total * factor + jnp.sum(weights, axis=-1)
            update = jnp.einsum(
                "hqk,khd->hqd",
                weights.astype(jnp.bfloat16),
                value_block,
                preferred_element_type=jnp.float32,
            )
            weighted = weighted * factor[..., None] + update
            return (new_highest, total, weighted)

        start_state = (
            jnp.full((heads_here, BLK), -jnp.inf, jnp.float32),
            jnp.zeros((heads_here, BLK), jnp.float32),
            jnp.zeros((heads_here, BLK, HD), jnp.float32),
        )
        highest, total, weighted = lax.fori_loop(0, live_slots, one_slot, start_state)
        result = (
            (weighted / total[..., None])
            .transpose(1, 0, 2)
            .reshape(BLK, width)
            .astype(jnp.bfloat16)
        )
        return (carry, result)

    _, results = lax.scan(
        one_block, jnp.zeros((), jnp.int32), (query_blocks, block_lists, block_ids)
    )
    attended = results.reshape(count_blocks * BLK, width)
    regrouped = lax.all_to_all(attended, "head", split_axis=0, concat_axis=1, tiled=True)
    summed = jnp.dot(
        regrouped,
        lax.all_gather(w_out, "head", axis=0, tiled=True),
        preferred_element_type=jnp.float32,
    )
    return (resid + summed).astype(jnp.bfloat16)


def project_kernel(number, groups, place, *rest):
    pieces, rest = rest[:number], rest[number:]
    own, other, cosine, sine = rest[:4]
    outs, rest = rest[4 : 4 + 4 * groups], rest[4 + 4 * groups :]
    rows, weights, results, row_sems, weight_sems, out_sems = rest
    count = rows.shape[0]
    row_copies, start = [], 0
    for i, ref in enumerate(pieces):
        size = ref.shape[0]
        row_copies.append(
            pltpu.make_async_copy(ref, rows.at[pl.ds(start, size)], row_sems.at[i])
        )
        start += size
    weight_copies = [
        pltpu.make_async_copy(
            ref.at[part],
            weights.at[w * 3 + part],
            weight_sems.at[w * 3 + part],
        )
        for w, ref in enumerate((own, other))
        for part in range(3)
    ]
    for copy in row_copies + weight_copies:
        copy.start()
    for copy in row_copies:
        copy.wait()
    query_scale = math.log2(math.e) / math.sqrt(HD)
    step = count // (2 * max(1, count // 384))
    for w in range(2):
        for part in range(3):
            weight_copies[w * 3 + part].wait()

            def tile(at, w=w, part=part):
                piece = pl.ds(at, step)
                product = jnp.dot(
                    rows[piece], weights[w * 3 + part], preferred_element_type=jnp.float32
                )
                for h in range(2):
                    vector = product[:, h * HD : (h + 1) * HD]
                    if part < 2:
                        turned = pltpu.roll(vector, HD // 2, 1)
                        vector = vector * cosine[piece] + turned * sine[piece]
                    if part == 0:
                        vector = vector * query_scale
                    column = slice(part * HD, (part + 1) * HD)
                    results[w * 2 + h, piece, column] = vector.astype(jnp.bfloat16)

            for at in range(0, count, step):
                tile(at)
    copies = [
        pltpu.make_async_copy(
            results.at[place[shift], pl.ds(group * (count // groups), count // groups)],
            outs[group * 4 + shift],
            out_sems.at[group * 4 + shift],
        )
        for group in range(groups)
        for shift in range(4)
    ]
    for copy in copies:
        copy.start()
    for copy in copies:
        copy.wait()


def project(place, pieces, own, other, cosine, sine, groups=1):
    count = sum(piece.shape[0] for piece in pieces)
    number = len(pieces)
    width = own.shape[2]
    any_space = pl.BlockSpec(memory_space=pl.ANY)
    vmem = pl.BlockSpec(memory_space=pltpu.VMEM)
    return pl.pallas_call(
        functools.partial(project_kernel, number, groups),
        out_shape=[jax.ShapeDtypeStruct((count // groups, 3 * HD), jnp.bfloat16)] * (4 * groups),
        in_specs=[pl.BlockSpec(memory_space=pltpu.SMEM)] + [any_space] * (number + 2) + [vmem] * 2,
        out_specs=[any_space] * (4 * groups),
        scratch_shapes=[
            pltpu.VMEM((count, D), jnp.bfloat16),
            pltpu.VMEM((6, D, width), jnp.bfloat16),
            pltpu.VMEM((4, count, 3 * HD), jnp.bfloat16),
            pltpu.SemaphoreType.DMA((number,)),
            pltpu.SemaphoreType.DMA((6,)),
            pltpu.SemaphoreType.DMA((4 * groups,)),
        ],
        compiler_params=pltpu.CompilerParams(vmem_limit_bytes=VMEM_LIMIT),
        cost_estimate=pl.CostEstimate(
            flops=2 * count * D * 6 * width, bytes_accessed=2 * 6 * D * width, transcendentals=0
        ),
        name="project_and_rotate",
    )(place, *pieces, own, other, cosine, sine)


def attend_kernel(blocks_here, near, place, *rest):
    lists, rest = rest[:4], rest[4:]
    near_pieces, far_pieces, rest = rest[:16], rest[16:22], rest[22:]
    out, rows, query_rows, values_t, queries, tops, sums, item_q, item_k, sems = rest
    section, chip, core = place[0], place[1], place[2]
    rows_here = near_pieces[0].shape[0]
    tok = blocks_here * BLK
    slots = lists[0].shape[1]
    wide = 2 * TILE
    pair_blocks = blocks_here // 2
    total_blocks = 4 * pair_blocks
    pair = chip // 2 if near else 1 - chip // 2
    copies = []

    def fetch(ref, relative, source, side):
        owner, size = chip ^ relative, rows_here
        start = source * tok + owner * (2 * rows_here) + side * rows_here
        number = len(copies)
        copies.append(
            pltpu.make_async_copy(
                ref.at[..., pl.ds(HD, 2 * HD)],
                rows.at[pl.ds(pl.multiple_of(start, size), size)],
                sems.at[number],
            )
        )
        if (relative < 2) == near:
            start = source * (tok // 2) + lax.rem(owner, 2) * (2 * rows_here)
            start = start + side * rows_here
            copies.append(
                pltpu.make_async_copy(
                    ref.at[..., pl.ds(0, HD)],
                    query_rows.at[pl.ds(pl.multiple_of(start, size), size)],
                    sems.at[number + 1],
                )
            )

    for far, pieces in enumerate((near_pieces, far_pieces)):
        side = core if far == 0 else 1 - core
        for shift in range(4):
            source = lax.rem(section - shift + 4, 4)
            for relative in range(4):
                if far == 0:
                    ref = pieces[relative * 4 + shift]
                elif relative == 0:
                    ref = pieces[0].at[shift]
                elif relative < 3:
                    ref = pieces[1].at[(relative - 1) * 4 + shift]
                else:
                    ref = pieces[2 + shift]
                fetch(ref, relative, source, side)
    for copy in copies:
        copy.start()

    def key_block(block):
        return block // pair_blocks * blocks_here + pair * pair_blocks + lax.rem(block, pair_blocks)

    count = jnp.int32(0)
    for shift in range(4):
        block_list = lists[shift]
        first_block = lax.rem(section - shift + 4, 4) * pair_blocks

        def note(local, count, block_list=block_list, first_block=first_block):
            for slot in range(1, slots):
                source = block_list[pair * pair_blocks + local, slot]
                item_q[count] = first_block + local
                item_k[count] = source
                count = count + (source >= 0).astype(jnp.int32)
            return count

        count = lax.fori_loop(0, pair_blocks, note, count)
    for extra in range(STEP):
        item_q[count + extra] = total_blocks
        item_k[count + extra] = 0

    values_t[HD:, :] = jnp.ones((values_t.shape[0] - HD, values_t.shape[1]), jnp.bfloat16)
    queries[total_blocks] = jnp.zeros((wide, HD), jnp.bfloat16)
    tops[total_blocks] = jnp.zeros((8, wide), jnp.float32)
    sums[total_blocks] = jnp.zeros(sums.shape[1:], jnp.float32)
    for copy in copies:
        copy.wait()

    lane = lax.broadcasted_iota(jnp.int32, (BLK, wide), 1)
    key_at = lax.broadcasted_iota(jnp.int32, (BLK, wide), 0)

    def query_place(local):
        middle = lax.rem(local, 3) == 1
        offset = jnp.where(middle, core * TILE, core * wide)
        return offset, jnp.where(middle, TILE, 0)

    def scores_of(source, query):
        at = pl.multiple_of(source * BLK, BLK)
        return lax.dot_general(
            rows[pl.ds(at, BLK), 0:HD],
            query,
            (((1,), (1,)), ((), ())),
            preferred_element_type=jnp.float32,
        )

    def weigh(source, weights):
        at = pl.multiple_of(source * BLK, BLK)
        return jnp.dot(
            values_t[:, pl.ds(at, BLK)],
            weights.astype(jnp.bfloat16),
            preferred_element_type=jnp.float32,
        )

    def masked(local, scores):
        offset, gap = query_place(local)
        query_at = offset + lane + jnp.where(lane >= TILE, gap, 0)
        return jnp.where(key_at <= query_at, scores, -jnp.inf)

    def diagonal(step, carry):
        blocks = [step * 4 + i for i in range(4)]
        scores = []
        for block in blocks:
            offset, gap = query_place(lax.rem(block, pair_blocks))
            start = pl.multiple_of(block * BLK + offset, TILE)
            later = pl.multiple_of(start + TILE + gap, TILE)
            query = jnp.concatenate(
                [query_rows[pl.ds(start, TILE)], query_rows[pl.ds(later, TILE)]], axis=0
            )
            queries[block] = query
            scores.append(scores_of(key_block(block), query))
        for block, score in zip(blocks, scores):
            score = masked(lax.rem(block, pair_blocks), score)
            top = jnp.max(score, axis=0, keepdims=True)
            tops[block] = jnp.broadcast_to(top, (8, wide))
            sums[block] = weigh(key_block(block), jnp.exp2(score - top))
        return carry

    def turn(step, carry):
        for i in range(4):
            at = pl.multiple_of((step * 4 + i) * BLK, BLK)
            values_t[:HD, pl.ds(at, BLK)] = rows[pl.ds(at, BLK), HD : 2 * HD].T
        return carry

    lax.fori_loop(0, blocks_here, turn, 0)
    lax.fori_loop(0, total_blocks // 4, diagonal, 0)

    def below(step, carry):
        items = [step * STEP + i for i in range(STEP)]
        scores = scores_of(item_k[items[0]], queries[item_q[items[0]]])
        held = None
        for i, item in enumerate(items):
            if i + 1 < STEP:
                ahead = scores_of(item_k[items[i + 1]], queries[item_q[items[i + 1]]])
            weights = jnp.exp2(scores - tops[item_q[item], 0:1]).astype(jnp.bfloat16)
            if held is not None:
                sums[item_q[items[i - 1]]] += weigh(item_k[items[i - 1]], held)
            held, scores = weights, ahead
        sums[item_q[items[-1]]] += weigh(item_k[items[-1]], held)
        return carry

    lax.fori_loop(0, (count + STEP - 1) // STEP, below, 0)

    def store(block, result):
        local = lax.rem(block, pair_blocks)
        shift = lax.rem(block // pair_blocks - section + 4, 4)
        for part in range(2):
            tile = 2 * local + part
            which = lax.rem(tile // 3, 2) ^ lax.rem(chip, 2)
            i = lax.rem(tile, 3)
            if near:
                where = jnp.where(i == 2 - 2 * core, 4 + which, which * 2 + i - core)
            else:
                where = which * 3 + jnp.where(i == 2 - 2 * core, 2, i - core)
            out[shift, where] = result[part * TILE : (part + 1) * TILE]

    def leave(step, over):
        for i in range(4):
            block = step * 4 + i
            total = sums[block, HD : HD + 1]
            over = jnp.maximum(over, jnp.where(total < 2.0**100, 0.0, 1.0))
            store(block, (sums[block, 0:HD] / total).T.astype(jnp.bfloat16))
        return over

    over = lax.fori_loop(0, total_blocks // 4, leave, jnp.zeros((1, wide), jnp.float32))

    @pl.when(jnp.max(over) > 0)
    def _():
        for shift in range(4):
            block_list = lists[shift]
            first_block = lax.rem(section - shift + 4, 4) * pair_blocks

            def one_block(local, carry, block_list=block_list, first_block=first_block):
                block = first_block + local
                home = key_block(block)
                entry = pair * pair_blocks + local
                query = queries[block]
                live = jnp.int32(0)
                for slot in range(slots):
                    live = live + (block_list[entry, slot] >= 0).astype(jnp.int32)
                scores = masked(local, scores_of(home, query))
                highest = jnp.max(scores, axis=0, keepdims=True)
                weighted = weigh(home, jnp.exp2(scores - highest))

                def one_slot(slot, state):
                    highest, weighted = state
                    source = block_list[entry, slot]
                    scores = scores_of(source, query)
                    new_highest = jnp.maximum(highest, jnp.max(scores, axis=0, keepdims=True))
                    weights = jnp.exp2(scores - new_highest)
                    weighted = weighted * jnp.exp2(highest - new_highest) + weigh(source, weights)
                    return (new_highest, weighted)

                _, weighted = lax.fori_loop(1, live, one_slot, (highest, weighted))
                result = weighted[0:HD] / weighted[HD : HD + 1]
                store(block, result.T.astype(jnp.bfloat16))
                return carry

            lax.fori_loop(0, pair_blocks, one_block, 0)


def attend(near, place, lists, near_pieces, far_pieces):
    blocks_here, slots = lists[0].shape
    total_blocks = 2 * blocks_here
    tokens = 4 * blocks_here * BLK
    room = total_blocks * slots + STEP
    pairs = total_blocks * slots // 2
    return pl.pallas_call(
        functools.partial(attend_kernel, blocks_here, near),
        out_shape=jax.ShapeDtypeStruct((4, blocks_here, TILE, HD), jnp.bfloat16),
        in_specs=[pl.BlockSpec(memory_space=pltpu.SMEM)] * 5
        + [pl.BlockSpec(memory_space=pl.ANY)] * (len(near_pieces) + len(far_pieces)),
        out_specs=pl.BlockSpec(memory_space=pltpu.VMEM),
        scratch_shapes=[
            pltpu.VMEM((tokens, 2 * HD), jnp.bfloat16),
            pltpu.VMEM((tokens // 2, HD), jnp.bfloat16),
            pltpu.VMEM((HD + 16, tokens), jnp.bfloat16),
            pltpu.VMEM((total_blocks + 1, 2 * TILE, HD), jnp.bfloat16),
            pltpu.VMEM((total_blocks + 1, 8, 2 * TILE), jnp.float32),
            pltpu.VMEM((total_blocks + 1, HD + 16, 2 * TILE), jnp.float32),
            pltpu.SMEM((room,), jnp.int32),
            pltpu.SMEM((room,), jnp.int32),
            pltpu.SemaphoreType.DMA((48,)),
        ],
        compiler_params=pltpu.CompilerParams(vmem_limit_bytes=VMEM_LIMIT),
        cost_estimate=pl.CostEstimate(
            flops=pairs * 4 * BLK * 2 * TILE * HD,
            bytes_accessed=tokens * 5 * HD,
            transcendentals=pairs * BLK * 2 * TILE,
        ),
        name="attend_near" if near else "attend_far",
    )(place, *lists, *near_pieces, *far_pieces)


def finish_kernel(relatives, last, place, *rest):
    number = len(relatives)
    kept, given, rest = rest[:number], rest[number : 2 * number], rest[2 * number :]
    w_out, before, out, attended, weights, sems, given_sems, weight_sems = rest
    section, chip, core = place[0], place[1], place[2]
    odd = lax.rem(chip, 2)
    depth = 4 * HD
    copies, weight_copies = [], []
    for r, relative in enumerate(relatives):
        start = pl.multiple_of((chip ^ relative) * depth, depth)
        weight_copies.append(
            pltpu.make_async_copy(
                w_out.at[pl.ds(start, depth)],
                weights.at[pl.ds(r * depth, depth)],
                weight_sems.at[r],
            )
        )
        for shift in range(4):
            head = r * 4 + lax.rem(section - shift + 4, 4)
            column = pl.ds(pl.multiple_of(head * HD, HD), HD)
            for slot in range(2):
                to = jnp.where(core == 0, slot * (1 + odd), odd if slot == 0 else 2)
                copies.append(
                    pltpu.make_async_copy(
                        kept[r].at[shift, slot],
                        attended.at[pl.ds(pl.multiple_of(to * TILE, TILE), TILE), column],
                        sems.at[(r * 4 + shift) * 2 + slot],
                    )
                )
            to = jnp.where(core == 0, 2 - odd, 1 - odd)
            copies.append(
                pltpu.make_async_copy(
                    given[r].at[shift, 0],
                    attended.at[pl.ds(pl.multiple_of(to * TILE, TILE), TILE), column],
                    given_sems.at[r * 4 + shift],
                )
            )
    for copy in weight_copies + copies:
        copy.start()
    for copy in copies + weight_copies:
        copy.wait()
    half = out.shape[0] // 2
    step = 256
    for column in range(0, out.shape[1], step):
        for at in range(0, out.shape[0], half):
            piece = (slice(at, at + half), slice(column, column + step))
            summed = jnp.dot(
                attended[at : at + half],
                weights[:, column : column + step],
                preferred_element_type=jnp.float32,
            )
            out[piece] = (before[piece].astype(jnp.float32) + summed).astype(out.dtype)


def finish(relatives, place, kept, given, w_out, before, last):
    count = before.shape[0]
    number = len(relatives)
    any_space = pl.BlockSpec(memory_space=pl.ANY)
    vmem = pl.BlockSpec(memory_space=pltpu.VMEM)
    depth = number * 4 * HD
    return pl.pallas_call(
        functools.partial(finish_kernel, relatives, last),
        out_shape=jax.ShapeDtypeStruct((count, D), jnp.bfloat16 if last else jnp.float32),
        in_specs=[pl.BlockSpec(memory_space=pltpu.SMEM)] + [any_space] * (2 * number + 1) + [vmem],
        out_specs=vmem,
        scratch_shapes=[
            pltpu.VMEM((count, depth), jnp.bfloat16),
            pltpu.VMEM((depth, D), jnp.bfloat16),
            pltpu.SemaphoreType.DMA((number * 8,)),
            pltpu.SemaphoreType.DMA((number * 4,)),
            pltpu.SemaphoreType.DMA((number,)),
        ],
        compiler_params=pltpu.CompilerParams(vmem_limit_bytes=VMEM_LIMIT),
        cost_estimate=pl.CostEstimate(
            flops=2 * count * D * depth, bytes_accessed=2 * D * depth, transcendentals=0
        ),
        name="project_out_last" if last else "project_out_first",
    )(place, *kept, *given, w_out, before)


def by_head(hidden_in, norm_gain, w_qkv, w_out, block_lists):
    section = lax.axis_index("section")
    device = lax.axis_index("head")
    chip, core = device // 2, device % 2
    blocks_here = block_lists.shape[0]
    tok = blocks_here * BLK
    rows = hidden_in.shape[0]
    half = rows // 2

    other_core = [(i, i ^ 1) for i in range(8)]
    along_x = [(i, i ^ 2) for i in range(8)]
    along_y = [(i, i ^ 4) for i in range(8)]

    def to_section(array, shift):
        return lax.ppermute(array, "section", [(i, (i + shift) % 4) for i in range(4)])

    place = jnp.stack([section, chip, core]).astype(jnp.int32)
    shifts = jnp.arange(4, dtype=jnp.int32)
    chosen = (section + shifts - 2 * core + 4) % 4

    own = jnp.transpose(w_qkv, (1, 0, 2))
    other = lax.ppermute(own, "head", other_core)
    hidden_in, own = lax.optimization_barrier((hidden_in, own))

    resid = hidden_in.astype(jnp.float32)
    normed = (
        resid * lax.rsqrt(jnp.mean(resid * resid, axis=-1, keepdims=True) + EPS) * norm_gain
    ).astype(jnp.bfloat16)
    x_rows = lax.ppermute(normed, "head", along_x)
    y_rows = lax.ppermute(normed, "head", along_y)

    frequency = THETA ** (-(2.0 * jnp.arange(HD // 2, dtype=jnp.float32)) / HD)

    def projected(relatives, pieces, groups=1):
        starts = section * tok + (chip ^ jnp.array(relatives)) * (2 * rows) + core * rows
        positions = (starts[:, None] + jnp.arange(rows, dtype=jnp.int32)[None, :]).reshape(-1)
        angle = positions.astype(jnp.float32)[:, None] * frequency
        cosine, sine = jnp.cos(angle), jnp.sin(angle)
        cosine = jnp.concatenate([cosine, cosine], axis=-1)
        sine = jnp.concatenate([-sine, sine], axis=-1)
        return project(chosen, pieces, own, other, cosine, sine, groups)

    def sent(outs):
        return [outs[0]] + [to_section(outs[shift], shift) for shift in range(1, 4)]

    def to_other(array):
        return lax.ppermute(array, "head", other_core)

    own_parts = sent(projected([0], [normed]))
    axis_outs = projected([1, 2], [x_rows, y_rows], 2)
    x_rows, y_rows, block_lists, *held = lax.optimization_barrier(
        (x_rows, y_rows, block_lists, *own_parts, *axis_outs)
    )
    own_parts, x_outs, y_outs = held[:4], held[4:8], held[8:]
    d_low = lax.ppermute(y_rows[:half], "head", along_x)
    d_high = lax.ppermute(x_rows[half:], "head", along_y)
    x_parts = sent(x_outs)
    lists = [block_lists] + [to_section(block_lists, shift) for shift in range(1, 4)]
    w_out, d_low, d_high, *held = lax.optimization_barrier(
        (w_out, d_low, d_high, *lists, *x_parts, *y_outs)
    )
    lists, x_parts, y_outs = held[:4], held[4:8], held[8:]
    w_out_all = lax.all_gather(w_out, "head", axis=0, tiled=True)
    y_parts = sent(y_outs)
    diagonal_outs = projected([3], [d_low, d_high])
    held = lax.optimization_barrier((*y_parts, *diagonal_outs))
    y_parts, diagonal_outs = list(held[:4]), held[4:]
    diagonal_parts = sent(diagonal_outs)
    near_pieces = own_parts + x_parts + y_parts + diagonal_parts
    far_pieces = [to_other(jnp.stack(own_parts)), to_other(jnp.stack(x_parts + y_parts))]
    far_pieces += [to_other(part) for part in diagonal_parts]

    def back(attended):
        parts = [attended[0]] + [to_section(attended[shift], shift) for shift in range(1, 4)]
        return jnp.stack(parts)

    def to_chip(array, relative, cross):
        flip = 2 * relative + (1 if cross else 0)
        return lax.ppermute(array, "head", [(i, i ^ flip) for i in range(8)])

    far = back(attend(False, place, lists, near_pieces, far_pieces))
    near = back(attend(True, place, lists, near_pieces, far_pieces))
    y_part, d_part = to_chip(far[:, 0:3], 2, False), to_chip(far[:, 3:6], 3, False)
    swapped = to_other(jnp.stack([y_part[:, 2:3], d_part[:, 2:3]]))
    own_given, x_given = to_chip(near[:, 4:5], 0, True), to_chip(near[:, 5:6], 1, True)
    x_kept = to_chip(near[:, 2:4], 1, False)
    kept, given = [y_part, d_part, near[:, 0:2]], [swapped[0], swapped[1], own_given]
    partial = finish((2, 3, 0), place, kept, given, w_out_all, hidden_in, False)
    return finish((1,), place, [x_kept], [x_given], w_out_all, partial, True)


def solution(mesh):
    placed = (
        P(("section", "head"), None),
        P(),
        P(None, None, "head"),
        P("head", None),
        P("section", None),
    )

    def local(hidden_in, norm_gain, w_qkv, w_out, block_lists):
        fits = (
            mesh.shape["section"] == 4
            and mesh.shape["head"] == 8
            and w_qkv.shape[2] == 2 * HD
            and block_lists.shape[0] % 6 == 0
        )
        form = by_head if fits else general
        return form(hidden_in, norm_gain, w_qkv, w_out, block_lists)

    return jax.shard_map(
        local, mesh=mesh, in_specs=placed, out_specs=P(("section", "head"), None), check_vma=False
    )
```

```python
import functools
import math

import jax
import jax.numpy as jnp
from jax import lax
from jax.experimental import pallas as pl
from jax.experimental.pallas import tpu as pltpu
from jax.sharding import PartitionSpec as P

D = 2048
HD = 128
BLK = 512
TILE = 128
STEP = 12


EPS = 1e-05
THETA = 10000.0
VMEM_LIMIT = 56 * 1024 * 1024


def rotate(vectors, cosine, sine):
    half = vectors.shape[-1] // 2
    first = vectors[..., :half]
    second = vectors[..., half:]
    return jnp.concatenate(
        [first * cosine - second * sine, second * cosine + first * sine], axis=-1
    )


def general(hidden_in, norm_gain, w_qkv, w_out, block_lists):
    section_id = lax.axis_index("section")
    width = w_qkv.shape[2]
    heads_here = width // HD
    blocks_here = block_lists.shape[0]
    tok_dev = blocks_here * BLK
    scale = 1.0 / math.sqrt(HD)
    resid = hidden_in.astype(jnp.float32)
    normed = (
        resid * lax.rsqrt(jnp.mean(resid * resid, axis=-1, keepdims=True) + EPS) * norm_gain
    ).astype(jnp.bfloat16)
    flat_weight = w_qkv.reshape(D, 3 * width)
    frequency = THETA ** (-(2.0 * jnp.arange(HD // 2, dtype=jnp.float32)) / HD)
    piece = lax.all_gather(normed, "head", axis=0, tiled=True)
    count = piece.shape[0]
    mixed_rows = jnp.dot(piece, flat_weight, preferred_element_type=jnp.float32).reshape(
        count, 3, heads_here, HD
    )
    positions = (section_id * tok_dev + jnp.arange(count, dtype=jnp.int32)).astype(jnp.float32)
    angle = positions[:, None] * frequency[None, :]
    cosine = jnp.cos(angle)[:, None, :]
    sine = jnp.sin(angle)[:, None, :]
    query = rotate(mixed_rows[:, 0], cosine, sine).astype(jnp.bfloat16).reshape(count, width)
    keys = rotate(mixed_rows[:, 1], cosine, sine).astype(jnp.bfloat16).reshape(count, width)
    values = mixed_rows[:, 2].astype(jnp.bfloat16).reshape(count, width)
    keys_all, values_all = (
        lax.all_gather(keys, "section", axis=0, tiled=True),
        lax.all_gather(values, "section", axis=0, tiled=True),
    )
    count_blocks = block_lists.shape[0]
    query_blocks = query.reshape(count_blocks, BLK, heads_here, HD)
    block_ids = section_id * blocks_here + jnp.arange(count_blocks, dtype=jnp.int32)

    def one_block(carry, item):
        query_block, block_row, block_id = item
        live_slots = jnp.sum((block_row >= 0).astype(jnp.int32))
        query_positions = block_id * BLK + jnp.arange(BLK, dtype=jnp.int32)

        def one_slot(slot, state):
            highest, total, weighted = state
            source = block_row[slot]
            key_block = lax.dynamic_slice_in_dim(keys_all, source * BLK, BLK, 0).reshape(
                BLK, heads_here, HD
            )
            value_block = lax.dynamic_slice_in_dim(values_all, source * BLK, BLK, 0).reshape(
                BLK, heads_here, HD
            )
            scores = (
                jnp.einsum(
                    "qhd,khd->hqk", query_block, key_block, preferred_element_type=jnp.float32
                )
                * scale
            )
            key_positions = source * BLK + jnp.arange(BLK, dtype=jnp.int32)
            scores = jnp.where(
                key_positions[None, None, :] <= query_positions[None, :, None], scores, -jnp.inf
            )
            new_highest = jnp.maximum(highest, jnp.max(scores, axis=-1))
            factor = jnp.exp(highest - new_highest)
            weights = jnp.exp(scores - new_highest[..., None])
            total = total * factor + jnp.sum(weights, axis=-1)
            update = jnp.einsum(
                "hqk,khd->hqd",
                weights.astype(jnp.bfloat16),
                value_block,
                preferred_element_type=jnp.float32,
            )
            weighted = weighted * factor[..., None] + update
            return (new_highest, total, weighted)

        start_state = (
            jnp.full((heads_here, BLK), -jnp.inf, jnp.float32),
            jnp.zeros((heads_here, BLK), jnp.float32),
            jnp.zeros((heads_here, BLK, HD), jnp.float32),
        )
        highest, total, weighted = lax.fori_loop(0, live_slots, one_slot, start_state)
        result = (
            (weighted / total[..., None])
            .transpose(1, 0, 2)
            .reshape(BLK, width)
            .astype(jnp.bfloat16)
        )
        return (carry, result)

    _, results = lax.scan(
        one_block, jnp.zeros((), jnp.int32), (query_blocks, block_lists, block_ids)
    )
    attended = results.reshape(count_blocks * BLK, width)
    regrouped = lax.all_to_all(attended, "head", split_axis=0, concat_axis=1, tiled=True)
    summed = jnp.dot(
        regrouped,
        lax.all_gather(w_out, "head", axis=0, tiled=True),
        preferred_element_type=jnp.float32,
    )
    return (resid + summed).astype(jnp.bfloat16)


def project_kernel(number, place, *rest):
    pieces, rest = rest[:number], rest[number:]
    own, other, cosine, sine = rest[:4]
    outs, rest = rest[4:8], rest[8:]
    rows, weights, results, row_sems, weight_sems, out_sems = rest
    count = rows.shape[0]
    row_copies, start = [], 0
    for i, ref in enumerate(pieces):
        size = ref.shape[0]
        row_copies.append(
            pltpu.make_async_copy(ref, rows.at[pl.ds(start, size)], row_sems.at[i])
        )
        start += size
    weight_copies = [
        pltpu.make_async_copy(
            ref.at[part],
            weights.at[w * 3 + part],
            weight_sems.at[w * 3 + part],
        )
        for w, ref in enumerate((own, other))
        for part in range(3)
    ]
    for copy in row_copies + weight_copies[:2]:
        copy.start()
    for copy in row_copies:
        copy.wait()
    query_scale = math.log2(math.e) / math.sqrt(HD)
    step = count // 2

    def out_copy(result, shift):
        return pltpu.make_async_copy(results.at[result], outs[shift], out_sems.at[shift])

    for w in range(2):
        for part in range(3):
            weight_copies[w * 3 + part].wait()
            if w * 3 + part + 2 < 6:
                weight_copies[w * 3 + part + 2].start()
            for at in range(0, count, step):
                piece = slice(at, at + step)
                product = jnp.dot(
                    rows[piece], weights[w * 3 + part], preferred_element_type=jnp.float32
                )
                for h in range(2):
                    vector = product[:, h * HD : (h + 1) * HD]
                    if part < 2:
                        turned = pltpu.roll(vector, HD // 2, 1)
                        vector = vector * cosine[piece] + turned * sine[piece]
                    if part == 0:
                        vector = vector * query_scale
                    column = slice(part * HD, (part + 1) * HD)
                    results[w * 2 + h, piece, column] = vector.astype(jnp.bfloat16)
        for h in range(2):
            for shift in range(4):

                @pl.when(place[shift] == w * 2 + h)
                def _(shift=shift, result=w * 2 + h):
                    out_copy(result, shift).start()

    for shift in range(4):
        out_copy(0, shift).wait()


def project(place, pieces, own, other, cosine, sine):
    count = sum(piece.shape[0] for piece in pieces)
    number = len(pieces)
    width = own.shape[2]
    any_space = pl.BlockSpec(memory_space=pl.ANY)
    vmem = pl.BlockSpec(memory_space=pltpu.VMEM)
    return pl.pallas_call(
        functools.partial(project_kernel, number),
        out_shape=[jax.ShapeDtypeStruct((count, 3 * HD), jnp.bfloat16)] * 4,
        in_specs=[pl.BlockSpec(memory_space=pltpu.SMEM)] + [any_space] * (number + 2) + [vmem] * 2,
        out_specs=[any_space] * 4,
        scratch_shapes=[
            pltpu.VMEM((count, D), jnp.bfloat16),
            pltpu.VMEM((6, D, width), jnp.bfloat16),
            pltpu.VMEM((4, count, 3 * HD), jnp.bfloat16),
            pltpu.SemaphoreType.DMA((number,)),
            pltpu.SemaphoreType.DMA((6,)),
            pltpu.SemaphoreType.DMA((4,)),
        ],
        compiler_params=pltpu.CompilerParams(vmem_limit_bytes=VMEM_LIMIT),
        cost_estimate=pl.CostEstimate(
            flops=2 * count * D * 6 * width, bytes_accessed=2 * 6 * D * width, transcendentals=0
        ),
        name="project_and_rotate",
    )(place, *pieces, own, other, cosine, sine)


def attend_kernel(mode, blocks_here, place, *refs):
    refs = list(refs)

    def take(number):
        taken = refs[:number]
        del refs[:number]
        return taken

    near, early, late = mode in ("near", "local"), mode == "early", mode == "late"
    targets = {"near": (1, 2, 3), "local": (0,)}.get(mode, (0, 1, 2, 3))
    lists = take(4)
    have = (0, 2, 3) if early else (0, 1, 2, 3)
    here = {relative: take(4) for relative in have}
    there = {relative: take(4 if relative == 1 else 1) for relative in have}
    state = take(3) if late else []
    outs = take(3 if early else len(targets))
    if early:
        queries, tops, sums = outs
        rows, query_rows, values_t, item_q, item_k, sems = refs
    else:
        rows, query_rows, values_t, queries, tops, sums, item_q, item_k, sems = refs
    section, chip, core = place[0], place[1], place[2]
    rows_here = here[0][0].shape[0]
    tok = blocks_here * BLK
    slots = lists[0].shape[1]
    wide = 2 * TILE
    pair_blocks = blocks_here // 2
    total_blocks = 4 * pair_blocks
    own_pair = chip // 2
    pair = own_pair if near else 1 - own_pair
    parity = lax.rem(chip, 2)

    ends = []

    def fetches(relatives, with_queries, first):
        copies = []
        ends.clear()
        for shift in range(4):
            for relative in relatives:
                owner = chip ^ relative
                source = lax.rem(section - shift + 4, 4)
                for far in range(2):
                    side = core if far == 0 else 1 - core
                    if far == 0:
                        ref = here[relative][shift]
                    elif relative == 1:
                        ref = there[relative][shift]
                    else:
                        ref = there[relative][0].at[shift]
                    start = source * tok + owner * (2 * rows_here) + side * rows_here
                    start = pl.multiple_of(start, rows_here)
                    copies.append(
                        pltpu.make_async_copy(
                            ref.at[..., pl.ds(HD, 2 * HD)],
                            rows.at[pl.ds(start, rows_here)],
                            sems.at[first + len(copies)],
                        )
                    )
                    if not with_queries or (relative < 2) != near or (4 - shift) % 4 not in targets:
                        continue
                    start = source * (tok // 2) + lax.rem(owner, 2) * (2 * rows_here)
                    start = pl.multiple_of(start + side * rows_here, rows_here)
                    copies.append(
                        pltpu.make_async_copy(
                            ref.at[..., pl.ds(0, HD)],
                            query_rows.at[pl.ds(start, rows_here)],
                            sems.at[first + len(copies)],
                        )
                    )
            ends.append(len(copies))
        return copies

    def key_block(block):
        return block // pair_blocks * blocks_here + pair * pair_blocks + lax.rem(block, pair_blocks)

    copies = fetches((0, 1) if late else have, not late, 0)
    state_copies = [
        pltpu.make_async_copy(ref, held, sems.at[48 + i])
        for i, (ref, held) in enumerate(zip(state, (queries, tops, sums)))
    ]
    for copy in copies + state_copies:
        copy.start()

    count = jnp.int32(0)
    for target in targets:
        block_list = lists[(4 - target) % 4]
        first_block = lax.rem(section + target, 4) * pair_blocks

        def note(local, count, block_list=block_list, first_block=first_block):
            for slot in range(1, slots):
                source = block_list[pair * pair_blocks + local, slot]
                item_q[count] = first_block + local
                item_k[count] = source
                wanted = source >= 0
                if not near:
                    in_section = lax.rem(jnp.maximum(source, 0), blocks_here)
                    whole = (in_section // pair_blocks != own_pair) | (
                        lax.rem(in_section, pair_blocks) == parity * (pair_blocks - 1)
                    )
                    wanted = wanted & (whole if early else jnp.logical_not(whole))
                count = count + wanted.astype(jnp.int32)
            return count

        count = lax.fori_loop(0, pair_blocks, note, count)
    for extra in range(STEP):
        item_q[count + extra] = total_blocks
        item_k[count + extra] = (own_pair if late else pair) * pair_blocks

    values_t[HD:, :] = jnp.ones((values_t.shape[0] - HD, values_t.shape[1]), jnp.bfloat16)
    if not late:
        queries[total_blocks] = jnp.zeros((wide, HD), jnp.bfloat16)
        tops[total_blocks] = jnp.zeros((8, wide), jnp.float32)
        sums[total_blocks] = jnp.zeros(sums.shape[1:], jnp.float32)

    lane = lax.broadcasted_iota(jnp.int32, (BLK, wide), 1)
    key_at = lax.broadcasted_iota(jnp.int32, (BLK, wide), 0)

    def query_place(local):
        return (core * TILE, TILE) if local == 1 else (core * wide, 0)

    def scores_of(source, query):
        at = pl.multiple_of(source * BLK, BLK)
        return lax.dot_general(
            rows[pl.ds(at, BLK), 0:HD],
            query,
            (((1,), (1,)), ((), ())),
            preferred_element_type=jnp.float32,
        )

    def weigh(source, weights):
        at = pl.multiple_of(source * BLK, BLK)
        return jnp.dot(
            values_t[:, pl.ds(at, BLK)],
            weights.astype(jnp.bfloat16),
            preferred_element_type=jnp.float32,
        )

    def masked(local, scores):
        offset, gap = query_place(local)
        query_at = offset + lane
        if gap:
            query_at = query_at + jnp.where(lane >= TILE, gap, 0)
        return jnp.where(key_at <= query_at, scores, -jnp.inf)

    def diagonal(blocks):
        scores = []
        for local, block in enumerate(blocks):
            offset, gap = query_place(local)
            start = pl.multiple_of(block * BLK + offset, TILE)
            later = pl.multiple_of(start + TILE + gap, TILE)
            query = jnp.concatenate(
                [query_rows[pl.ds(start, TILE)], query_rows[pl.ds(later, TILE)]], axis=0
            )
            queries[block] = query
            scores.append(scores_of(key_block(block), query))
        for local, (block, score) in enumerate(zip(blocks, scores)):
            score = masked(local, score)
            top = jnp.max(score, axis=0, keepdims=True)
            tops[block] = jnp.broadcast_to(top, (8, wide))
            sums[block] = weigh(key_block(block), jnp.exp2(score - top))

    def turn(first, number):
        for i in range(number):
            at = pl.multiple_of((first + i) * BLK, BLK)
            values_t[:HD, pl.ds(at, BLK)] = rows[pl.ds(at, BLK), HD : 2 * HD].T

    for shift in range(4):
        source = lax.rem(section - shift + 4, 4)
        for copy in copies[ends[shift - 1] if shift else 0 : ends[shift]]:
            copy.wait()
        if late:
            turn(source * blocks_here + own_pair * pair_blocks, pair_blocks)
        else:
            turn(source * blocks_here, blocks_here)
        if not late and (4 - shift) % 4 in targets:
            diagonal([source * pair_blocks + local for local in range(pair_blocks)])
    for copy in state_copies:
        copy.wait()

    def below(step, carry):
        items = [step * STEP + i for i in range(STEP)]
        scores = scores_of(item_k[items[0]], queries[item_q[items[0]]])
        held = None
        for i, item in enumerate(items):
            if i + 1 < STEP:
                ahead = scores_of(item_k[items[i + 1]], queries[item_q[items[i + 1]]])
            weights = jnp.exp2(scores - tops[item_q[item], 0:1]).astype(jnp.bfloat16)
            if held is not None:
                sums[item_q[items[i - 1]]] += weigh(item_k[items[i - 1]], held)
            held, scores = weights, ahead
        sums[item_q[items[-1]]] += weigh(item_k[items[-1]], held)
        return carry

    lax.fori_loop(0, (count + STEP - 1) // STEP, below, 0)
    if early:
        return

    def store(number, local, result):
        for part in range(2):
            tile = 2 * local + part
            i = tile % 3
            which = (tile // 3) ^ parity
            given = i == 2 - 2 * core
            if near:
                where = jnp.where(given, 4 + which, which * 2 + i - core)
            else:
                where = which * 3 + jnp.where(given, 2, i - core)
            outs[number][where] = result[part * TILE : (part + 1) * TILE]

    over = jnp.zeros((1, wide), jnp.float32)
    for number, target in enumerate(targets):
        for local in range(pair_blocks):
            block = lax.rem(section + target, 4) * pair_blocks + local
            total = sums[block, HD : HD + 1]
            over = jnp.maximum(over, jnp.where(total < 2.0**100, 0.0, 1.0))
            store(number, local, (sums[block, 0:HD] / total).T.astype(jnp.bfloat16))

    @pl.when(jnp.max(over) > 0)
    def _():
        if late:
            copies = fetches((2, 3), False, 16)
            for copy in copies:
                copy.start()
            for copy in copies:
                copy.wait()
            for source in range(4):
                turn(source * blocks_here, blocks_here)
        for number, target in enumerate(targets):
            block_list = lists[(4 - target) % 4]
            first_block = lax.rem(section + target, 4) * pair_blocks
            for local in range(pair_blocks):
                block = first_block + local
                home = key_block(block)
                entry = pair * pair_blocks + local
                query = queries[block]
                live = jnp.int32(0)
                for slot in range(slots):
                    live = live + (block_list[entry, slot] >= 0).astype(jnp.int32)
                scores = masked(local, scores_of(home, query))
                highest = jnp.max(scores, axis=0, keepdims=True)
                weighted = weigh(home, jnp.exp2(scores - highest))

                def one_slot(slot, state, block_list=block_list, entry=entry, query=query):
                    highest, weighted = state
                    source = block_list[entry, slot]
                    scores = scores_of(source, query)
                    new_highest = jnp.maximum(highest, jnp.max(scores, axis=0, keepdims=True))
                    weights = jnp.exp2(scores - new_highest)
                    weighted = weighted * jnp.exp2(highest - new_highest) + weigh(source, weights)
                    return (new_highest, weighted)

                _, weighted = lax.fori_loop(1, live, one_slot, (highest, weighted))
                result = weighted[0:HD] / weighted[HD : HD + 1]
                store(number, local, result.T.astype(jnp.bfloat16))


def attend(mode, place, lists, here, there, state=()):
    blocks_here, slots = lists[0].shape
    total_blocks = 2 * blocks_here
    tokens = 4 * blocks_here * BLK
    room = total_blocks * slots + STEP
    pairs = total_blocks * slots // 4
    have = (0, 2, 3) if mode == "early" else (0, 1, 2, 3)
    pieces = [piece for relative in have for piece in here[relative]]
    pieces += [piece for relative in have for piece in there[relative]]
    sums = [
        jax.ShapeDtypeStruct((total_blocks + 1, 2 * TILE, HD), jnp.bfloat16),
        jax.ShapeDtypeStruct((total_blocks + 1, 8, 2 * TILE), jnp.float32),
        jax.ShapeDtypeStruct((total_blocks + 1, HD + 16, 2 * TILE), jnp.float32),
    ]
    if mode == "early":
        outs = sums
    else:
        number = {"late": 4, "near": 3, "local": 1}[mode]
        outs = [jax.ShapeDtypeStruct((blocks_here, TILE, HD), jnp.bfloat16)] * number
    held = [] if mode == "early" else [pltpu.VMEM(each.shape, each.dtype) for each in sums]
    return pl.pallas_call(
        functools.partial(attend_kernel, mode, blocks_here),
        out_shape=outs,
        in_specs=[pl.BlockSpec(memory_space=pltpu.SMEM)] * 5
        + [pl.BlockSpec(memory_space=pl.ANY)] * (len(pieces) + len(state)),
        out_specs=[pl.BlockSpec(memory_space=pltpu.VMEM)] * len(outs),
        scratch_shapes=[
            pltpu.VMEM((tokens, 2 * HD), jnp.bfloat16),
            pltpu.VMEM((tokens // 2, HD), jnp.bfloat16),
            pltpu.VMEM((HD + 16, tokens), jnp.bfloat16),
            *held,
            pltpu.SMEM((room,), jnp.int32),
            pltpu.SMEM((room,), jnp.int32),
            pltpu.SemaphoreType.DMA((51,)),
        ],
        compiler_params=pltpu.CompilerParams(vmem_limit_bytes=VMEM_LIMIT),
        cost_estimate=pl.CostEstimate(
            flops=pairs * 4 * BLK * 2 * TILE * HD,
            bytes_accessed=tokens * 5 * HD,
            transcendentals=pairs * BLK * 2 * TILE,
        ),
        name="attend_" + mode,
    )(place, *lists, *pieces, *state)


def finish_kernel(relatives, kept_parts, place, *rest):
    number = len(relatives)
    kept = []
    for parts in kept_parts:
        kept.append(rest[:parts])
        rest = rest[parts:]
    given, rest = rest[:number], rest[number:]
    w_out, before, out, attended, weights, sems, given_sems, weight_sems = rest
    section, chip, core = place[0], place[1], place[2]
    odd = lax.rem(chip, 2)
    depth = 4 * HD
    copies, weight_copies = [], []
    for r, relative in enumerate(relatives):
        start = pl.multiple_of((chip ^ relative) * depth, depth)
        weight_copies.append(
            pltpu.make_async_copy(
                w_out.at[pl.ds(start, depth)],
                weights.at[pl.ds(r * depth, depth)],
                weight_sems.at[r],
            )
        )
        for shift in range(4):
            head = r * 4 + lax.rem(section - shift + 4, 4)
            column = pl.ds(pl.multiple_of(head * HD, HD), HD)
            for slot in range(2):
                to = jnp.where(core == 0, slot * (1 + odd), odd if slot == 0 else 2)
                source = kept[r][0].at[shift] if kept_parts[r] == 1 else kept[r][shift]
                copies.append(
                    pltpu.make_async_copy(
                        source.at[slot],
                        attended.at[pl.ds(pl.multiple_of(to * TILE, TILE), TILE), column],
                        sems.at[(r * 4 + shift) * 2 + slot],
                    )
                )
            to = jnp.where(core == 0, 2 - odd, 1 - odd)
            copies.append(
                pltpu.make_async_copy(
                    given[r].at[shift, 0],
                    attended.at[pl.ds(pl.multiple_of(to * TILE, TILE), TILE), column],
                    given_sems.at[r * 4 + shift],
                )
            )
    for copy in weight_copies + copies:
        copy.start()
    for copy in copies + weight_copies:
        copy.wait()
    half = out.shape[0] // 2
    step = 256
    for column in range(0, out.shape[1], step):
        for at in range(0, out.shape[0], half):
            piece = (slice(at, at + half), slice(column, column + step))
            summed = jnp.dot(
                attended[at : at + half],
                weights[:, column : column + step],
                preferred_element_type=jnp.float32,
            )
            out[piece] = (before[piece].astype(jnp.float32) + summed).astype(out.dtype)


def finish(relatives, place, kept, given, w_out, before, last):
    count = before.shape[0]
    number = len(relatives)
    any_space = pl.BlockSpec(memory_space=pl.ANY)
    vmem = pl.BlockSpec(memory_space=pltpu.VMEM)
    depth = number * 4 * HD
    return pl.pallas_call(
        functools.partial(finish_kernel, relatives, [len(parts) for parts in kept]),
        out_shape=jax.ShapeDtypeStruct((count, D), jnp.bfloat16 if last else jnp.float32),
        in_specs=[pl.BlockSpec(memory_space=pltpu.SMEM)] + [any_space] * (sum(map(len, kept)) + number + 1) + [vmem],
        out_specs=vmem,
        scratch_shapes=[
            pltpu.VMEM((count, depth), jnp.bfloat16),
            pltpu.VMEM((depth, D), jnp.bfloat16),
            pltpu.SemaphoreType.DMA((number * 8,)),
            pltpu.SemaphoreType.DMA((number * 4,)),
            pltpu.SemaphoreType.DMA((number,)),
        ],
        compiler_params=pltpu.CompilerParams(vmem_limit_bytes=VMEM_LIMIT),
        cost_estimate=pl.CostEstimate(
            flops=2 * count * D * depth, bytes_accessed=2 * D * depth, transcendentals=0
        ),
        name="project_out_last" if last else "project_out_first",
    )(place, *[part for parts in kept for part in parts], *given, w_out, before)


def by_head(hidden_in, norm_gain, w_qkv, w_out, block_lists):
    section = lax.axis_index("section")
    device = lax.axis_index("head")
    chip, core = device // 2, device % 2
    blocks_here = block_lists.shape[0]
    tok = blocks_here * BLK
    rows = hidden_in.shape[0]
    half = rows // 2

    other_core = [(i, i ^ 1) for i in range(8)]
    along_x = [(i, i ^ 2) for i in range(8)]
    along_y = [(i, i ^ 4) for i in range(8)]

    def to_section(array, shift):
        return lax.ppermute(array, "section", [(i, (i + shift) % 4) for i in range(4)])

    place = jnp.stack([section, chip, core]).astype(jnp.int32)
    shifts = jnp.arange(4, dtype=jnp.int32)
    chosen = (section + shifts - 2 * core + 4) % 4

    own = jnp.transpose(w_qkv, (1, 0, 2))
    other = lax.ppermute(own, "head", other_core)
    hidden_in, own = lax.optimization_barrier((hidden_in, own))

    resid = hidden_in.astype(jnp.float32)
    normed = (
        resid * lax.rsqrt(jnp.mean(resid * resid, axis=-1, keepdims=True) + EPS) * norm_gain
    ).astype(jnp.bfloat16)
    y_rows = lax.ppermute(normed, "head", along_y)
    x_rows = lax.ppermute(normed, "head", along_x)

    frequency = THETA ** (-(2.0 * jnp.arange(HD // 2, dtype=jnp.float32)) / HD)

    def projected(relatives, pieces):
        starts = section * tok + (chip ^ jnp.array(relatives)) * (2 * rows) + core * rows
        positions = (starts[:, None] + jnp.arange(rows, dtype=jnp.int32)[None, :]).reshape(-1)
        angle = positions.astype(jnp.float32)[:, None] * frequency
        cosine, sine = jnp.cos(angle), jnp.sin(angle)
        cosine = jnp.concatenate([cosine, cosine], axis=-1)
        sine = jnp.concatenate([-sine, sine], axis=-1)
        return project(chosen, pieces, own, other, cosine, sine)

    def sent(outs):
        return [outs[0]] + [to_section(outs[shift], shift) for shift in range(1, 4)]

    def to_other(array):
        return lax.ppermute(array, "head", other_core)

    def after(first, second):
        joined = lax.optimization_barrier((*first, *second))
        return list(joined[: len(first)]), list(joined[len(first) :])

    own_parts = sent(projected([0], [normed]))
    y_outs = projected([2], [y_rows])
    own_parts, held = after(own_parts, [x_rows[half:], y_rows[:half], *y_outs])
    x_high, y_low, *y_outs = held
    d_low = lax.ppermute(y_low, "head", along_x)
    d_high = lax.ppermute(x_high, "head", along_y)
    y_parts = sent(y_outs)
    d_outs = projected([3], [d_low, d_high])
    y_parts, held = after(y_parts, [block_lists, w_out, x_rows, *d_outs])
    block_lists, w_out, x_rows, *d_outs = held
    lists = [block_lists] + [to_section(block_lists, shift) for shift in range(1, 4)]
    w_out_all = lax.all_gather(w_out, "head", axis=0, tiled=True)
    d_parts = sent(d_outs)
    d_parts, x_outs = after(d_parts, projected([1], [x_rows]))
    x_parts = sent(x_outs)

    here = {0: own_parts, 1: x_parts, 2: y_parts, 3: d_parts}
    there = {relative: [to_other(jnp.stack(here[relative]))] for relative in (0, 2, 3)}
    state = attend("early", place, lists, here, there)
    x_parts, state = after(x_parts, state)
    here[1], there[1] = x_parts, [to_other(part) for part in x_parts]

    def to_chip(array, relative, cross):
        flip = 2 * relative + (1 if cross else 0)
        return lax.ppermute(array, "head", [(i, i ^ flip) for i in range(8)])

    far = attend("late", place, lists, here, there, state)
    far = [far[0]] + [to_section(far[shift], shift) for shift in range(1, 4)]
    near = attend("near", place, lists, here, there)
    near, (place, *far) = after(near, [place, *far])
    y_part = to_chip(jnp.stack([part[0:3] for part in far]), 2, False)
    d_part = to_chip(jnp.stack([part[3:6] for part in far]), 3, False)
    near = [to_section(near[shift - 1], shift) for shift in range(1, 4)]
    near = [*attend("local", place, lists, here, there), *near]
    swapped = to_other(jnp.stack([y_part[:, 2:3], d_part[:, 2:3]]))
    partial = finish(
        (2, 3), place, [[y_part], [d_part]], [swapped[0], swapped[1]], w_out_all, hidden_in, False
    )
    x_kept = to_chip(jnp.stack([part[2:4] for part in near]), 1, False)
    x_given = to_chip(jnp.stack([part[5:6] for part in near]), 1, True)
    (own_given,), (partial,) = after([jnp.stack([part[4:5] for part in near])], [partial])
    own_given = to_other(own_given)
    return finish((0, 1), place, [near, [x_kept]], [own_given, x_given], w_out_all, partial, True)


def solution(mesh):
    placed = (
        P(("section", "head"), None),
        P(),
        P(None, None, "head"),
        P("head", None),
        P("section", None),
    )

    def local(hidden_in, norm_gain, w_qkv, w_out, block_lists):
        fits = (
            mesh.shape["section"] == 4
            and mesh.shape["head"] == 8
            and w_qkv.shape[2] == 2 * HD
            and block_lists.shape[0] == 6
            and hidden_in.shape[0] == 3 * TILE
        )
        form = by_head if fits else general
        return form(hidden_in, norm_gain, w_qkv, w_out, block_lists)

    return jax.shard_map(
        local, mesh=mesh, in_specs=placed, out_specs=P(("section", "head"), None), check_vma=False
    )
```

```python
import functools
import math

import jax
import jax.numpy as jnp
from jax import lax
from jax.experimental import pallas as pl
from jax.experimental.pallas import tpu as pltpu
from jax.sharding import PartitionSpec as P

D = 2048
HD = 128
BLK = 512
TILE = 128
STEP = 12


EPS = 1e-05
THETA = 10000.0
VMEM_LIMIT = 56 * 1024 * 1024


def rotate(vectors, cosine, sine):
    half = vectors.shape[-1] // 2
    first = vectors[..., :half]
    second = vectors[..., half:]
    return jnp.concatenate(
        [first * cosine - second * sine, second * cosine + first * sine], axis=-1
    )


def general(hidden_in, norm_gain, w_qkv, w_out, block_lists):
    section_id = lax.axis_index("section")
    width = w_qkv.shape[2]
    heads_here = width // HD
    blocks_here = block_lists.shape[0]
    tok_dev = blocks_here * BLK
    scale = 1.0 / math.sqrt(HD)
    resid = hidden_in.astype(jnp.float32)
    normed = (
        resid * lax.rsqrt(jnp.mean(resid * resid, axis=-1, keepdims=True) + EPS) * norm_gain
    ).astype(jnp.bfloat16)
    flat_weight = w_qkv.reshape(D, 3 * width)
    frequency = THETA ** (-(2.0 * jnp.arange(HD // 2, dtype=jnp.float32)) / HD)
    piece = lax.all_gather(normed, "head", axis=0, tiled=True)
    count = piece.shape[0]
    mixed_rows = jnp.dot(piece, flat_weight, preferred_element_type=jnp.float32).reshape(
        count, 3, heads_here, HD
    )
    positions = (section_id * tok_dev + jnp.arange(count, dtype=jnp.int32)).astype(jnp.float32)
    angle = positions[:, None] * frequency[None, :]
    cosine = jnp.cos(angle)[:, None, :]
    sine = jnp.sin(angle)[:, None, :]
    query = rotate(mixed_rows[:, 0], cosine, sine).astype(jnp.bfloat16).reshape(count, width)
    keys = rotate(mixed_rows[:, 1], cosine, sine).astype(jnp.bfloat16).reshape(count, width)
    values = mixed_rows[:, 2].astype(jnp.bfloat16).reshape(count, width)
    keys_all, values_all = (
        lax.all_gather(keys, "section", axis=0, tiled=True),
        lax.all_gather(values, "section", axis=0, tiled=True),
    )
    count_blocks = block_lists.shape[0]
    query_blocks = query.reshape(count_blocks, BLK, heads_here, HD)
    block_ids = section_id * blocks_here + jnp.arange(count_blocks, dtype=jnp.int32)

    def one_block(carry, item):
        query_block, block_row, block_id = item
        live_slots = jnp.sum((block_row >= 0).astype(jnp.int32))
        query_positions = block_id * BLK + jnp.arange(BLK, dtype=jnp.int32)

        def one_slot(slot, state):
            highest, total, weighted = state
            source = block_row[slot]
            key_block = lax.dynamic_slice_in_dim(keys_all, source * BLK, BLK, 0).reshape(
                BLK, heads_here, HD
            )
            value_block = lax.dynamic_slice_in_dim(values_all, source * BLK, BLK, 0).reshape(
                BLK, heads_here, HD
            )
            scores = (
                jnp.einsum(
                    "qhd,khd->hqk", query_block, key_block, preferred_element_type=jnp.float32
                )
                * scale
            )
            key_positions = source * BLK + jnp.arange(BLK, dtype=jnp.int32)
            scores = jnp.where(
                key_positions[None, None, :] <= query_positions[None, :, None], scores, -jnp.inf
            )
            new_highest = jnp.maximum(highest, jnp.max(scores, axis=-1))
            factor = jnp.exp(highest - new_highest)
            weights = jnp.exp(scores - new_highest[..., None])
            total = total * factor + jnp.sum(weights, axis=-1)
            update = jnp.einsum(
                "hqk,khd->hqd",
                weights.astype(jnp.bfloat16),
                value_block,
                preferred_element_type=jnp.float32,
            )
            weighted = weighted * factor[..., None] + update
            return (new_highest, total, weighted)

        start_state = (
            jnp.full((heads_here, BLK), -jnp.inf, jnp.float32),
            jnp.zeros((heads_here, BLK), jnp.float32),
            jnp.zeros((heads_here, BLK, HD), jnp.float32),
        )
        highest, total, weighted = lax.fori_loop(0, live_slots, one_slot, start_state)
        result = (
            (weighted / total[..., None])
            .transpose(1, 0, 2)
            .reshape(BLK, width)
            .astype(jnp.bfloat16)
        )
        return (carry, result)

    _, results = lax.scan(
        one_block, jnp.zeros((), jnp.int32), (query_blocks, block_lists, block_ids)
    )
    attended = results.reshape(count_blocks * BLK, width)
    regrouped = lax.all_to_all(attended, "head", split_axis=0, concat_axis=1, tiled=True)
    summed = jnp.dot(
        regrouped,
        lax.all_gather(w_out, "head", axis=0, tiled=True),
        preferred_element_type=jnp.float32,
    )
    return (resid + summed).astype(jnp.bfloat16)


def project_kernel(number, noted, place, *rest):
    pieces, rest = rest[:number], rest[number:]
    if noted:
        note, rest = rest[0], rest[1:]
    own, other, cosine, sine = rest[:4]
    outs, rest = rest[4:8], rest[8:]
    rows, weights, results, row_sems, weight_sems, out_sems = rest
    count = rows.shape[0]
    row_copies, start = [], 0
    for i, ref in enumerate(pieces):
        size = ref.shape[0]
        row_copies.append(
            pltpu.make_async_copy(ref, rows.at[pl.ds(start, size)], row_sems.at[i])
        )
        start += size
    weight_copies = [
        pltpu.make_async_copy(
            ref.at[part],
            weights.at[w * 3 + part],
            weight_sems.at[w * 3 + part],
        )
        for w, ref in enumerate((own, other))
        for part in range(3)
    ]
    for copy in row_copies + weight_copies[:2]:
        copy.start()
    for copy in row_copies:
        copy.wait()
    query_scale = math.log2(math.e) / math.sqrt(HD)
    step = count // 2

    def out_copy(result, shift):
        return pltpu.make_async_copy(results.at[result], outs[shift], out_sems.at[shift])

    if noted:
        for result in range(4):
            results[result, count:, :] = note[...]

    for w in range(2):
        for part in range(3):
            weight_copies[w * 3 + part].wait()
            if w * 3 + part + 2 < 6:
                weight_copies[w * 3 + part + 2].start()
            for at in range(0, count, step):
                piece = slice(at, at + step)
                product = jnp.dot(
                    rows[piece], weights[w * 3 + part], preferred_element_type=jnp.float32
                )
                for h in range(2):
                    vector = product[:, h * HD : (h + 1) * HD]
                    if part < 2:
                        turned = pltpu.roll(vector, HD // 2, 1)
                        vector = vector * cosine[piece] + turned * sine[piece]
                    if part == 0:
                        vector = vector * query_scale
                    column = slice(part * HD, (part + 1) * HD)
                    results[w * 2 + h, piece, column] = vector.astype(jnp.bfloat16)
        for h in range(2):
            for shift in range(4):

                @pl.when(place[shift] == w * 2 + h)
                def _(shift=shift, result=w * 2 + h):
                    out_copy(result, shift).start()

    for shift in range(4):
        out_copy(0, shift).wait()


def project(place, pieces, own, other, cosine, sine, note=None):
    count = sum(piece.shape[0] for piece in pieces)
    number = len(pieces)
    width = own.shape[2]
    notes = [] if note is None else [note]
    full = count + sum(each.shape[0] for each in notes)
    any_space = pl.BlockSpec(memory_space=pl.ANY)
    vmem = pl.BlockSpec(memory_space=pltpu.VMEM)
    return pl.pallas_call(
        functools.partial(project_kernel, number, len(notes) > 0),
        out_shape=[jax.ShapeDtypeStruct((full, 3 * HD), jnp.bfloat16)] * 4,
        in_specs=[pl.BlockSpec(memory_space=pltpu.SMEM)] + [any_space] * number
        + [vmem] * len(notes)
        + [any_space] * 2
        + [vmem] * 2,
        out_specs=[any_space] * 4,
        scratch_shapes=[
            pltpu.VMEM((count, D), jnp.bfloat16),
            pltpu.VMEM((6, D, width), jnp.bfloat16),
            pltpu.VMEM((4, full, 3 * HD), jnp.bfloat16),
            pltpu.SemaphoreType.DMA((number,)),
            pltpu.SemaphoreType.DMA((6,)),
            pltpu.SemaphoreType.DMA((4,)),
        ],
        compiler_params=pltpu.CompilerParams(vmem_limit_bytes=VMEM_LIMIT),
        cost_estimate=pl.CostEstimate(
            flops=2 * count * D * 6 * width, bytes_accessed=2 * 6 * D * width, transcendentals=0
        ),
        name="project_and_rotate",
    )(place, *pieces, *notes, own, other, cosine, sine)


def attend_kernel(mode, blocks_here, place, *refs):
    refs = list(refs)

    def take(number):
        taken = refs[:number]
        del refs[:number]
        return taken

    near, early, late = mode in ("near", "local"), mode == "early", mode == "late"
    targets = {"near": (1, 2, 3), "local": (0,)}.get(mode, (0, 1, 2, 3))
    lists = take(4)
    have = (0, 2, 3) if early else (0, 1, 2, 3)
    here = {relative: take(4) for relative in have}
    there = {relative: take(4 if relative == 1 else 1) for relative in have}
    state = take(3) if late else []
    outs = take(3 if early else len(targets))
    if early:
        queries, tops, sums = outs
        rows, query_rows, values_t, item_q, item_k, sems = refs
    else:
        rows, query_rows, values_t, queries, tops, sums, item_q, item_k, sems = refs
    section, chip, core = place[0], place[1], place[2]
    rows_here = here[2][0].shape[0]
    tok = blocks_here * BLK
    slots = lists[0].shape[1]
    wide = 2 * TILE
    pair_blocks = blocks_here // 2
    total_blocks = 4 * pair_blocks
    own_pair = chip // 2
    pair = own_pair if near else 1 - own_pair
    parity = lax.rem(chip, 2)

    ends = []

    def fetches(relatives, with_queries, first):
        copies = []
        ends.clear()
        for shift in range(4):
            for relative in relatives:
                owner = chip ^ relative
                source = lax.rem(section - shift + 4, 4)
                for far in range(2):
                    side = core if far == 0 else 1 - core
                    if far == 0:
                        ref = here[relative][shift]
                    elif relative == 1:
                        ref = there[relative][shift]
                    else:
                        ref = there[relative][0].at[shift]
                    start = source * tok + owner * (2 * rows_here) + side * rows_here
                    start = pl.multiple_of(start, rows_here)
                    copies.append(
                        pltpu.make_async_copy(
                            ref.at[pl.ds(0, rows_here), pl.ds(HD, 2 * HD)],
                            rows.at[pl.ds(start, rows_here)],
                            sems.at[first + len(copies)],
                        )
                    )
                    if not with_queries or (relative < 2) != near or (4 - shift) % 4 not in targets:
                        continue
                    start = source * (tok // 2) + lax.rem(owner, 2) * (2 * rows_here)
                    start = pl.multiple_of(start + side * rows_here, rows_here)
                    copies.append(
                        pltpu.make_async_copy(
                            ref.at[pl.ds(0, rows_here), pl.ds(0, HD)],
                            query_rows.at[pl.ds(start, rows_here)],
                            sems.at[first + len(copies)],
                        )
                    )
            ends.append(len(copies))
        return copies

    def key_block(block):
        return block // pair_blocks * blocks_here + pair * pair_blocks + lax.rem(block, pair_blocks)

    copies = fetches((0, 1) if late else have, not late, 0)
    state_copies = [
        pltpu.make_async_copy(ref, held, sems.at[48 + i])
        for i, (ref, held) in enumerate(zip(state, (queries, tops, sums)))
    ]
    for copy in copies + state_copies:
        copy.start()

    count = jnp.int32(0)
    for target in targets:
        block_list = lists[(4 - target) % 4]
        first_block = lax.rem(section + target, 4) * pair_blocks

        def note(local, count, block_list=block_list, first_block=first_block):
            for slot in range(1, slots):
                source = block_list[pair * pair_blocks + local, slot]
                item_q[count] = first_block + local
                item_k[count] = source
                wanted = source >= 0
                if not near:
                    in_section = lax.rem(jnp.maximum(source, 0), blocks_here)
                    whole = (in_section // pair_blocks != own_pair) | (
                        lax.rem(in_section, pair_blocks) == parity * (pair_blocks - 1)
                    )
                    wanted = wanted & (whole if early else jnp.logical_not(whole))
                count = count + wanted.astype(jnp.int32)
            return count

        count = lax.fori_loop(0, pair_blocks, note, count)
    for extra in range(STEP):
        item_q[count + extra] = total_blocks
        item_k[count + extra] = (own_pair if late else pair) * pair_blocks

    values_t[HD:, :] = jnp.ones((values_t.shape[0] - HD, values_t.shape[1]), jnp.bfloat16)
    if not late:
        queries[total_blocks] = jnp.zeros((wide, HD), jnp.bfloat16)
        tops[total_blocks] = jnp.zeros((8, wide), jnp.float32)
        sums[total_blocks] = jnp.zeros(sums.shape[1:], jnp.float32)

    lane = lax.broadcasted_iota(jnp.int32, (BLK, wide), 1)
    key_at = lax.broadcasted_iota(jnp.int32, (BLK, wide), 0)

    def query_place(local):
        return (core * TILE, TILE) if local == 1 else (core * wide, 0)

    def scores_of(source, query):
        at = pl.multiple_of(source * BLK, BLK)
        return lax.dot_general(
            rows[pl.ds(at, BLK), 0:HD],
            query,
            (((1,), (1,)), ((), ())),
            preferred_element_type=jnp.float32,
        )

    def weigh(source, weights):
        at = pl.multiple_of(source * BLK, BLK)
        return jnp.dot(
            values_t[:, pl.ds(at, BLK)],
            weights.astype(jnp.bfloat16),
            preferred_element_type=jnp.float32,
        )

    def masked(local, scores):
        offset, gap = query_place(local)
        query_at = offset + lane
        if gap:
            query_at = query_at + jnp.where(lane >= TILE, gap, 0)
        return jnp.where(key_at <= query_at, scores, -jnp.inf)

    def diagonal(blocks):
        scores = []
        for local, block in enumerate(blocks):
            offset, gap = query_place(local)
            start = pl.multiple_of(block * BLK + offset, TILE)
            later = pl.multiple_of(start + TILE + gap, TILE)
            query = jnp.concatenate(
                [query_rows[pl.ds(start, TILE)], query_rows[pl.ds(later, TILE)]], axis=0
            )
            queries[block] = query
            scores.append(scores_of(key_block(block), query))
        for local, (block, score) in enumerate(zip(blocks, scores)):
            score = masked(local, score)
            top = jnp.max(score, axis=0, keepdims=True)
            tops[block] = jnp.broadcast_to(top, (8, wide))
            sums[block] = weigh(key_block(block), jnp.exp2(score - top))

    def turn(first, number):
        for i in range(number):
            at = pl.multiple_of((first + i) * BLK, BLK)
            values_t[:HD, pl.ds(at, BLK)] = rows[pl.ds(at, BLK), HD : 2 * HD].T

    for shift in range(4):
        source = lax.rem(section - shift + 4, 4)
        for copy in copies[ends[shift - 1] if shift else 0 : ends[shift]]:
            copy.wait()
        if late:
            turn(source * blocks_here + own_pair * pair_blocks, pair_blocks)
        else:
            turn(source * blocks_here, blocks_here)
        if not late and (4 - shift) % 4 in targets:
            diagonal([source * pair_blocks + local for local in range(pair_blocks)])
    for copy in state_copies:
        copy.wait()

    def below(step, carry):
        items = [step * STEP + i for i in range(STEP)]
        scores = scores_of(item_k[items[0]], queries[item_q[items[0]]])
        held = None
        for i, item in enumerate(items):
            if i + 1 < STEP:
                ahead = scores_of(item_k[items[i + 1]], queries[item_q[items[i + 1]]])
            weights = jnp.exp2(scores - tops[item_q[item], 0:1]).astype(jnp.bfloat16)
            if held is not None:
                sums[item_q[items[i - 1]]] += weigh(item_k[items[i - 1]], held)
            held, scores = weights, ahead
        sums[item_q[items[-1]]] += weigh(item_k[items[-1]], held)
        return carry

    lax.fori_loop(0, (count + STEP - 1) // STEP, below, 0)
    if early:
        return

    def store(number, local, result):
        for part in range(2):
            tile = 2 * local + part
            i = tile % 3
            which = (tile // 3) ^ parity
            given = i == 2 - 2 * core
            if near:
                where = jnp.where(given, 4 + which, which * 2 + i - core)
            else:
                where = which * 3 + jnp.where(given, 2, i - core)
            outs[number][where] = result[part * TILE : (part + 1) * TILE]

    over = jnp.zeros((1, wide), jnp.float32)
    for number, target in enumerate(targets):
        for local in range(pair_blocks):
            block = lax.rem(section + target, 4) * pair_blocks + local
            total = sums[block, HD : HD + 1]
            over = jnp.maximum(over, jnp.where(total < 2.0**100, 0.0, 1.0))
            store(number, local, (sums[block, 0:HD] / total).T.astype(jnp.bfloat16))

    @pl.when(jnp.max(over) > 0)
    def _():
        if late:
            copies = fetches((2, 3), False, 16)
            for copy in copies:
                copy.start()
            for copy in copies:
                copy.wait()
            for source in range(4):
                turn(source * blocks_here, blocks_here)
        for number, target in enumerate(targets):
            block_list = lists[(4 - target) % 4]
            first_block = lax.rem(section + target, 4) * pair_blocks
            for local in range(pair_blocks):
                block = first_block + local
                home = key_block(block)
                entry = pair * pair_blocks + local
                query = queries[block]
                live = jnp.int32(0)
                for slot in range(slots):
                    live = live + (block_list[entry, slot] >= 0).astype(jnp.int32)
                scores = masked(local, scores_of(home, query))
                highest = jnp.max(scores, axis=0, keepdims=True)
                weighted = weigh(home, jnp.exp2(scores - highest))

                def one_slot(slot, state, block_list=block_list, entry=entry, query=query):
                    highest, weighted = state
                    source = block_list[entry, slot]
                    scores = scores_of(source, query)
                    new_highest = jnp.maximum(highest, jnp.max(scores, axis=0, keepdims=True))
                    weights = jnp.exp2(scores - new_highest)
                    weighted = weighted * jnp.exp2(highest - new_highest) + weigh(source, weights)
                    return (new_highest, weighted)

                _, weighted = lax.fori_loop(1, live, one_slot, (highest, weighted))
                result = weighted[0:HD] / weighted[HD : HD + 1]
                store(number, local, result.T.astype(jnp.bfloat16))


def attend(mode, place, lists, here, there, state=()):
    blocks_here, slots = lists[0].shape
    total_blocks = 2 * blocks_here
    tokens = 4 * blocks_here * BLK
    room = total_blocks * slots + STEP
    pairs = total_blocks * slots // 4
    have = (0, 2, 3) if mode == "early" else (0, 1, 2, 3)
    pieces = [piece for relative in have for piece in here[relative]]
    pieces += [piece for relative in have for piece in there[relative]]
    sums = [
        jax.ShapeDtypeStruct((total_blocks + 1, 2 * TILE, HD), jnp.bfloat16),
        jax.ShapeDtypeStruct((total_blocks + 1, 8, 2 * TILE), jnp.float32),
        jax.ShapeDtypeStruct((total_blocks + 1, HD + 16, 2 * TILE), jnp.float32),
    ]
    if mode == "early":
        outs = sums
    else:
        number = {"late": 4, "near": 3, "local": 1}[mode]
        outs = [jax.ShapeDtypeStruct((blocks_here, TILE, HD), jnp.bfloat16)] * number
    held = [] if mode == "early" else [pltpu.VMEM(each.shape, each.dtype) for each in sums]
    return pl.pallas_call(
        functools.partial(attend_kernel, mode, blocks_here),
        out_shape=outs,
        in_specs=[pl.BlockSpec(memory_space=pltpu.SMEM)] * 5
        + [pl.BlockSpec(memory_space=pl.ANY)] * (len(pieces) + len(state)),
        out_specs=[pl.BlockSpec(memory_space=pltpu.VMEM)] * len(outs),
        scratch_shapes=[
            pltpu.VMEM((tokens, 2 * HD), jnp.bfloat16),
            pltpu.VMEM((tokens // 2, HD), jnp.bfloat16),
            pltpu.VMEM((HD + 16, tokens), jnp.bfloat16),
            *held,
            pltpu.SMEM((room,), jnp.int32),
            pltpu.SMEM((room,), jnp.int32),
            pltpu.SemaphoreType.DMA((51,)),
        ],
        compiler_params=pltpu.CompilerParams(vmem_limit_bytes=VMEM_LIMIT),
        cost_estimate=pl.CostEstimate(
            flops=pairs * 4 * BLK * 2 * TILE * HD,
            bytes_accessed=tokens * 5 * HD,
            transcendentals=pairs * BLK * 2 * TILE,
        ),
        name="attend_" + mode,
    )(place, *lists, *pieces, *state)


def finish_kernel(relatives, kept_parts, place, *rest):
    number = len(relatives)
    kept = []
    for parts in kept_parts:
        kept.append(rest[:parts])
        rest = rest[parts:]
    given, rest = rest[:number], rest[number:]
    w_out, hidden, out, attended, weights, sums, sems, given_sems, weight_sems = rest
    section, chip, core = place[0], place[1], place[2]
    odd = lax.rem(chip, 2)
    depth = 4 * HD
    copies = []
    for r, relative in enumerate(relatives):
        start = pl.multiple_of((chip ^ relative) * depth, depth)
        group = [
            pltpu.make_async_copy(w_out.at[pl.ds(start, depth)], weights.at[r], weight_sems.at[r])
        ]
        for shift in range(4):
            head = lax.rem(section - shift + 4, 4)
            column = pl.ds(pl.multiple_of(head * HD, HD), HD)
            for slot in range(2):
                to = jnp.where(core == 0, slot * (1 + odd), odd if slot == 0 else 2)
                source = kept[r][0].at[shift] if kept_parts[r] == 1 else kept[r][shift]
                group.append(
                    pltpu.make_async_copy(
                        source.at[slot],
                        attended.at[r, pl.ds(pl.multiple_of(to * TILE, TILE), TILE), column],
                        sems.at[(r * 4 + shift) * 2 + slot],
                    )
                )
            to = jnp.where(core == 0, 2 - odd, 1 - odd)
            group.append(
                pltpu.make_async_copy(
                    given[r].at[shift, 0],
                    attended.at[r, pl.ds(pl.multiple_of(to * TILE, TILE), TILE), column],
                    given_sems.at[r * 4 + shift],
                )
            )
        copies.append(group)
    for copy in copies[0] + copies[1]:
        copy.start()
    half = out.shape[0] // 2
    step = 512
    for r in range(number):
        for copy in copies[r]:
            copy.wait()
        if r + 2 < number:
            for copy in copies[r + 2]:
                copy.start()
        for column in range(0, out.shape[1], step):
            for at in range(0, out.shape[0], half):
                piece = (slice(at, at + half), slice(column, column + step))
                summed = jnp.dot(
                    attended[r, at : at + half],
                    weights[r, :, column : column + step],
                    preferred_element_type=jnp.float32,
                )
                summed = summed + (hidden[piece].astype(jnp.float32) if r == 0 else sums[piece])
                if r + 1 < number:
                    sums[piece] = summed
                else:
                    out[piece] = summed.astype(out.dtype)


def finish(relatives, place, kept, given, w_out, hidden):
    count = hidden.shape[0]
    number = len(relatives)
    any_space = pl.BlockSpec(memory_space=pl.ANY)
    vmem = pl.BlockSpec(memory_space=pltpu.VMEM)
    depth = 4 * HD
    return pl.pallas_call(
        functools.partial(finish_kernel, relatives, [len(parts) for parts in kept]),
        out_shape=jax.ShapeDtypeStruct((count, D), jnp.bfloat16),
        in_specs=[pl.BlockSpec(memory_space=pltpu.SMEM)]
        + [any_space] * (sum(map(len, kept)) + number + 1)
        + [vmem],
        out_specs=vmem,
        scratch_shapes=[
            pltpu.VMEM((number, count, depth), jnp.bfloat16),
            pltpu.VMEM((number, depth, D), jnp.bfloat16),
            pltpu.VMEM((count, D), jnp.float32),
            pltpu.SemaphoreType.DMA((number * 8,)),
            pltpu.SemaphoreType.DMA((number * 4,)),
            pltpu.SemaphoreType.DMA((number,)),
        ],
        compiler_params=pltpu.CompilerParams(vmem_limit_bytes=VMEM_LIMIT),
        cost_estimate=pl.CostEstimate(
            flops=2 * count * D * D, bytes_accessed=2 * D * D, transcendentals=0
        ),
        name="project_out",
    )(place, *[part for parts in kept for part in parts], *given, w_out, hidden)


def by_head(hidden_in, norm_gain, w_qkv, w_out, block_lists):
    section = lax.axis_index("section")
    device = lax.axis_index("head")
    chip, core = device // 2, device % 2
    blocks_here = block_lists.shape[0]
    tok = blocks_here * BLK
    rows = hidden_in.shape[0]
    half = rows // 2

    other_core = [(i, i ^ 1) for i in range(8)]
    along_x = [(i, i ^ 2) for i in range(8)]
    along_y = [(i, i ^ 4) for i in range(8)]

    def to_section(array, shift):
        return lax.ppermute(array, "section", [(i, (i + shift) % 4) for i in range(4)])

    place = jnp.stack([section, chip, core]).astype(jnp.int32)
    shifts = jnp.arange(4, dtype=jnp.int32)
    chosen = (section + shifts - 2 * core + 4) % 4

    own = jnp.transpose(w_qkv, (1, 0, 2))
    other = lax.ppermute(own, "head", other_core)
    hidden_in, own = lax.optimization_barrier((hidden_in, own))

    resid = hidden_in.astype(jnp.float32)
    normed = (
        resid * lax.rsqrt(jnp.mean(resid * resid, axis=-1, keepdims=True) + EPS) * norm_gain
    ).astype(jnp.bfloat16)
    y_rows = lax.ppermute(normed, "head", along_y)
    x_rows = lax.ppermute(normed, "head", along_x)

    frequency = THETA ** (-(2.0 * jnp.arange(HD // 2, dtype=jnp.float32)) / HD)

    def projected(relatives, pieces, note=None):
        starts = section * tok + (chip ^ jnp.array(relatives)) * (2 * rows) + core * rows
        positions = (starts[:, None] + jnp.arange(rows, dtype=jnp.int32)[None, :]).reshape(-1)
        angle = positions.astype(jnp.float32)[:, None] * frequency
        cosine, sine = jnp.cos(angle), jnp.sin(angle)
        cosine = jnp.concatenate([cosine, cosine], axis=-1)
        sine = jnp.concatenate([-sine, sine], axis=-1)
        return project(chosen, pieces, own, other, cosine, sine, note)

    def sent(outs):
        return [outs[0]] + [to_section(outs[shift], shift) for shift in range(1, 4)]

    def to_other(array):
        return lax.ppermute(array, "head", other_core)

    def after(first, second):
        joined = lax.optimization_barrier((*first, *second))
        return list(joined[: len(first)]), list(joined[len(first) :])

    note = jnp.pad(
        block_lists.astype(jnp.bfloat16),
        ((0, 16 - blocks_here), (0, 3 * HD - block_lists.shape[1])),
    )
    own_parts = sent(projected([0], [normed], note))
    y_outs = projected([2], [y_rows])
    own_parts, held = after(own_parts, [x_rows[half:], y_rows[:half], *y_outs])
    x_high, y_low, *y_outs = held
    d_low = lax.ppermute(y_low, "head", along_x)
    d_high = lax.ppermute(x_high, "head", along_y)
    y_parts = sent(y_outs)
    d_outs = projected([3], [d_low, d_high])
    y_parts, held = after(y_parts, [w_out, x_rows, *d_outs])
    w_out, x_rows, *d_outs = held
    lists = [block_lists] + [
        part[rows : rows + blocks_here, : block_lists.shape[1]].astype(jnp.int32)
        for part in own_parts[1:]
    ]
    w_out_all = lax.all_gather(w_out, "head", axis=0, tiled=True)
    d_parts = sent(d_outs)
    d_parts, x_outs = after(d_parts, projected([1], [x_rows]))
    x_parts = sent(x_outs)

    here = {0: own_parts, 1: x_parts, 2: y_parts, 3: d_parts}
    there = {relative: [to_other(jnp.stack(here[relative]))] for relative in (0, 2, 3)}
    state = attend("early", place, lists, here, there)
    x_parts, state = after(x_parts, state)
    here[1], there[1] = x_parts, [to_other(part) for part in x_parts]

    def to_chip(array, relative, cross):
        flip = 2 * relative + (1 if cross else 0)
        return lax.ppermute(array, "head", [(i, i ^ flip) for i in range(8)])

    far = attend("late", place, lists, here, there, state)
    far = [far[0]] + [to_section(far[shift], shift) for shift in range(1, 4)]
    near = attend("near", place, lists, here, there)
    near, (place, *far) = after(near, [place, *far])
    y_part = to_chip(jnp.stack([part[0:3] for part in far]), 2, False)
    d_part = to_chip(jnp.stack([part[3:6] for part in far]), 3, False)
    near = [to_section(near[shift - 1], shift) for shift in range(1, 4)]
    near = [*attend("local", place, lists, here, there), *near]
    swapped = to_other(jnp.stack([y_part[:, 2:3], d_part[:, 2:3]]))
    x_kept = to_chip(jnp.stack([part[2:4] for part in near]), 1, False)
    x_given = to_chip(jnp.stack([part[5:6] for part in near]), 1, True)
    own_given = to_other(jnp.stack([part[4:5] for part in near]))
    kept = [near, [x_kept], [y_part], [d_part]]
    given = [own_given, x_given, swapped[0], swapped[1]]
    return finish((0, 1, 2, 3), place, kept, given, w_out_all, hidden_in)


def solution(mesh):
    placed = (
        P(("section", "head"), None),
        P(),
        P(None, None, "head"),
        P("head", None),
        P("section", None),
    )

    def local(hidden_in, norm_gain, w_qkv, w_out, block_lists):
        fits = (
            mesh.shape["section"] == 4
            and mesh.shape["head"] == 8
            and w_qkv.shape[2] == 2 * HD
            and block_lists.shape[0] == 6
            and hidden_in.shape[0] == 3 * TILE
        )
        form = by_head if fits else general
        return form(hidden_in, norm_gain, w_qkv, w_out, block_lists)

    return jax.shard_map(
        local, mesh=mesh, in_specs=placed, out_specs=P(("section", "head"), None), check_vma=False
    )
```

```python
import functools
import math

import jax
import jax.numpy as jnp
from jax import lax
from jax.experimental import pallas as pl
from jax.experimental.pallas import tpu as pltpu
from jax.sharding import PartitionSpec as P

D = 2048
HD = 128
BLK = 512
TILE = 128
STEP = 12


EPS = 1e-05
THETA = 10000.0
VMEM_LIMIT = 56 * 1024 * 1024


def rotate(vectors, cosine, sine):
    half = vectors.shape[-1] // 2
    first = vectors[..., :half]
    second = vectors[..., half:]
    return jnp.concatenate(
        [first * cosine - second * sine, second * cosine + first * sine], axis=-1
    )


def general(hidden_in, norm_gain, w_qkv, w_out, block_lists):
    section_id = lax.axis_index("section")
    width = w_qkv.shape[2]
    heads_here = width // HD
    blocks_here = block_lists.shape[0]
    tok_dev = blocks_here * BLK
    scale = 1.0 / math.sqrt(HD)
    resid = hidden_in.astype(jnp.float32)
    normed = (
        resid * lax.rsqrt(jnp.mean(resid * resid, axis=-1, keepdims=True) + EPS) * norm_gain
    ).astype(jnp.bfloat16)
    flat_weight = w_qkv.reshape(D, 3 * width)
    frequency = THETA ** (-(2.0 * jnp.arange(HD // 2, dtype=jnp.float32)) / HD)
    piece = lax.all_gather(normed, "head", axis=0, tiled=True)
    count = piece.shape[0]
    mixed_rows = jnp.dot(piece, flat_weight, preferred_element_type=jnp.float32).reshape(
        count, 3, heads_here, HD
    )
    positions = (section_id * tok_dev + jnp.arange(count, dtype=jnp.int32)).astype(jnp.float32)
    angle = positions[:, None] * frequency[None, :]
    cosine = jnp.cos(angle)[:, None, :]
    sine = jnp.sin(angle)[:, None, :]
    query = rotate(mixed_rows[:, 0], cosine, sine).astype(jnp.bfloat16).reshape(count, width)
    keys = rotate(mixed_rows[:, 1], cosine, sine).astype(jnp.bfloat16).reshape(count, width)
    values = mixed_rows[:, 2].astype(jnp.bfloat16).reshape(count, width)
    keys_all, values_all = (
        lax.all_gather(keys, "section", axis=0, tiled=True),
        lax.all_gather(values, "section", axis=0, tiled=True),
    )
    count_blocks = block_lists.shape[0]
    query_blocks = query.reshape(count_blocks, BLK, heads_here, HD)
    block_ids = section_id * blocks_here + jnp.arange(count_blocks, dtype=jnp.int32)

    def one_block(carry, item):
        query_block, block_row, block_id = item
        live_slots = jnp.sum((block_row >= 0).astype(jnp.int32))
        query_positions = block_id * BLK + jnp.arange(BLK, dtype=jnp.int32)

        def one_slot(slot, state):
            highest, total, weighted = state
            source = block_row[slot]
            key_block = lax.dynamic_slice_in_dim(keys_all, source * BLK, BLK, 0).reshape(
                BLK, heads_here, HD
            )
            value_block = lax.dynamic_slice_in_dim(values_all, source * BLK, BLK, 0).reshape(
                BLK, heads_here, HD
            )
            scores = (
                jnp.einsum(
                    "qhd,khd->hqk", query_block, key_block, preferred_element_type=jnp.float32
                )
                * scale
            )
            key_positions = source * BLK + jnp.arange(BLK, dtype=jnp.int32)
            scores = jnp.where(
                key_positions[None, None, :] <= query_positions[None, :, None], scores, -jnp.inf
            )
            new_highest = jnp.maximum(highest, jnp.max(scores, axis=-1))
            factor = jnp.exp(highest - new_highest)
            weights = jnp.exp(scores - new_highest[..., None])
            total = total * factor + jnp.sum(weights, axis=-1)
            update = jnp.einsum(
                "hqk,khd->hqd",
                weights.astype(jnp.bfloat16),
                value_block,
                preferred_element_type=jnp.float32,
            )
            weighted = weighted * factor[..., None] + update
            return (new_highest, total, weighted)

        start_state = (
            jnp.full((heads_here, BLK), -jnp.inf, jnp.float32),
            jnp.zeros((heads_here, BLK), jnp.float32),
            jnp.zeros((heads_here, BLK, HD), jnp.float32),
        )
        highest, total, weighted = lax.fori_loop(0, live_slots, one_slot, start_state)
        result = (
            (weighted / total[..., None])
            .transpose(1, 0, 2)
            .reshape(BLK, width)
            .astype(jnp.bfloat16)
        )
        return (carry, result)

    _, results = lax.scan(
        one_block, jnp.zeros((), jnp.int32), (query_blocks, block_lists, block_ids)
    )
    attended = results.reshape(count_blocks * BLK, width)
    regrouped = lax.all_to_all(attended, "head", split_axis=0, concat_axis=1, tiled=True)
    summed = jnp.dot(
        regrouped,
        lax.all_gather(w_out, "head", axis=0, tiled=True),
        preferred_element_type=jnp.float32,
    )
    return (resid + summed).astype(jnp.bfloat16)


def project_kernel(number, noted, unrolled, place, *rest):
    pieces, rest = rest[:number], rest[number:]
    if noted:
        note, rest = rest[0], rest[1:]
    own, other, cosine, sine = rest[:4]
    outs, rest = rest[4:8], rest[8:]
    rows, weights, results, row_sems, weight_sems, out_sems = rest
    count = rows.shape[0]
    row_copies, start = [], 0
    for i, ref in enumerate(pieces):
        size = ref.shape[0]
        row_copies.append(
            pltpu.make_async_copy(ref, rows.at[pl.ds(start, size)], row_sems.at[i])
        )
        start += size
    weight_copies = [
        pltpu.make_async_copy(
            ref.at[part],
            weights.at[w * 3 + part],
            weight_sems.at[w * 3 + part],
        )
        for w, ref in enumerate((own, other))
        for part in range(3)
    ]
    for copy in row_copies + weight_copies[:2]:
        copy.start()
    for copy in row_copies:
        copy.wait()
    query_scale = math.log2(math.e) / math.sqrt(HD)
    step = count // 2

    def out_copy(result, shift):
        return pltpu.make_async_copy(results.at[result], outs[shift], out_sems.at[shift])

    if noted:
        for result in range(4):
            results[result, count:, :] = note[...]

    for w in range(2):
        for part in range(3):
            weight_copies[w * 3 + part].wait()
            if w * 3 + part + 2 < 6:
                weight_copies[w * 3 + part + 2].start()

            def tile(i, carry, w=w, part=part):
                piece = pl.ds(pl.multiple_of(i * step, step), step)
                product = jnp.dot(
                    rows[piece], weights[w * 3 + part], preferred_element_type=jnp.float32
                )
                for h in range(2):
                    vector = product[:, h * HD : (h + 1) * HD]
                    if part < 2:
                        turned = pltpu.roll(vector, HD // 2, 1)
                        vector = vector * cosine[piece] + turned * sine[piece]
                    if part == 0:
                        vector = vector * query_scale
                    column = slice(part * HD, (part + 1) * HD)
                    results[w * 2 + h, piece, column] = vector.astype(jnp.bfloat16)
                return carry

            if unrolled:
                tile(0, 0)
                tile(1, 0)
            else:
                lax.fori_loop(0, 2, tile, 0)
        for h in range(2):
            for shift in range(4):

                @pl.when(place[shift] == w * 2 + h)
                def _(shift=shift, result=w * 2 + h):
                    out_copy(result, shift).start()

    for shift in range(4):
        out_copy(0, shift).wait()


def project(place, pieces, own, other, cosine, sine, note, unrolled):
    count = sum(piece.shape[0] for piece in pieces)
    number = len(pieces)
    width = own.shape[2]
    notes = [] if note is None else [note]
    full = count + sum(each.shape[0] for each in notes)
    any_space = pl.BlockSpec(memory_space=pl.ANY)
    vmem = pl.BlockSpec(memory_space=pltpu.VMEM)
    return pl.pallas_call(
        functools.partial(project_kernel, number, len(notes) > 0, unrolled),
        out_shape=[jax.ShapeDtypeStruct((full, 3 * HD), jnp.bfloat16)] * 4,
        in_specs=[pl.BlockSpec(memory_space=pltpu.SMEM)] + [any_space] * number
        + [vmem] * len(notes)
        + [any_space] * 2
        + [vmem] * 2,
        out_specs=[any_space] * 4,
        scratch_shapes=[
            pltpu.VMEM((count, D), jnp.bfloat16),
            pltpu.VMEM((6, D, width), jnp.bfloat16),
            pltpu.VMEM((4, full, 3 * HD), jnp.bfloat16),
            pltpu.SemaphoreType.DMA((number,)),
            pltpu.SemaphoreType.DMA((6,)),
            pltpu.SemaphoreType.DMA((4,)),
        ],
        compiler_params=pltpu.CompilerParams(vmem_limit_bytes=VMEM_LIMIT),
        cost_estimate=pl.CostEstimate(
            flops=2 * count * D * 6 * width, bytes_accessed=2 * 6 * D * width, transcendentals=0
        ),
        name="project_and_rotate",
    )(place, *pieces, *notes, own, other, cosine, sine)


def attend_kernel(mode, blocks_here, place, *refs):
    refs = list(refs)

    def take(number):
        taken = refs[:number]
        del refs[:number]
        return taken

    near, early, late = mode in ("near", "local"), mode == "early", mode == "late"
    targets = {"near": (1, 2, 3), "local": (0,)}.get(mode, (0, 1, 2, 3))
    lists = take(4)
    have = (0, 2, 3) if early else (0, 1, 2, 3)
    here = {relative: take(4) for relative in have}
    there = {relative: take(4 if relative == 1 else 1) for relative in have}
    state = take(3) if late else []
    outs = take(3 if early else len(targets))
    if early:
        queries, tops, sums = outs
        rows, query_rows, values_t, item_q, item_k, table, sems = refs
    else:
        rows, query_rows, values_t, queries, tops, sums, item_q, item_k, table, sems = refs
    section, chip, core = place[0], place[1], place[2]
    rows_here = here[2][0].shape[0]
    tok = blocks_here * BLK
    slots = lists[0].shape[1]
    wide = 2 * TILE
    pair_blocks = blocks_here // 2
    total_blocks = 4 * pair_blocks
    own_pair = chip // 2
    pair = own_pair if near else 1 - own_pair
    parity = lax.rem(chip, 2)

    def fetches(relatives, with_queries, first):
        copies = []
        for shift in range(4):
            number, query_number = first + shift * 12, first + shift * 12 + 8
            for relative in relatives:
                owner = chip ^ relative
                source = lax.rem(section - shift + 4, 4)
                for far in range(2):
                    side = core if far == 0 else 1 - core
                    if far == 0:
                        ref = here[relative][shift]
                    elif relative == 1:
                        ref = there[relative][shift]
                    else:
                        ref = there[relative][0].at[shift]
                    start = source * tok + owner * (2 * rows_here) + side * rows_here
                    start = pl.multiple_of(start, rows_here)
                    copies.append(
                        pltpu.make_async_copy(
                            ref.at[pl.ds(0, rows_here), pl.ds(HD, 2 * HD)],
                            rows.at[pl.ds(start, rows_here)],
                            sems.at[number],
                        )
                    )
                    number += 1
                    if not with_queries or (relative < 2) != near:
                        continue
                    start = source * (tok // 2) + lax.rem(owner, 2) * (2 * rows_here)
                    start = pl.multiple_of(start + side * rows_here, rows_here)
                    copies.append(
                        pltpu.make_async_copy(
                            ref.at[pl.ds(0, rows_here), pl.ds(0, HD)],
                            query_rows.at[pl.ds(start, rows_here)],
                            sems.at[query_number],
                        )
                    )
                    query_number += 1
        return copies

    def key_block(block):
        return block // pair_blocks * blocks_here + pair * pair_blocks + lax.rem(block, pair_blocks)

    copies = fetches((0, 1) if late else have, not late, 0)
    state_copies = [
        pltpu.make_async_copy(ref, held, sems.at[48 + i])
        for i, (ref, held) in enumerate(zip(state, (queries, tops, sums)))
    ]
    for copy in copies + state_copies:
        copy.start()

    count = jnp.int32(0)
    for target in targets:
        block_list = lists[(4 - target) % 4]
        first_block = lax.rem(section + target, 4) * pair_blocks

        def note(local, count, block_list=block_list, first_block=first_block):
            for slot in range(1, slots):
                source = block_list[pair * pair_blocks + local, slot]
                item_q[count] = first_block + local
                item_k[count] = source
                table[(first_block + local) * slots + slot] = source
                wanted = source >= 0
                if not near:
                    in_section = lax.rem(jnp.maximum(source, 0), blocks_here)
                    whole = (in_section // pair_blocks != own_pair) | (
                        lax.rem(in_section, pair_blocks) == parity * (pair_blocks - 1)
                    )
                    wanted = wanted & (whole if early else jnp.logical_not(whole))
                count = count + wanted.astype(jnp.int32)
            return count

        count = lax.fori_loop(0, pair_blocks, note, count)
    for extra in range(STEP):
        item_q[count + extra] = total_blocks
        item_k[count + extra] = (own_pair if late else pair) * pair_blocks

    values_t[HD:, :] = jnp.ones((values_t.shape[0] - HD, values_t.shape[1]), jnp.bfloat16)
    if not late:
        queries[total_blocks] = jnp.zeros((wide, HD), jnp.bfloat16)
        tops[total_blocks] = jnp.zeros((8, wide), jnp.float32)
        sums[total_blocks] = jnp.zeros(sums.shape[1:], jnp.float32)

    lane = lax.broadcasted_iota(jnp.int32, (BLK, wide), 1)
    key_at = lax.broadcasted_iota(jnp.int32, (BLK, wide), 0)

    def query_place(local):
        middle = local == 1
        return jnp.where(middle, core * TILE, core * wide), jnp.where(middle, TILE, 0)

    def scores_of(source, query):
        at = pl.multiple_of(source * BLK, BLK)
        return lax.dot_general(
            rows[pl.ds(at, BLK), 0:HD],
            query,
            (((1,), (1,)), ((), ())),
            preferred_element_type=jnp.float32,
        )

    def weigh(source, weights):
        at = pl.multiple_of(source * BLK, BLK)
        return jnp.dot(
            values_t[:, pl.ds(at, BLK)],
            weights.astype(jnp.bfloat16),
            preferred_element_type=jnp.float32,
        )

    def masked(local, scores):
        offset, gap = query_place(local)
        query_at = offset + lane + jnp.where(lane >= TILE, gap, 0)
        return jnp.where(key_at <= query_at, scores, -jnp.inf)

    def diagonal(first):
        blocks = [first + local for local in range(pair_blocks)]
        scores = []
        for local, block in enumerate(blocks):
            offset, gap = query_place(local)
            start = pl.multiple_of(block * BLK + offset, TILE)
            later = pl.multiple_of(start + TILE + gap, TILE)
            query = jnp.concatenate(
                [query_rows[pl.ds(start, TILE)], query_rows[pl.ds(later, TILE)]], axis=0
            )
            queries[block] = query
            scores.append(scores_of(key_block(block), query))
        for local, (block, score) in enumerate(zip(blocks, scores)):
            score = masked(local, score)
            top = jnp.max(score, axis=0, keepdims=True)
            tops[block] = jnp.broadcast_to(top, (8, wide))
            sums[block] = weigh(key_block(block), jnp.exp2(score - top))

    def turn(first, number):
        for i in range(number):
            at = pl.multiple_of((first + i) * BLK, BLK)
            values_t[:HD, pl.ds(at, BLK)] = rows[pl.ds(at, BLK), HD : 2 * HD].T

    waits = 4 if late else 2 * len(have)

    def arrive(shift, carry):
        source = lax.rem(section - shift + 4, 4)
        for number in range(waits):
            pltpu.make_async_copy(
                rows.at[pl.ds(0, rows_here)],
                rows.at[pl.ds(0, rows_here)],
                sems.at[shift * 12 + number],
            ).wait()
        if late:
            turn(source * blocks_here + own_pair * pair_blocks, pair_blocks)
            return carry
        for number in range(4):
            pltpu.make_async_copy(
                query_rows.at[pl.ds(0, rows_here)],
                query_rows.at[pl.ds(0, rows_here)],
                sems.at[shift * 12 + 8 + number],
            ).wait()
        turn(source * blocks_here, blocks_here)
        if mode == "early":
            diagonal(source * pair_blocks)
        else:
            wanted = shift == 0 if mode == "local" else shift != 0
            pl.when(wanted)(lambda: diagonal(source * pair_blocks))
        return carry

    lax.fori_loop(0, 4, arrive, 0)
    for copy in state_copies:
        copy.wait()

    def below(step, carry):
        items = [step * STEP + i for i in range(STEP)]
        scores = scores_of(item_k[items[0]], queries[item_q[items[0]]])
        held = None
        for i, item in enumerate(items):
            if i + 1 < STEP:
                ahead = scores_of(item_k[items[i + 1]], queries[item_q[items[i + 1]]])
            weights = jnp.exp2(scores - tops[item_q[item], 0:1]).astype(jnp.bfloat16)
            if held is not None:
                sums[item_q[items[i - 1]]] += weigh(item_k[items[i - 1]], held)
            held, scores = weights, ahead
        sums[item_q[items[-1]]] += weigh(item_k[items[-1]], held)
        return carry

    lax.fori_loop(0, (count + STEP - 1) // STEP, below, 0)
    if early:
        return

    def over_in(i, over):
        block = lax.rem(section * pair_blocks + targets[0] * pair_blocks + i, total_blocks)
        return jnp.maximum(over, jnp.where(sums[block, HD : HD + 1] < 2.0**100, 0.0, 1.0))

    number_blocks = len(targets) * pair_blocks
    over = lax.fori_loop(0, number_blocks, over_in, jnp.zeros((1, wide), jnp.float32))

    @pl.when(jnp.max(over) > 0)
    def _():
        if late:
            copies = fetches((2, 3), False, 0)
            for copy in copies:
                copy.start()
            for copy in copies:
                copy.wait()

            def turn_all(step, carry):
                turn(step * pair_blocks, pair_blocks)
                return carry

            lax.fori_loop(0, 8, turn_all, 0)

        def one_block(i, carry):
            block = lax.rem(section * pair_blocks + targets[0] * pair_blocks + i, total_blocks)
            home = key_block(block)
            query = queries[block]
            scores = masked(lax.rem(block, pair_blocks), scores_of(home, query))
            highest = jnp.max(scores, axis=0, keepdims=True)
            weighted = weigh(home, jnp.exp2(scores - highest))

            def one_slot(slot, state):
                highest, weighted = state
                source = table[block * slots + slot]
                scores = scores_of(jnp.maximum(source, 0), query)
                scores = jnp.where(source >= 0, scores, -jnp.inf)
                new_highest = jnp.maximum(highest, jnp.max(scores, axis=0, keepdims=True))
                weights = jnp.exp2(scores - new_highest)
                weighted = weighted * jnp.exp2(highest - new_highest)
                weighted = weighted + weigh(jnp.maximum(source, 0), weights)
                return (new_highest, weighted)

            _, sums[block] = lax.fori_loop(1, slots, one_slot, (highest, weighted))
            return carry

        lax.fori_loop(0, number_blocks, one_block, 0)

    for number, target in enumerate(targets):

        def leave(local, carry, number=number, target=target):
            block = lax.rem(section + target, 4) * pair_blocks + local
            result = (sums[block, 0:HD] / sums[block, HD : HD + 1]).T.astype(jnp.bfloat16)
            for part in range(2):
                tile = 2 * local + part
                upper = (tile >= 3).astype(jnp.int32)
                i = tile - 3 * upper
                which = upper ^ parity
                given = i == 2 - 2 * core
                if near:
                    where = jnp.where(given, 4 + which, which * 2 + i - core)
                else:
                    where = which * 3 + jnp.where(given, 2, i - core)
                outs[number][where] = result[part * TILE : (part + 1) * TILE]
            return carry

        lax.fori_loop(0, pair_blocks, leave, 0)


def attend(mode, place, lists, here, there, state=()):
    blocks_here, slots = lists[0].shape
    total_blocks = 2 * blocks_here
    tokens = 4 * blocks_here * BLK
    room = total_blocks * slots + STEP
    pairs = total_blocks * slots // 4
    have = (0, 2, 3) if mode == "early" else (0, 1, 2, 3)
    pieces = [piece for relative in have for piece in here[relative]]
    pieces += [piece for relative in have for piece in there[relative]]
    sums = [
        jax.ShapeDtypeStruct((total_blocks + 1, 2 * TILE, HD), jnp.bfloat16),
        jax.ShapeDtypeStruct((total_blocks + 1, 8, 2 * TILE), jnp.float32),
        jax.ShapeDtypeStruct((total_blocks + 1, HD + 16, 2 * TILE), jnp.float32),
    ]
    if mode == "early":
        outs = sums
    else:
        number = {"late": 4, "near": 3, "local": 1}[mode]
        outs = [jax.ShapeDtypeStruct((blocks_here, TILE, HD), jnp.bfloat16)] * number
    held = [] if mode == "early" else [pltpu.VMEM(each.shape, each.dtype) for each in sums]
    return pl.pallas_call(
        functools.partial(attend_kernel, mode, blocks_here),
        out_shape=outs,
        in_specs=[pl.BlockSpec(memory_space=pltpu.SMEM)] * 5
        + [pl.BlockSpec(memory_space=pl.ANY)] * (len(pieces) + len(state)),
        out_specs=[pl.BlockSpec(memory_space=pltpu.VMEM)] * len(outs),
        scratch_shapes=[
            pltpu.VMEM((tokens, 2 * HD), jnp.bfloat16),
            pltpu.VMEM((tokens // 2, HD), jnp.bfloat16),
            pltpu.VMEM((HD + 16, tokens), jnp.bfloat16),
            *held,
            pltpu.SMEM((room,), jnp.int32),
            pltpu.SMEM((room,), jnp.int32),
            pltpu.SMEM((room,), jnp.int32),
            pltpu.SemaphoreType.DMA((51,)),
        ],
        compiler_params=pltpu.CompilerParams(vmem_limit_bytes=VMEM_LIMIT),
        cost_estimate=pl.CostEstimate(
            flops=pairs * 4 * BLK * 2 * TILE * HD,
            bytes_accessed=tokens * 5 * HD,
            transcendentals=pairs * BLK * 2 * TILE,
        ),
        name="attend_" + mode,
    )(place, *lists, *pieces, *state)


def finish_kernel(relatives, kept_parts, place, *rest):
    number = len(relatives)
    kept = []
    for parts in kept_parts:
        kept.append(rest[:parts])
        rest = rest[parts:]
    given, rest = rest[:number], rest[number:]
    w_out, hidden, out, attended, weights, sums, sems, given_sems, weight_sems = rest
    section, chip, core = place[0], place[1], place[2]
    odd = lax.rem(chip, 2)
    depth = 4 * HD
    copies = []
    for r, relative in enumerate(relatives):
        start = pl.multiple_of((chip ^ relative) * depth, depth)
        group = [
            pltpu.make_async_copy(w_out.at[pl.ds(start, depth)], weights.at[r], weight_sems.at[r])
        ]
        for shift in range(4):
            head = lax.rem(section - shift + 4, 4)
            column = pl.ds(pl.multiple_of(head * HD, HD), HD)
            for slot in range(2):
                to = jnp.where(core == 0, slot * (1 + odd), odd if slot == 0 else 2)
                source = kept[r][0].at[shift] if kept_parts[r] == 1 else kept[r][shift]
                group.append(
                    pltpu.make_async_copy(
                        source.at[slot],
                        attended.at[r, pl.ds(pl.multiple_of(to * TILE, TILE), TILE), column],
                        sems.at[(r * 4 + shift) * 2 + slot],
                    )
                )
            to = jnp.where(core == 0, 2 - odd, 1 - odd)
            group.append(
                pltpu.make_async_copy(
                    given[r].at[shift, 0],
                    attended.at[r, pl.ds(pl.multiple_of(to * TILE, TILE), TILE), column],
                    given_sems.at[r * 4 + shift],
                )
            )
        copies.append(group)
    for copy in copies[0] + copies[1]:
        copy.start()
    half = out.shape[0] // 2
    step = 512
    for r in range(number):
        for copy in copies[r]:
            copy.wait()
        if r + 2 < number:
            for copy in copies[r + 2]:
                copy.start()

        def columns(i, carry, r=r):
            column = pl.ds(pl.multiple_of(i * step, step), step)
            for at in range(0, out.shape[0], half):
                piece = (slice(at, at + half), column)
                summed = jnp.dot(
                    attended[r, at : at + half],
                    weights[r, :, column],
                    preferred_element_type=jnp.float32,
                )
                summed = summed + (hidden[piece].astype(jnp.float32) if r == 0 else sums[piece])
                if r + 1 < number:
                    sums[piece] = summed
                else:
                    out[piece] = summed.astype(out.dtype)
            return carry

        for i in range(out.shape[1] // step):
            columns(i, 0)


def finish(relatives, place, kept, given, w_out, hidden):
    count = hidden.shape[0]
    number = len(relatives)
    any_space = pl.BlockSpec(memory_space=pl.ANY)
    vmem = pl.BlockSpec(memory_space=pltpu.VMEM)
    depth = 4 * HD
    return pl.pallas_call(
        functools.partial(finish_kernel, relatives, [len(parts) for parts in kept]),
        out_shape=jax.ShapeDtypeStruct((count, D), jnp.bfloat16),
        in_specs=[pl.BlockSpec(memory_space=pltpu.SMEM)]
        + [any_space] * (sum(map(len, kept)) + number + 1)
        + [vmem],
        out_specs=vmem,
        scratch_shapes=[
            pltpu.VMEM((number, count, depth), jnp.bfloat16),
            pltpu.VMEM((number, depth, D), jnp.bfloat16),
            pltpu.VMEM((count, D), jnp.float32),
            pltpu.SemaphoreType.DMA((number * 8,)),
            pltpu.SemaphoreType.DMA((number * 4,)),
            pltpu.SemaphoreType.DMA((number,)),
        ],
        compiler_params=pltpu.CompilerParams(vmem_limit_bytes=VMEM_LIMIT),
        cost_estimate=pl.CostEstimate(
            flops=2 * count * D * D, bytes_accessed=2 * D * D, transcendentals=0
        ),
        name="project_out",
    )(place, *[part for parts in kept for part in parts], *given, w_out, hidden)


def by_head(hidden_in, norm_gain, w_qkv, w_out, block_lists):
    section = lax.axis_index("section")
    device = lax.axis_index("head")
    chip, core = device // 2, device % 2
    blocks_here = block_lists.shape[0]
    tok = blocks_here * BLK
    rows = hidden_in.shape[0]
    half = rows // 2

    other_core = [(i, i ^ 1) for i in range(8)]
    along_x = [(i, i ^ 2) for i in range(8)]
    along_y = [(i, i ^ 4) for i in range(8)]

    def to_section(array, shift):
        return lax.ppermute(array, "section", [(i, (i + shift) % 4) for i in range(4)])

    place = jnp.stack([section, chip, core]).astype(jnp.int32)
    shifts = jnp.arange(4, dtype=jnp.int32)
    chosen = (section + shifts - 2 * core + 4) % 4

    own = jnp.transpose(w_qkv, (1, 0, 2))
    other = lax.ppermute(own, "head", other_core)
    hidden_in, own = lax.optimization_barrier((hidden_in, own))

    resid = hidden_in.astype(jnp.float32)
    normed = (
        resid * lax.rsqrt(jnp.mean(resid * resid, axis=-1, keepdims=True) + EPS) * norm_gain
    ).astype(jnp.bfloat16)
    y_rows = lax.ppermute(normed, "head", along_y)
    x_rows = lax.ppermute(normed, "head", along_x)

    frequency = THETA ** (-(2.0 * jnp.arange(HD // 2, dtype=jnp.float32)) / HD)

    def projected(relatives, pieces, note=None, unrolled=False):
        starts = section * tok + (chip ^ jnp.array(relatives)) * (2 * rows) + core * rows
        positions = (starts[:, None] + jnp.arange(rows, dtype=jnp.int32)[None, :]).reshape(-1)
        angle = positions.astype(jnp.float32)[:, None] * frequency
        cosine, sine = jnp.cos(angle), jnp.sin(angle)
        cosine = jnp.concatenate([cosine, cosine], axis=-1)
        sine = jnp.concatenate([-sine, sine], axis=-1)
        return project(chosen, pieces, own, other, cosine, sine, note, unrolled)

    def sent(outs):
        return [outs[0]] + [to_section(outs[shift], shift) for shift in range(1, 4)]

    def to_other(array):
        return lax.ppermute(array, "head", other_core)

    def after(first, second):
        joined = lax.optimization_barrier((*first, *second))
        return list(joined[: len(first)]), list(joined[len(first) :])

    note = jnp.pad(
        block_lists.astype(jnp.bfloat16),
        ((0, 16 - blocks_here), (0, 3 * HD - block_lists.shape[1])),
    )
    own_parts = sent(projected([0], [normed], note, True))
    y_outs = projected([2], [y_rows], None, True)
    own_parts, held = after(own_parts, [x_rows[half:], y_rows[:half], *y_outs])
    x_high, y_low, *y_outs = held
    d_low = lax.ppermute(y_low, "head", along_x)
    d_high = lax.ppermute(x_high, "head", along_y)
    y_parts = sent(y_outs)
    d_outs = projected([3], [d_low, d_high])
    y_parts, held = after(y_parts, [w_out, x_rows, *d_outs])
    w_out, x_rows, *d_outs = held
    lists = [block_lists] + [
        part[rows : rows + blocks_here, : block_lists.shape[1]].astype(jnp.int32)
        for part in own_parts[1:]
    ]
    w_out_all = lax.all_gather(w_out, "head", axis=0, tiled=True)
    d_parts = sent(d_outs)
    d_parts, x_outs = after(d_parts, projected([1], [x_rows]))
    x_parts = sent(x_outs)

    here = {0: own_parts, 1: x_parts, 2: y_parts, 3: d_parts}
    there = {relative: [to_other(jnp.stack(here[relative]))] for relative in (0, 2, 3)}
    state = attend("early", place, lists, here, there)
    x_parts, state = after(x_parts, state)
    here[1], there[1] = x_parts, [to_other(part) for part in x_parts]

    def to_chip(array, relative, cross):
        flip = 2 * relative + (1 if cross else 0)
        return lax.ppermute(array, "head", [(i, i ^ flip) for i in range(8)])

    far = attend("late", place, lists, here, there, state)
    far = [far[0]] + [to_section(far[shift], shift) for shift in range(1, 4)]
    near = attend("near", place, lists, here, there)
    near, (place, *far) = after(near, [place, *far])
    y_part = to_chip(jnp.stack([part[0:3] for part in far]), 2, False)
    d_part = to_chip(jnp.stack([part[3:6] for part in far]), 3, False)
    near = [to_section(near[shift - 1], shift) for shift in range(1, 4)]
    near = [*attend("local", place, lists, here, there), *near]
    swapped = to_other(jnp.stack([y_part[:, 2:3], d_part[:, 2:3]]))
    x_kept = to_chip(jnp.stack([part[2:4] for part in near]), 1, False)
    x_given = to_chip(jnp.stack([part[5:6] for part in near]), 1, True)
    own_given = to_other(jnp.stack([part[4:5] for part in near]))
    kept = [near, [x_kept], [y_part], [d_part]]
    given = [own_given, x_given, swapped[0], swapped[1]]
    return finish((0, 1, 2, 3), place, kept, given, w_out_all, hidden_in)


def solution(mesh):
    placed = (
        P(("section", "head"), None),
        P(),
        P(None, None, "head"),
        P("head", None),
        P("section", None),
    )

    def local(hidden_in, norm_gain, w_qkv, w_out, block_lists):
        fits = (
            mesh.shape["section"] == 4
            and mesh.shape["head"] == 8
            and w_qkv.shape[2] == 2 * HD
            and block_lists.shape[0] == 6
            and hidden_in.shape[0] == 3 * TILE
        )
        form = by_head if fits else general
        return form(hidden_in, norm_gain, w_qkv, w_out, block_lists)

    return jax.shard_map(
        local, mesh=mesh, in_specs=placed, out_specs=P(("section", "head"), None), check_vma=False
    )
```

```python
import functools
import math

import jax
import jax.numpy as jnp
from jax import lax
from jax.experimental import pallas as pl
from jax.experimental.pallas import tpu as pltpu
from jax.sharding import PartitionSpec as P

D = 2048
HD = 128
BLK = 512
TILE = 128
STEP = 12


EPS = 1e-05
THETA = 10000.0
VMEM_LIMIT = 56 * 1024 * 1024
ATTEND_LIMIT = 32 * 1024 * 1024


def rotate(vectors, cosine, sine):
    half = vectors.shape[-1] // 2
    first = vectors[..., :half]
    second = vectors[..., half:]
    return jnp.concatenate(
        [first * cosine - second * sine, second * cosine + first * sine], axis=-1
    )


def general(hidden_in, norm_gain, w_qkv, w_out, block_lists):
    section_id = lax.axis_index("section")
    width = w_qkv.shape[2]
    heads_here = width // HD
    blocks_here = block_lists.shape[0]
    tok_dev = blocks_here * BLK
    scale = 1.0 / math.sqrt(HD)
    resid = hidden_in.astype(jnp.float32)
    normed = (
        resid * lax.rsqrt(jnp.mean(resid * resid, axis=-1, keepdims=True) + EPS) * norm_gain
    ).astype(jnp.bfloat16)
    flat_weight = w_qkv.reshape(D, 3 * width)
    frequency = THETA ** (-(2.0 * jnp.arange(HD // 2, dtype=jnp.float32)) / HD)
    piece = lax.all_gather(normed, "head", axis=0, tiled=True)
    count = piece.shape[0]
    mixed_rows = jnp.dot(piece, flat_weight, preferred_element_type=jnp.float32).reshape(
        count, 3, heads_here, HD
    )
    positions = (section_id * tok_dev + jnp.arange(count, dtype=jnp.int32)).astype(jnp.float32)
    angle = positions[:, None] * frequency[None, :]
    cosine = jnp.cos(angle)[:, None, :]
    sine = jnp.sin(angle)[:, None, :]
    query = rotate(mixed_rows[:, 0], cosine, sine).astype(jnp.bfloat16).reshape(count, width)
    keys = rotate(mixed_rows[:, 1], cosine, sine).astype(jnp.bfloat16).reshape(count, width)
    values = mixed_rows[:, 2].astype(jnp.bfloat16).reshape(count, width)
    keys_all, values_all = (
        lax.all_gather(keys, "section", axis=0, tiled=True),
        lax.all_gather(values, "section", axis=0, tiled=True),
    )
    count_blocks = block_lists.shape[0]
    query_blocks = query.reshape(count_blocks, BLK, heads_here, HD)
    block_ids = section_id * blocks_here + jnp.arange(count_blocks, dtype=jnp.int32)

    def one_block(carry, item):
        query_block, block_row, block_id = item
        live_slots = jnp.sum((block_row >= 0).astype(jnp.int32))
        query_positions = block_id * BLK + jnp.arange(BLK, dtype=jnp.int32)

        def one_slot(slot, state):
            highest, total, weighted = state
            source = block_row[slot]
            key_block = lax.dynamic_slice_in_dim(keys_all, source * BLK, BLK, 0).reshape(
                BLK, heads_here, HD
            )
            value_block = lax.dynamic_slice_in_dim(values_all, source * BLK, BLK, 0).reshape(
                BLK, heads_here, HD
            )
            scores = (
                jnp.einsum(
                    "qhd,khd->hqk", query_block, key_block, preferred_element_type=jnp.float32
                )
                * scale
            )
            key_positions = source * BLK + jnp.arange(BLK, dtype=jnp.int32)
            scores = jnp.where(
                key_positions[None, None, :] <= query_positions[None, :, None], scores, -jnp.inf
            )
            new_highest = jnp.maximum(highest, jnp.max(scores, axis=-1))
            factor = jnp.exp(highest - new_highest)
            weights = jnp.exp(scores - new_highest[..., None])
            total = total * factor + jnp.sum(weights, axis=-1)
            update = jnp.einsum(
                "hqk,khd->hqd",
                weights.astype(jnp.bfloat16),
                value_block,
                preferred_element_type=jnp.float32,
            )
            weighted = weighted * factor[..., None] + update
            return (new_highest, total, weighted)

        start_state = (
            jnp.full((heads_here, BLK), -jnp.inf, jnp.float32),
            jnp.zeros((heads_here, BLK), jnp.float32),
            jnp.zeros((heads_here, BLK, HD), jnp.float32),
        )
        highest, total, weighted = lax.fori_loop(0, live_slots, one_slot, start_state)
        result = (
            (weighted / total[..., None])
            .transpose(1, 0, 2)
            .reshape(BLK, width)
            .astype(jnp.bfloat16)
        )
        return (carry, result)

    _, results = lax.scan(
        one_block, jnp.zeros((), jnp.int32), (query_blocks, block_lists, block_ids)
    )
    attended = results.reshape(count_blocks * BLK, width)
    regrouped = lax.all_to_all(attended, "head", split_axis=0, concat_axis=1, tiled=True)
    summed = jnp.dot(
        regrouped,
        lax.all_gather(w_out, "head", axis=0, tiled=True),
        preferred_element_type=jnp.float32,
    )
    return (resid + summed).astype(jnp.bfloat16)


def project_kernel(number, noted, unrolled, halved, place, *rest):
    pieces, rest = rest[:number], rest[number:]
    if halved:
        beside, rest = rest[0], rest[1:]
    if noted:
        note, rest = rest[0], rest[1:]
    own, other, cosine, sine = rest[:4]
    outs, rest = rest[4:8], rest[8:]
    if halved:
        half = beside.shape[0] // 2
        (low, high), rest = rest[:2], rest[2:]
    rows, weights, results, row_sems, weight_sems, out_sems = rest[:6]
    count = rows.shape[0]
    half_copies, fetch_half = [], []
    if halved:
        staged = rest[6]
        fetch_half = [
            pltpu.make_async_copy(beside.at[pl.ds(half, half)], staged, row_sems.at[number])
        ]
        half_copies = [
            pltpu.make_async_copy(rows.at[pl.ds(0, half)], low, out_sems.at[4]),
            pltpu.make_async_copy(staged, high, out_sems.at[5]),
        ]
    row_copies, start = [], 0
    for i, ref in enumerate(pieces):
        size = ref.shape[0]
        row_copies.append(
            pltpu.make_async_copy(ref, rows.at[pl.ds(start, size)], row_sems.at[i])
        )
        start += size
    weight_copies = [
        pltpu.make_async_copy(
            ref.at[part],
            weights.at[w * 3 + part],
            weight_sems.at[w * 3 + part],
        )
        for w, ref in enumerate((own, other))
        for part in range(3)
    ]
    for copy in row_copies + weight_copies[:2] + fetch_half:
        copy.start()
    for copy in row_copies + fetch_half:
        copy.wait()
    for copy in half_copies:
        copy.start()
    query_scale = math.log2(math.e) / math.sqrt(HD)
    step = count // 2

    def out_copy(result, shift):
        return pltpu.make_async_copy(results.at[result], outs[shift], out_sems.at[shift])

    if noted:
        for result in range(4):
            results[result, count:, :] = note[...]

    for w in range(2):
        for part in range(3):
            weight_copies[w * 3 + part].wait()
            if w * 3 + part + 2 < 6:
                weight_copies[w * 3 + part + 2].start()

            def tile(i, carry, w=w, part=part):
                piece = pl.ds(pl.multiple_of(i * step, step), step)
                product = jnp.dot(
                    rows[piece], weights[w * 3 + part], preferred_element_type=jnp.float32
                )
                for h in range(2):
                    vector = product[:, h * HD : (h + 1) * HD]
                    if part < 2:
                        turned = pltpu.roll(vector, HD // 2, 1)
                        vector = vector * cosine[piece] + turned * sine[piece]
                    if part == 0:
                        vector = vector * query_scale
                    column = slice(part * HD, (part + 1) * HD)
                    results[w * 2 + h, piece, column] = vector.astype(jnp.bfloat16)
                return carry

            if unrolled:
                tile(0, 0)
                tile(1, 0)
            else:
                lax.fori_loop(0, 2, tile, 0)
        for h in range(2):
            for shift in range(4):

                @pl.when(place[shift] == w * 2 + h)
                def _(shift=shift, result=w * 2 + h):
                    out_copy(result, shift).start()

    for shift in range(4):
        out_copy(0, shift).wait()
    for copy in half_copies:
        copy.wait()


def project(place, pieces, own, other, cosine, sine, note, unrolled, beside):
    count = sum(piece.shape[0] for piece in pieces)
    number = len(pieces)
    width = own.shape[2]
    notes = [] if note is None else [note]
    extra = [] if beside is None else [beside]
    halves = [jax.ShapeDtypeStruct((count // 2, D), jnp.bfloat16)] * (2 * len(extra))
    full = count + sum(each.shape[0] for each in notes)
    any_space = pl.BlockSpec(memory_space=pl.ANY)
    vmem = pl.BlockSpec(memory_space=pltpu.VMEM)
    return pl.pallas_call(
        functools.partial(project_kernel, number, len(notes) > 0, unrolled, len(extra) > 0),
        out_shape=[jax.ShapeDtypeStruct((full, 3 * HD), jnp.bfloat16)] * 4 + halves,
        in_specs=[pl.BlockSpec(memory_space=pltpu.SMEM)]
        + [any_space] * (number + len(extra))
        + [vmem] * len(notes)
        + [any_space] * 2
        + [vmem] * 2,
        out_specs=[any_space] * (4 + len(halves)),
        scratch_shapes=[
            pltpu.VMEM((count, D), jnp.bfloat16),
            pltpu.VMEM((6, D, width), jnp.bfloat16),
            pltpu.VMEM((4, full, 3 * HD), jnp.bfloat16),
            pltpu.SemaphoreType.DMA((number + 1,)),
            pltpu.SemaphoreType.DMA((6,)),
            pltpu.SemaphoreType.DMA((6,)),
        ]
        + [pltpu.VMEM((count // 2, D), jnp.bfloat16)] * len(extra),
        compiler_params=pltpu.CompilerParams(vmem_limit_bytes=VMEM_LIMIT),
        cost_estimate=pl.CostEstimate(
            flops=2 * count * D * 6 * width, bytes_accessed=2 * 6 * D * width, transcendentals=0
        ),
        name="project_and_rotate",
    )(place, *pieces, *extra, *notes, own, other, cosine, sine)


def attend_kernel(mode, blocks_here, place, *refs):
    refs = list(refs)

    def take(number):
        taken = refs[:number]
        del refs[:number]
        return taken

    near, early, late = mode in ("near", "local"), mode == "early", mode == "late"
    targets = {"near": (1, 2, 3), "local": (0,)}.get(mode, (0, 1, 2, 3))
    lists = take(4)
    have = (0, 2, 3) if early else (0, 1, 2, 3)
    here = {relative: take(4) for relative in have}
    there = {relative: take(4 if relative == 1 else 1) for relative in have}
    state = take(3) if late else []
    outs = take(3 if early else len(targets))
    if early:
        queries, tops, sums = outs
        rows, query_rows, values_t, item_q, item_k, table, sems = refs
    else:
        rows, query_rows, values_t, queries, tops, sums, item_q, item_k, table, sems = refs
    section, chip, core = place[0], place[1], place[2]
    rows_here = here[2][0].shape[0]
    tok = blocks_here * BLK
    slots = lists[0].shape[1]
    wide = 2 * TILE
    pair_blocks = blocks_here // 2
    total_blocks = 4 * pair_blocks
    own_pair = chip // 2
    pair = own_pair if near else 1 - own_pair
    parity = lax.rem(chip, 2)

    def fetches(relatives, with_queries, first):
        copies = []
        for shift in range(4):
            number, query_number = first + shift * 12, first + shift * 12 + 8
            for relative in relatives:
                owner = chip ^ relative
                source = lax.rem(section - shift + 4, 4)
                for far in range(2):
                    side = core if far == 0 else 1 - core
                    if far == 0:
                        ref = here[relative][shift]
                    elif relative == 1:
                        ref = there[relative][shift]
                    else:
                        ref = there[relative][0].at[shift]
                    start = source * tok + owner * (2 * rows_here) + side * rows_here
                    start = pl.multiple_of(start, rows_here)
                    copies.append(
                        pltpu.make_async_copy(
                            ref.at[pl.ds(0, rows_here), pl.ds(HD, 2 * HD)],
                            rows.at[pl.ds(start, rows_here)],
                            sems.at[number],
                        )
                    )
                    number += 1
                    if not with_queries or (relative < 2) != near:
                        continue
                    start = source * (tok // 2) + lax.rem(owner, 2) * (2 * rows_here)
                    start = pl.multiple_of(start + side * rows_here, rows_here)
                    copies.append(
                        pltpu.make_async_copy(
                            ref.at[pl.ds(0, rows_here), pl.ds(0, HD)],
                            query_rows.at[pl.ds(start, rows_here)],
                            sems.at[query_number],
                        )
                    )
                    query_number += 1
        return copies

    def key_block(block):
        return block // pair_blocks * blocks_here + pair * pair_blocks + lax.rem(block, pair_blocks)

    copies = fetches((0, 1) if late else have, not late, 0)
    state_copies = [
        pltpu.make_async_copy(ref, held, sems.at[48 + i])
        for i, (ref, held) in enumerate(zip(state, (queries, tops, sums)))
    ]
    for copy in copies + state_copies:
        copy.start()

    count = jnp.int32(0)
    for target in targets:
        block_list = lists[(4 - target) % 4]
        first_block = lax.rem(section + target, 4) * pair_blocks

        def note(local, count, block_list=block_list, first_block=first_block):
            for slot in range(1, slots):
                source = block_list[pair * pair_blocks + local, slot]
                item_q[count] = first_block + local
                item_k[count] = source
                table[(first_block + local) * slots + slot] = source
                wanted = source >= 0
                if not near:
                    in_section = lax.rem(jnp.maximum(source, 0), blocks_here)
                    whole = (in_section // pair_blocks != own_pair) | (
                        lax.rem(in_section, pair_blocks) == parity * (pair_blocks - 1)
                    )
                    wanted = wanted & (whole if early else jnp.logical_not(whole))
                count = count + wanted.astype(jnp.int32)
            return count

        count = lax.fori_loop(0, pair_blocks, note, count)
    for extra in range(STEP):
        item_q[count + extra] = total_blocks
        item_k[count + extra] = (own_pair if late else pair) * pair_blocks

    values_t[HD:, :] = jnp.ones((values_t.shape[0] - HD, values_t.shape[1]), jnp.bfloat16)
    if not late:
        queries[total_blocks] = jnp.zeros((wide, HD), jnp.bfloat16)
        tops[total_blocks] = jnp.zeros((8, wide), jnp.float32)
        sums[total_blocks] = jnp.zeros(sums.shape[1:], jnp.float32)

    lane = lax.broadcasted_iota(jnp.int32, (BLK, wide), 1)
    key_at = lax.broadcasted_iota(jnp.int32, (BLK, wide), 0)

    def query_place(local):
        middle = local == 1
        return jnp.where(middle, core * TILE, core * wide), jnp.where(middle, TILE, 0)

    def scores_of(source, query):
        at = pl.multiple_of(source * BLK, BLK)
        return lax.dot_general(
            rows[pl.ds(at, BLK), 0:HD],
            query,
            (((1,), (1,)), ((), ())),
            preferred_element_type=jnp.float32,
        )

    def weigh(source, weights):
        at = pl.multiple_of(source * BLK, BLK)
        return jnp.dot(
            values_t[:, pl.ds(at, BLK)],
            weights.astype(jnp.bfloat16),
            preferred_element_type=jnp.float32,
        )

    def masked(local, scores):
        offset, gap = query_place(local)
        query_at = offset + lane + jnp.where(lane >= TILE, gap, 0)
        return jnp.where(key_at <= query_at, scores, -jnp.inf)

    def diagonal(first):
        blocks = [first + local for local in range(pair_blocks)]
        scores = []
        for local, block in enumerate(blocks):
            offset, gap = query_place(local)
            start = pl.multiple_of(block * BLK + offset, TILE)
            later = pl.multiple_of(start + TILE + gap, TILE)
            query = jnp.concatenate(
                [query_rows[pl.ds(start, TILE)], query_rows[pl.ds(later, TILE)]], axis=0
            )
            queries[block] = query
            scores.append(scores_of(key_block(block), query))
        for local, (block, score) in enumerate(zip(blocks, scores)):
            score = masked(local, score)
            top = jnp.max(score, axis=0, keepdims=True)
            tops[block] = jnp.broadcast_to(top, (8, wide))
            sums[block] = weigh(key_block(block), jnp.exp2(score - top))

    def turn(first, number):
        for i in range(number):
            at = pl.multiple_of((first + i) * BLK, BLK)
            values_t[:HD, pl.ds(at, BLK)] = rows[pl.ds(at, BLK), HD : 2 * HD].T

    waits = 4 if late else 2 * len(have)

    def arrive(shift, carry):
        source = lax.rem(section - shift + 4, 4)
        for number in range(waits):
            pltpu.make_async_copy(
                rows.at[pl.ds(0, rows_here)],
                rows.at[pl.ds(0, rows_here)],
                sems.at[shift * 12 + number],
            ).wait()
        if late:
            turn(source * blocks_here + own_pair * pair_blocks, pair_blocks)
            return carry
        for number in range(4):
            pltpu.make_async_copy(
                query_rows.at[pl.ds(0, rows_here)],
                query_rows.at[pl.ds(0, rows_here)],
                sems.at[shift * 12 + 8 + number],
            ).wait()
        turn(source * blocks_here, blocks_here)
        if mode == "early":
            diagonal(source * pair_blocks)
        else:
            wanted = shift == 0 if mode == "local" else shift != 0
            pl.when(wanted)(lambda: diagonal(source * pair_blocks))
        return carry

    lax.fori_loop(0, 4, arrive, 0)
    for copy in state_copies:
        copy.wait()

    def below(step, carry):
        items = [step * STEP + i for i in range(STEP)]
        scores = scores_of(item_k[items[0]], queries[item_q[items[0]]])
        held = None
        for i, item in enumerate(items):
            if i + 1 < STEP:
                ahead = scores_of(item_k[items[i + 1]], queries[item_q[items[i + 1]]])
            weights = jnp.exp2(scores - tops[item_q[item], 0:1]).astype(jnp.bfloat16)
            if held is not None:
                sums[item_q[items[i - 1]]] += weigh(item_k[items[i - 1]], held)
            held, scores = weights, ahead
        sums[item_q[items[-1]]] += weigh(item_k[items[-1]], held)
        return carry

    lax.fori_loop(0, (count + STEP - 1) // STEP, below, 0)
    if early:
        return

    def over_in(i, over):
        block = lax.rem(section * pair_blocks + targets[0] * pair_blocks + i, total_blocks)
        return jnp.maximum(over, jnp.where(sums[block, HD : HD + 1] < 2.0**100, 0.0, 1.0))

    number_blocks = len(targets) * pair_blocks
    over = lax.fori_loop(0, number_blocks, over_in, jnp.zeros((1, wide), jnp.float32))

    @pl.when(jnp.max(over) > 0)
    def _():
        if late:
            copies = fetches((2, 3), False, 0)
            for copy in copies:
                copy.start()
            for copy in copies:
                copy.wait()

            def turn_all(step, carry):
                turn(step * pair_blocks, pair_blocks)
                return carry

            lax.fori_loop(0, 8, turn_all, 0)

        def one_block(i, carry):
            block = lax.rem(section * pair_blocks + targets[0] * pair_blocks + i, total_blocks)
            home = key_block(block)
            query = queries[block]
            scores = masked(lax.rem(block, pair_blocks), scores_of(home, query))
            highest = jnp.max(scores, axis=0, keepdims=True)
            weighted = weigh(home, jnp.exp2(scores - highest))

            def one_slot(slot, state):
                highest, weighted = state
                source = table[block * slots + slot]
                scores = scores_of(jnp.maximum(source, 0), query)
                scores = jnp.where(source >= 0, scores, -jnp.inf)
                new_highest = jnp.maximum(highest, jnp.max(scores, axis=0, keepdims=True))
                weights = jnp.exp2(scores - new_highest)
                weighted = weighted * jnp.exp2(highest - new_highest)
                weighted = weighted + weigh(jnp.maximum(source, 0), weights)
                return (new_highest, weighted)

            _, sums[block] = lax.fori_loop(1, slots, one_slot, (highest, weighted))
            return carry

        lax.fori_loop(0, number_blocks, one_block, 0)

    for number, target in enumerate(targets):

        def leave(local, carry, number=number, target=target):
            block = lax.rem(section + target, 4) * pair_blocks + local
            result = (sums[block, 0:HD] / sums[block, HD : HD + 1]).T.astype(jnp.bfloat16)
            for part in range(2):
                tile = 2 * local + part
                upper = (tile >= 3).astype(jnp.int32)
                i = tile - 3 * upper
                which = upper ^ parity
                given = i == 2 - 2 * core
                if near:
                    where = jnp.where(given, 4 + which, which * 2 + i - core)
                else:
                    where = which * 3 + jnp.where(given, 2, i - core)
                outs[number][where] = result[part * TILE : (part + 1) * TILE]
            return carry

        lax.fori_loop(0, pair_blocks, leave, 0)


def attend(mode, place, lists, here, there, state=()):
    blocks_here, slots = lists[0].shape
    total_blocks = 2 * blocks_here
    tokens = 4 * blocks_here * BLK
    room = total_blocks * slots + STEP
    pairs = total_blocks * slots // 4
    have = (0, 2, 3) if mode == "early" else (0, 1, 2, 3)
    pieces = [piece for relative in have for piece in here[relative]]
    pieces += [piece for relative in have for piece in there[relative]]
    sums = [
        jax.ShapeDtypeStruct((total_blocks + 1, 2 * TILE, HD), jnp.bfloat16),
        jax.ShapeDtypeStruct((total_blocks + 1, 8, 2 * TILE), jnp.float32),
        jax.ShapeDtypeStruct((total_blocks + 1, HD + 16, 2 * TILE), jnp.float32),
    ]
    if mode == "early":
        outs = sums
    else:
        number = {"late": 4, "near": 3, "local": 1}[mode]
        outs = [jax.ShapeDtypeStruct((blocks_here, TILE, HD), jnp.bfloat16)] * number
    held = [] if mode == "early" else [pltpu.VMEM(each.shape, each.dtype) for each in sums]
    return pl.pallas_call(
        functools.partial(attend_kernel, mode, blocks_here),
        out_shape=outs,
        in_specs=[pl.BlockSpec(memory_space=pltpu.SMEM)] * 5
        + [pl.BlockSpec(memory_space=pl.ANY)] * (len(pieces) + len(state)),
        out_specs=[pl.BlockSpec(memory_space=pltpu.VMEM)] * len(outs),
        scratch_shapes=[
            pltpu.VMEM((tokens, 2 * HD), jnp.bfloat16),
            pltpu.VMEM((tokens // 2, HD), jnp.bfloat16),
            pltpu.VMEM((HD + 16, tokens), jnp.bfloat16),
            *held,
            pltpu.SMEM((room,), jnp.int32),
            pltpu.SMEM((room,), jnp.int32),
            pltpu.SMEM((room,), jnp.int32),
            pltpu.SemaphoreType.DMA((51,)),
        ],
        compiler_params=pltpu.CompilerParams(vmem_limit_bytes=ATTEND_LIMIT),
        cost_estimate=pl.CostEstimate(
            flops=pairs * 4 * BLK * 2 * TILE * HD,
            bytes_accessed=tokens * 5 * HD,
            transcendentals=pairs * BLK * 2 * TILE,
        ),
        name="attend_" + mode,
    )(place, *lists, *pieces, *state)


def finish_kernel(relatives, kept_parts, place, *rest):
    number = len(relatives)
    kept = []
    for parts in kept_parts:
        kept.append(rest[:parts])
        rest = rest[parts:]
    given, rest = rest[:number], rest[number:]
    w_out, hidden, out, attended, weights, sums, sems, given_sems, weight_sems = rest
    section, chip, core = place[0], place[1], place[2]
    odd = lax.rem(chip, 2)
    depth = 4 * HD
    copies = []
    for r, relative in enumerate(relatives):
        start = pl.multiple_of((chip ^ relative) * depth, depth)
        group = [
            pltpu.make_async_copy(w_out.at[pl.ds(start, depth)], weights.at[r], weight_sems.at[r])
        ]
        for shift in range(4):
            head = lax.rem(section - shift + 4, 4)
            column = pl.ds(pl.multiple_of(head * HD, HD), HD)
            for slot in range(2):
                to = jnp.where(core == 0, slot * (1 + odd), odd if slot == 0 else 2)
                source = kept[r][0].at[shift] if kept_parts[r] == 1 else kept[r][shift]
                group.append(
                    pltpu.make_async_copy(
                        source.at[slot],
                        attended.at[r, pl.ds(pl.multiple_of(to * TILE, TILE), TILE), column],
                        sems.at[(r * 4 + shift) * 2 + slot],
                    )
                )
            to = jnp.where(core == 0, 2 - odd, 1 - odd)
            group.append(
                pltpu.make_async_copy(
                    given[r].at[shift, 0],
                    attended.at[r, pl.ds(pl.multiple_of(to * TILE, TILE), TILE), column],
                    given_sems.at[r * 4 + shift],
                )
            )
        copies.append(group)
    for copy in copies[0] + copies[1]:
        copy.start()
    half = out.shape[0] // 2
    step = 512
    for r in range(number):
        for copy in copies[r]:
            copy.wait()
        if r + 2 < number:
            for copy in copies[r + 2]:
                copy.start()

        def columns(i, carry, r=r):
            column = pl.ds(pl.multiple_of(i * step, step), step)
            for at in range(0, out.shape[0], half):
                piece = (slice(at, at + half), column)
                summed = jnp.dot(
                    attended[r, at : at + half],
                    weights[r, :, column],
                    preferred_element_type=jnp.float32,
                )
                summed = summed + (hidden[piece].astype(jnp.float32) if r == 0 else sums[piece])
                if r + 1 < number:
                    sums[piece] = summed
                else:
                    out[piece] = summed.astype(out.dtype)
            return carry

        for i in range(out.shape[1] // step):
            columns(i, 0)


def finish(relatives, place, kept, given, w_out, hidden):
    count = hidden.shape[0]
    number = len(relatives)
    any_space = pl.BlockSpec(memory_space=pl.ANY)
    vmem = pl.BlockSpec(memory_space=pltpu.VMEM)
    depth = 4 * HD
    return pl.pallas_call(
        functools.partial(finish_kernel, relatives, [len(parts) for parts in kept]),
        out_shape=jax.ShapeDtypeStruct((count, D), jnp.bfloat16),
        in_specs=[pl.BlockSpec(memory_space=pltpu.SMEM)]
        + [any_space] * (sum(map(len, kept)) + number + 1)
        + [vmem],
        out_specs=vmem,
        scratch_shapes=[
            pltpu.VMEM((number, count, depth), jnp.bfloat16),
            pltpu.VMEM((number, depth, D), jnp.bfloat16),
            pltpu.VMEM((count, D), jnp.float32),
            pltpu.SemaphoreType.DMA((number * 8,)),
            pltpu.SemaphoreType.DMA((number * 4,)),
            pltpu.SemaphoreType.DMA((number,)),
        ],
        compiler_params=pltpu.CompilerParams(vmem_limit_bytes=VMEM_LIMIT),
        cost_estimate=pl.CostEstimate(
            flops=2 * count * D * D, bytes_accessed=2 * D * D, transcendentals=0
        ),
        name="project_out",
    )(place, *[part for parts in kept for part in parts], *given, w_out, hidden)


def by_head(hidden_in, norm_gain, w_qkv, w_out, block_lists):
    section = lax.axis_index("section")
    device = lax.axis_index("head")
    chip, core = device // 2, device % 2
    blocks_here = block_lists.shape[0]
    tok = blocks_here * BLK
    rows = hidden_in.shape[0]
    half = rows // 2

    other_core = [(i, i ^ 1) for i in range(8)]
    along_x = [(i, i ^ 2) for i in range(8)]
    along_y = [(i, i ^ 4) for i in range(8)]

    def to_section(array, shift):
        return lax.ppermute(array, "section", [(i, (i + shift) % 4) for i in range(4)])

    place = jnp.stack([section, chip, core]).astype(jnp.int32)
    shifts = jnp.arange(4, dtype=jnp.int32)
    chosen = (section + shifts - 2 * core + 4) % 4

    own = jnp.transpose(w_qkv, (1, 0, 2))
    other = lax.ppermute(own, "head", other_core)
    hidden_in, own = lax.optimization_barrier((hidden_in, own))

    resid = hidden_in.astype(jnp.float32)
    normed = (
        resid * lax.rsqrt(jnp.mean(resid * resid, axis=-1, keepdims=True) + EPS) * norm_gain
    ).astype(jnp.bfloat16)
    y_rows = lax.ppermute(normed, "head", along_y)
    x_rows = lax.ppermute(normed, "head", along_x)

    frequency = THETA ** (-(2.0 * jnp.arange(HD // 2, dtype=jnp.float32)) / HD)

    def projected(relatives, pieces, note=None, unrolled=False, beside=None, base=None):
        starts = (section if base is None else base) * tok + (chip ^ jnp.array(relatives)) * (2 * rows) + core * rows
        positions = (starts[:, None] + jnp.arange(rows, dtype=jnp.int32)[None, :]).reshape(-1)
        angle = positions.astype(jnp.float32)[:, None] * frequency
        cosine, sine = jnp.cos(angle), jnp.sin(angle)
        cosine = jnp.concatenate([cosine, cosine], axis=-1)
        sine = jnp.concatenate([-sine, sine], axis=-1)
        return project(chosen, pieces, own, other, cosine, sine, note, unrolled, beside)

    def sent(outs):
        return [outs[0]] + [to_section(outs[shift], shift) for shift in range(1, 4)]

    def to_other(array):
        return lax.ppermute(array, "head", other_core)

    def after(first, second):
        joined = lax.optimization_barrier((*first, *second))
        return list(joined[: len(first)]), list(joined[len(first) :])

    note = jnp.pad(
        block_lists.astype(jnp.bfloat16),
        ((0, 16 - blocks_here), (0, 3 * HD - block_lists.shape[1])),
    )
    own_outs = projected([0], [normed], note, True)
    own_outs, (base,) = after(own_outs, [section])
    own_parts = sent(own_outs)
    *y_outs, y_low, x_high = projected([2], [y_rows], None, True, x_rows, base)
    own_parts, held = after(own_parts, [x_high, y_low, *y_outs])
    x_high, y_low, *y_outs = held
    d_low = lax.ppermute(y_low, "head", along_x)
    d_high = lax.ppermute(x_high, "head", along_y)
    y_parts = sent(y_outs)
    d_outs = projected([3], [d_low, d_high], base=base)
    y_parts, held = after(y_parts, [w_out, x_rows, *d_outs])
    w_out, x_rows, *d_outs = held
    lists = [block_lists] + [
        part[rows : rows + blocks_here, : block_lists.shape[1]].astype(jnp.int32)
        for part in own_parts[1:]
    ]
    w_out_all = lax.all_gather(w_out, "head", axis=0, tiled=True)
    d_parts = sent(d_outs)
    d_parts, x_outs = after(d_parts, projected([1], [x_rows], base=base))
    x_parts = sent(x_outs)

    here = {0: own_parts, 1: x_parts, 2: y_parts, 3: d_parts}
    there = {relative: [to_other(jnp.stack(here[relative]))] for relative in (0, 2, 3)}
    state = attend("early", place, lists, here, there)
    x_parts, state = after(x_parts, state)
    here[1], there[1] = x_parts, [to_other(part) for part in x_parts]

    def to_chip(array, relative, cross):
        flip = 2 * relative + (1 if cross else 0)
        return lax.ppermute(array, "head", [(i, i ^ flip) for i in range(8)])

    far = attend("late", place, lists, here, there, state)
    far = [far[0]] + [to_section(far[shift], shift) for shift in range(1, 4)]
    near = attend("near", place, lists, here, there)
    near, (place, *far) = after(near, [place, *far])
    y_part = to_chip(jnp.stack([part[0:3] for part in far]), 2, False)
    d_part = to_chip(jnp.stack([part[3:6] for part in far]), 3, False)
    near = [to_section(near[shift - 1], shift) for shift in range(1, 4)]
    near = [*attend("local", place, lists, here, there), *near]
    swapped = to_other(jnp.stack([y_part[:, 2:3], d_part[:, 2:3]]))
    x_kept = to_chip(jnp.stack([part[2:4] for part in near]), 1, False)
    x_given = to_chip(jnp.stack([part[5:6] for part in near]), 1, True)
    own_given = to_other(jnp.stack([part[4:5] for part in near]))
    kept = [near, [x_kept], [y_part], [d_part]]
    given = [own_given, x_given, swapped[0], swapped[1]]
    return finish((0, 1, 2, 3), place, kept, given, w_out_all, hidden_in)


def solution(mesh):
    placed = (
        P(("section", "head"), None),
        P(),
        P(None, None, "head"),
        P("head", None),
        P("section", None),
    )

    def local(hidden_in, norm_gain, w_qkv, w_out, block_lists):
        fits = (
            mesh.shape["section"] == 4
            and mesh.shape["head"] == 8
            and w_qkv.shape[2] == 2 * HD
            and block_lists.shape[0] == 6
            and hidden_in.shape[0] == 3 * TILE
        )
        form = by_head if fits else general
        return form(hidden_in, norm_gain, w_qkv, w_out, block_lists)

    return jax.shard_map(
        local, mesh=mesh, in_specs=placed, out_specs=P(("section", "head"), None), check_vma=False
    )
```

```python
import functools
import math

import jax
import jax.numpy as jnp
from jax import lax
from jax.experimental import pallas as pl
from jax.experimental.pallas import tpu as pltpu
from jax.sharding import PartitionSpec as P

D = 2048
HD = 128
BLK = 512
TILE = 128
STEPS = {"early": 4, "late": 12, "near": 12, "local": 3}


EPS = 1e-05
THETA = 10000.0
VMEM_LIMIT = 56 * 1024 * 1024
ATTEND_LIMIT = 32 * 1024 * 1024


def rotate(vectors, cosine, sine):
    half = vectors.shape[-1] // 2
    first = vectors[..., :half]
    second = vectors[..., half:]
    return jnp.concatenate(
        [first * cosine - second * sine, second * cosine + first * sine], axis=-1
    )


def general(hidden_in, norm_gain, w_qkv, w_out, block_lists):
    section_id = lax.axis_index("section")
    width = w_qkv.shape[2]
    heads_here = width // HD
    blocks_here = block_lists.shape[0]
    tok_dev = blocks_here * BLK
    scale = 1.0 / math.sqrt(HD)
    resid = hidden_in.astype(jnp.float32)
    normed = (
        resid * lax.rsqrt(jnp.mean(resid * resid, axis=-1, keepdims=True) + EPS) * norm_gain
    ).astype(jnp.bfloat16)
    flat_weight = w_qkv.reshape(D, 3 * width)
    frequency = THETA ** (-(2.0 * jnp.arange(HD // 2, dtype=jnp.float32)) / HD)
    piece = lax.all_gather(normed, "head", axis=0, tiled=True)
    count = piece.shape[0]
    mixed_rows = jnp.dot(piece, flat_weight, preferred_element_type=jnp.float32).reshape(
        count, 3, heads_here, HD
    )
    positions = (section_id * tok_dev + jnp.arange(count, dtype=jnp.int32)).astype(jnp.float32)
    angle = positions[:, None] * frequency[None, :]
    cosine = jnp.cos(angle)[:, None, :]
    sine = jnp.sin(angle)[:, None, :]
    query = rotate(mixed_rows[:, 0], cosine, sine).astype(jnp.bfloat16).reshape(count, width)
    keys = rotate(mixed_rows[:, 1], cosine, sine).astype(jnp.bfloat16).reshape(count, width)
    values = mixed_rows[:, 2].astype(jnp.bfloat16).reshape(count, width)
    keys_all, values_all = (
        lax.all_gather(keys, "section", axis=0, tiled=True),
        lax.all_gather(values, "section", axis=0, tiled=True),
    )
    count_blocks = block_lists.shape[0]
    query_blocks = query.reshape(count_blocks, BLK, heads_here, HD)
    block_ids = section_id * blocks_here + jnp.arange(count_blocks, dtype=jnp.int32)

    def one_block(carry, item):
        query_block, block_row, block_id = item
        live_slots = jnp.sum((block_row >= 0).astype(jnp.int32))
        query_positions = block_id * BLK + jnp.arange(BLK, dtype=jnp.int32)

        def one_slot(slot, state):
            highest, total, weighted = state
            source = block_row[slot]
            key_block = lax.dynamic_slice_in_dim(keys_all, source * BLK, BLK, 0).reshape(
                BLK, heads_here, HD
            )
            value_block = lax.dynamic_slice_in_dim(values_all, source * BLK, BLK, 0).reshape(
                BLK, heads_here, HD
            )
            scores = (
                jnp.einsum(
                    "qhd,khd->hqk", query_block, key_block, preferred_element_type=jnp.float32
                )
                * scale
            )
            key_positions = source * BLK + jnp.arange(BLK, dtype=jnp.int32)
            scores = jnp.where(
                key_positions[None, None, :] <= query_positions[None, :, None], scores, -jnp.inf
            )
            new_highest = jnp.maximum(highest, jnp.max(scores, axis=-1))
            factor = jnp.exp(highest - new_highest)
            weights = jnp.exp(scores - new_highest[..., None])
            total = total * factor + jnp.sum(weights, axis=-1)
            update = jnp.einsum(
                "hqk,khd->hqd",
                weights.astype(jnp.bfloat16),
                value_block,
                preferred_element_type=jnp.float32,
            )
            weighted = weighted * factor[..., None] + update
            return (new_highest, total, weighted)

        start_state = (
            jnp.full((heads_here, BLK), -jnp.inf, jnp.float32),
            jnp.zeros((heads_here, BLK), jnp.float32),
            jnp.zeros((heads_here, BLK, HD), jnp.float32),
        )
        highest, total, weighted = lax.fori_loop(0, live_slots, one_slot, start_state)
        result = (
            (weighted / total[..., None])
            .transpose(1, 0, 2)
            .reshape(BLK, width)
            .astype(jnp.bfloat16)
        )
        return (carry, result)

    _, results = lax.scan(
        one_block, jnp.zeros((), jnp.int32), (query_blocks, block_lists, block_ids)
    )
    attended = results.reshape(count_blocks * BLK, width)
    regrouped = lax.all_to_all(attended, "head", split_axis=0, concat_axis=1, tiled=True)
    summed = jnp.dot(
        regrouped,
        lax.all_gather(w_out, "head", axis=0, tiled=True),
        preferred_element_type=jnp.float32,
    )
    return (resid + summed).astype(jnp.bfloat16)


def project_kernel(number, noted, unrolled, halved, place, *rest):
    pieces, rest = rest[:number], rest[number:]
    if halved:
        beside, rest = rest[0], rest[1:]
    if noted:
        note, rest = rest[0], rest[1:]
    own, other, cosine, sine = rest[:4]
    outs, rest = rest[4:8], rest[8:]
    if halved:
        half = beside.shape[0] // 2
        (low, high), rest = rest[:2], rest[2:]
    rows, weights, results, row_sems, weight_sems, out_sems = rest[:6]
    count = rows.shape[0]
    half_copies, fetch_half = [], []
    if halved:
        staged = rest[6]
        fetch_half = [
            pltpu.make_async_copy(beside.at[pl.ds(half, half)], staged, row_sems.at[number])
        ]
        half_copies = [
            pltpu.make_async_copy(rows.at[pl.ds(0, half)], low, out_sems.at[4]),
            pltpu.make_async_copy(staged, high, out_sems.at[5]),
        ]
    row_copies, start = [], 0
    for i, ref in enumerate(pieces):
        size = ref.shape[0]
        row_copies.append(
            pltpu.make_async_copy(ref, rows.at[pl.ds(start, size)], row_sems.at[i])
        )
        start += size
    weight_copies = [
        pltpu.make_async_copy(
            ref.at[part],
            weights.at[w * 3 + part],
            weight_sems.at[w * 3 + part],
        )
        for w, ref in enumerate((own, other))
        for part in range(3)
    ]
    for copy in row_copies + weight_copies[:2] + fetch_half:
        copy.start()
    for copy in row_copies + fetch_half:
        copy.wait()
    for copy in half_copies:
        copy.start()
    query_scale = math.log2(math.e) / math.sqrt(HD)
    step = count // 2

    def out_copy(result, shift):
        return pltpu.make_async_copy(results.at[result], outs[shift], out_sems.at[shift])

    if noted:
        for result in range(4):
            results[result, count:, :] = note[...]

    for w in range(2):
        for part in range(3):
            weight_copies[w * 3 + part].wait()
            if w * 3 + part + 2 < 6:
                weight_copies[w * 3 + part + 2].start()

            def tile(i, carry, w=w, part=part):
                piece = pl.ds(pl.multiple_of(i * step, step), step)
                product = jnp.dot(
                    rows[piece], weights[w * 3 + part], preferred_element_type=jnp.float32
                )
                for h in range(2):
                    vector = product[:, h * HD : (h + 1) * HD]
                    if part < 2:
                        turned = pltpu.roll(vector, HD // 2, 1)
                        vector = vector * cosine[piece] + turned * sine[piece]
                    if part == 0:
                        vector = vector * query_scale
                    column = slice(part * HD, (part + 1) * HD)
                    results[w * 2 + h, piece, column] = vector.astype(jnp.bfloat16)
                return carry

            if unrolled:
                tile(0, 0)
                tile(1, 0)
            else:
                lax.fori_loop(0, 2, tile, 0)
        for h in range(2):
            for shift in range(4):

                @pl.when(place[shift] == w * 2 + h)
                def _(shift=shift, result=w * 2 + h):
                    out_copy(result, shift).start()

    for shift in range(4):
        out_copy(0, shift).wait()
    for copy in half_copies:
        copy.wait()


def project(place, pieces, own, other, cosine, sine, note, unrolled, beside):
    count = sum(piece.shape[0] for piece in pieces)
    number = len(pieces)
    width = own.shape[2]
    notes = [] if note is None else [note]
    extra = [] if beside is None else [beside]
    halves = [jax.ShapeDtypeStruct((count // 2, D), jnp.bfloat16)] * (2 * len(extra))
    full = count + sum(each.shape[0] for each in notes)
    any_space = pl.BlockSpec(memory_space=pl.ANY)
    vmem = pl.BlockSpec(memory_space=pltpu.VMEM)
    return pl.pallas_call(
        functools.partial(project_kernel, number, len(notes) > 0, unrolled, len(extra) > 0),
        out_shape=[jax.ShapeDtypeStruct((full, 3 * HD), jnp.bfloat16)] * 4 + halves,
        in_specs=[pl.BlockSpec(memory_space=pltpu.SMEM)]
        + [any_space] * (number + len(extra))
        + [vmem] * len(notes)
        + [any_space] * 2
        + [vmem] * 2,
        out_specs=[any_space] * (4 + len(halves)),
        scratch_shapes=[
            pltpu.VMEM((count, D), jnp.bfloat16),
            pltpu.VMEM((6, D, width), jnp.bfloat16),
            pltpu.VMEM((4, full, 3 * HD), jnp.bfloat16),
            pltpu.SemaphoreType.DMA((number + 1,)),
            pltpu.SemaphoreType.DMA((6,)),
            pltpu.SemaphoreType.DMA((6,)),
        ]
        + [pltpu.VMEM((count // 2, D), jnp.bfloat16)] * len(extra),
        compiler_params=pltpu.CompilerParams(vmem_limit_bytes=VMEM_LIMIT),
        cost_estimate=pl.CostEstimate(
            flops=2 * count * D * 6 * width, bytes_accessed=2 * 6 * D * width, transcendentals=0
        ),
        name="project_and_rotate",
    )(place, *pieces, *extra, *notes, own, other, cosine, sine)


def attend_kernel(mode, blocks_here, place, *refs):
    refs = list(refs)

    def take(number):
        taken = refs[:number]
        del refs[:number]
        return taken

    near, early, late = mode in ("near", "local"), mode == "early", mode == "late"
    steps = STEPS[mode]
    targets = {"near": (1, 2, 3), "local": (0,)}.get(mode, (0, 1, 2, 3))
    lists = take(4)
    have = (0, 2, 3) if early else (0, 1, 2, 3)
    here = {relative: take(4) for relative in have}
    there = {relative: take(4 if relative == 1 else 1) for relative in have}
    state = take(3) if late else []
    outs = take(3 if early else len(targets))
    if early:
        queries, tops, sums = outs
        rows, query_rows, values_t, item_q, item_k, table, sems = refs
    else:
        rows, query_rows, values_t, queries, tops, sums, item_q, item_k, table, sems = refs
    section, chip, core = place[0], place[1], place[2]
    rows_here = here[2][0].shape[0]
    tok = blocks_here * BLK
    slots = lists[0].shape[1]
    wide = 2 * TILE
    pair_blocks = blocks_here // 2
    total_blocks = 4 * pair_blocks
    own_pair = chip // 2
    pair = own_pair if near else 1 - own_pair
    parity = lax.rem(chip, 2)

    def fetches(relatives, with_queries, first):
        copies = []
        for shift in range(4):
            number, query_number = first + shift * 12, first + shift * 12 + 8
            for relative in relatives:
                owner = chip ^ relative
                source = lax.rem(section - shift + 4, 4)
                for far in range(2):
                    side = core if far == 0 else 1 - core
                    if far == 0:
                        ref = here[relative][shift]
                    elif relative == 1:
                        ref = there[relative][shift]
                    else:
                        ref = there[relative][0].at[shift]
                    start = source * tok + owner * (2 * rows_here) + side * rows_here
                    start = pl.multiple_of(start, rows_here)
                    copies.append(
                        pltpu.make_async_copy(
                            ref.at[pl.ds(0, rows_here), pl.ds(HD, 2 * HD)],
                            rows.at[pl.ds(start, rows_here)],
                            sems.at[number],
                        )
                    )
                    number += 1
                    if not with_queries or (relative < 2) != near:
                        continue
                    start = source * (tok // 2) + lax.rem(owner, 2) * (2 * rows_here)
                    start = pl.multiple_of(start + side * rows_here, rows_here)
                    copies.append(
                        pltpu.make_async_copy(
                            ref.at[pl.ds(0, rows_here), pl.ds(0, HD)],
                            query_rows.at[pl.ds(start, rows_here)],
                            sems.at[query_number],
                        )
                    )
                    query_number += 1
        return copies

    def key_block(block):
        return block // pair_blocks * blocks_here + pair * pair_blocks + lax.rem(block, pair_blocks)

    copies = fetches((0, 1) if late else have, not late, 0)
    state_copies = [
        pltpu.make_async_copy(ref, held, sems.at[48 + i])
        for i, (ref, held) in enumerate(zip(state, (queries, tops, sums)))
    ]
    for copy in copies + state_copies:
        copy.start()

    count = jnp.int32(0)
    for target in targets:
        block_list = lists[(4 - target) % 4]
        first_block = lax.rem(section + target, 4) * pair_blocks

        def note(local, count, block_list=block_list, first_block=first_block):
            def one(slot, count, local=local):
                source = block_list[pair * pair_blocks + local, slot]
                item_q[count] = first_block + local
                item_k[count] = source
                table[(first_block + local) * slots + slot] = source
                wanted = source >= 0
                if not near:
                    in_section = lax.rem(jnp.maximum(source, 0), blocks_here)
                    whole = (in_section // pair_blocks != own_pair) | (
                        lax.rem(in_section, pair_blocks) == parity * (pair_blocks - 1)
                    )
                    wanted = wanted & (whole if early else jnp.logical_not(whole))
                return count + wanted.astype(jnp.int32)

            if mode in ("early", "local"):
                return lax.fori_loop(1, slots, one, count)
            for slot in range(1, slots):
                count = one(slot, count)
            return count

        count = lax.fori_loop(0, pair_blocks, note, count)
    for extra in range(steps):
        item_q[count + extra] = total_blocks
        item_k[count + extra] = (own_pair if late else pair) * pair_blocks

    values_t[HD:, :] = jnp.ones((values_t.shape[0] - HD, values_t.shape[1]), jnp.bfloat16)
    if not late:
        queries[total_blocks] = jnp.zeros((wide, HD), jnp.bfloat16)
        tops[total_blocks] = jnp.zeros((8, wide), jnp.float32)
        sums[total_blocks] = jnp.zeros(sums.shape[1:], jnp.float32)

    lane = lax.broadcasted_iota(jnp.int32, (BLK, wide), 1)
    key_at = lax.broadcasted_iota(jnp.int32, (BLK, wide), 0)

    def query_place(local):
        middle = local == 1
        return jnp.where(middle, core * TILE, core * wide), jnp.where(middle, TILE, 0)

    def scores_of(source, query):
        at = pl.multiple_of(source * BLK, BLK)
        return lax.dot_general(
            rows[pl.ds(at, BLK), 0:HD],
            query,
            (((1,), (1,)), ((), ())),
            preferred_element_type=jnp.float32,
        )

    def weigh(source, weights):
        at = pl.multiple_of(source * BLK, BLK)
        return jnp.dot(
            values_t[:, pl.ds(at, BLK)],
            weights.astype(jnp.bfloat16),
            preferred_element_type=jnp.float32,
        )

    def masked(local, scores):
        offset, gap = query_place(local)
        query_at = offset + lane + jnp.where(lane >= TILE, gap, 0)
        return jnp.where(key_at <= query_at, scores, -jnp.inf)

    def diagonal(first):
        blocks = [first + local for local in range(pair_blocks)]
        scores = []
        for local, block in enumerate(blocks):
            offset, gap = query_place(local)
            start = pl.multiple_of(block * BLK + offset, TILE)
            later = pl.multiple_of(start + TILE + gap, TILE)
            query = jnp.concatenate(
                [query_rows[pl.ds(start, TILE)], query_rows[pl.ds(later, TILE)]], axis=0
            )
            queries[block] = query
            scores.append(scores_of(key_block(block), query))
        for local, (block, score) in enumerate(zip(blocks, scores)):
            score = masked(local, score)
            top = jnp.max(score, axis=0, keepdims=True)
            tops[block] = jnp.broadcast_to(top, (8, wide))
            sums[block] = weigh(key_block(block), jnp.exp2(score - top))

    def turn(first, number):
        for i in range(number):
            at = pl.multiple_of((first + i) * BLK, BLK)
            values_t[:HD, pl.ds(at, BLK)] = rows[pl.ds(at, BLK), HD : 2 * HD].T

    waits = 4 if late else 2 * len(have)

    def arrive(shift, carry):
        source = lax.rem(section - shift + 4, 4)
        for number in range(waits):
            pltpu.make_async_copy(
                rows.at[pl.ds(0, rows_here)],
                rows.at[pl.ds(0, rows_here)],
                sems.at[shift * 12 + number],
            ).wait()
        if late:
            turn(source * blocks_here + own_pair * pair_blocks, pair_blocks)
            return carry
        for number in range(4):
            pltpu.make_async_copy(
                query_rows.at[pl.ds(0, rows_here)],
                query_rows.at[pl.ds(0, rows_here)],
                sems.at[shift * 12 + 8 + number],
            ).wait()
        turn(source * blocks_here, blocks_here)
        if mode == "early":
            diagonal(source * pair_blocks)
        else:
            wanted = shift == 0 if mode == "local" else shift != 0
            pl.when(wanted)(lambda: diagonal(source * pair_blocks))
        return carry

    lax.fori_loop(0, 4, arrive, 0)
    for copy in state_copies:
        copy.wait()

    def below(step, carry):
        items = [step * steps + i for i in range(steps)]
        scores = scores_of(item_k[items[0]], queries[item_q[items[0]]])
        held = None
        for i, item in enumerate(items):
            if i + 1 < steps:
                ahead = scores_of(item_k[items[i + 1]], queries[item_q[items[i + 1]]])
            weights = jnp.exp2(scores - tops[item_q[item], 0:1]).astype(jnp.bfloat16)
            if held is not None:
                sums[item_q[items[i - 1]]] += weigh(item_k[items[i - 1]], held)
            held, scores = weights, ahead
        sums[item_q[items[-1]]] += weigh(item_k[items[-1]], held)
        return carry

    lax.fori_loop(0, (count + steps - 1) // steps, below, 0)
    if early:
        return

    def over_in(i, over):
        block = lax.rem(section * pair_blocks + targets[0] * pair_blocks + i, total_blocks)
        return jnp.maximum(over, jnp.where(sums[block, HD : HD + 1] < 2.0**100, 0.0, 1.0))

    number_blocks = len(targets) * pair_blocks
    over = lax.fori_loop(0, number_blocks, over_in, jnp.zeros((1, wide), jnp.float32))

    @pl.when(jnp.max(over) > 0)
    def _():
        if late:
            copies = fetches((2, 3), False, 0)
            for copy in copies:
                copy.start()
            for copy in copies:
                copy.wait()

            def turn_all(step, carry):
                turn(step * pair_blocks, pair_blocks)
                return carry

            lax.fori_loop(0, 8, turn_all, 0)

        def one_block(i, carry):
            block = lax.rem(section * pair_blocks + targets[0] * pair_blocks + i, total_blocks)
            home = key_block(block)
            query = queries[block]
            scores = masked(lax.rem(block, pair_blocks), scores_of(home, query))
            highest = jnp.max(scores, axis=0, keepdims=True)
            weighted = weigh(home, jnp.exp2(scores - highest))

            def one_slot(slot, state):
                highest, weighted = state
                source = table[block * slots + slot]
                scores = scores_of(jnp.maximum(source, 0), query)
                scores = jnp.where(source >= 0, scores, -jnp.inf)
                new_highest = jnp.maximum(highest, jnp.max(scores, axis=0, keepdims=True))
                weights = jnp.exp2(scores - new_highest)
                weighted = weighted * jnp.exp2(highest - new_highest)
                weighted = weighted + weigh(jnp.maximum(source, 0), weights)
                return (new_highest, weighted)

            _, sums[block] = lax.fori_loop(1, slots, one_slot, (highest, weighted))
            return carry

        lax.fori_loop(0, number_blocks, one_block, 0)

    for number, target in enumerate(targets):

        def leave(local, carry, number=number, target=target):
            block = lax.rem(section + target, 4) * pair_blocks + local
            result = (sums[block, 0:HD] / sums[block, HD : HD + 1]).T.astype(jnp.bfloat16)
            for part in range(2):
                tile = 2 * local + part
                upper = (tile >= 3).astype(jnp.int32)
                i = tile - 3 * upper
                which = upper ^ parity
                given = i == 2 - 2 * core
                if near:
                    where = jnp.where(given, 4 + which, which * 2 + i - core)
                else:
                    where = which * 3 + jnp.where(given, 2, i - core)
                outs[number][where] = result[part * TILE : (part + 1) * TILE]
            return carry

        lax.fori_loop(0, pair_blocks, leave, 0)


def attend(mode, place, lists, here, there, state=()):
    blocks_here, slots = lists[0].shape
    total_blocks = 2 * blocks_here
    tokens = 4 * blocks_here * BLK
    room = total_blocks * slots + STEPS[mode]
    pairs = total_blocks * slots // 4
    have = (0, 2, 3) if mode == "early" else (0, 1, 2, 3)
    pieces = [piece for relative in have for piece in here[relative]]
    pieces += [piece for relative in have for piece in there[relative]]
    sums = [
        jax.ShapeDtypeStruct((total_blocks + 1, 2 * TILE, HD), jnp.bfloat16),
        jax.ShapeDtypeStruct((total_blocks + 1, 8, 2 * TILE), jnp.float32),
        jax.ShapeDtypeStruct((total_blocks + 1, HD + 16, 2 * TILE), jnp.float32),
    ]
    if mode == "early":
        outs = sums
    else:
        number = {"late": 4, "near": 3, "local": 1}[mode]
        outs = [jax.ShapeDtypeStruct((blocks_here, TILE, HD), jnp.bfloat16)] * number
    held = [] if mode == "early" else [pltpu.VMEM(each.shape, each.dtype) for each in sums]
    return pl.pallas_call(
        functools.partial(attend_kernel, mode, blocks_here),
        out_shape=outs,
        in_specs=[pl.BlockSpec(memory_space=pltpu.SMEM)] * 5
        + [pl.BlockSpec(memory_space=pl.ANY)] * (len(pieces) + len(state)),
        out_specs=[pl.BlockSpec(memory_space=pltpu.VMEM)] * len(outs),
        scratch_shapes=[
            pltpu.VMEM((tokens, 2 * HD), jnp.bfloat16),
            pltpu.VMEM((tokens // 2, HD), jnp.bfloat16),
            pltpu.VMEM((HD + 16, tokens), jnp.bfloat16),
            *held,
            pltpu.SMEM((room,), jnp.int32),
            pltpu.SMEM((room,), jnp.int32),
            pltpu.SMEM((room,), jnp.int32),
            pltpu.SemaphoreType.DMA((51,)),
        ],
        compiler_params=pltpu.CompilerParams(vmem_limit_bytes=ATTEND_LIMIT),
        cost_estimate=pl.CostEstimate(
            flops=pairs * 4 * BLK * 2 * TILE * HD,
            bytes_accessed=tokens * 5 * HD,
            transcendentals=pairs * BLK * 2 * TILE,
        ),
        name="attend_" + mode,
    )(place, *lists, *pieces, *state)


def finish_kernel(relatives, kept_parts, place, *rest):
    number = len(relatives)
    kept = []
    for parts in kept_parts:
        kept.append(rest[:parts])
        rest = rest[parts:]
    given, rest = rest[:number], rest[number:]
    w_out, hidden, out, attended, weights, sums, sems, given_sems, weight_sems = rest
    section, chip, core = place[0], place[1], place[2]
    odd = lax.rem(chip, 2)
    depth = 4 * HD
    copies = []
    for r, relative in enumerate(relatives):
        start = pl.multiple_of((chip ^ relative) * depth, depth)
        group = [
            pltpu.make_async_copy(w_out.at[pl.ds(start, depth)], weights.at[r], weight_sems.at[r])
        ]
        for shift in range(4):
            head = lax.rem(section - shift + 4, 4)
            column = pl.ds(pl.multiple_of(head * HD, HD), HD)
            for slot in range(2):
                to = jnp.where(core == 0, slot * (1 + odd), odd if slot == 0 else 2)
                source = kept[r][0].at[shift] if kept_parts[r] == 1 else kept[r][shift]
                group.append(
                    pltpu.make_async_copy(
                        source.at[slot],
                        attended.at[r, pl.ds(pl.multiple_of(to * TILE, TILE), TILE), column],
                        sems.at[(r * 4 + shift) * 2 + slot],
                    )
                )
            to = jnp.where(core == 0, 2 - odd, 1 - odd)
            group.append(
                pltpu.make_async_copy(
                    given[r].at[shift, 0],
                    attended.at[r, pl.ds(pl.multiple_of(to * TILE, TILE), TILE), column],
                    given_sems.at[r * 4 + shift],
                )
            )
        copies.append(group)
    for copy in copies[0] + copies[1]:
        copy.start()
    half = out.shape[0] // 2
    step = 512
    for r in range(number):
        for copy in copies[r]:
            copy.wait()
        if r + 2 < number:
            for copy in copies[r + 2]:
                copy.start()

        def columns(i, carry, r=r):
            column = pl.ds(pl.multiple_of(i * step, step), step)
            for at in range(0, out.shape[0], half):
                piece = (slice(at, at + half), column)
                summed = jnp.dot(
                    attended[r, at : at + half],
                    weights[r, :, column],
                    preferred_element_type=jnp.float32,
                )
                summed = summed + (hidden[piece].astype(jnp.float32) if r == 0 else sums[piece])
                if r + 1 < number:
                    sums[piece] = summed
                else:
                    out[piece] = summed.astype(out.dtype)
            return carry

        for i in range(out.shape[1] // step):
            columns(i, 0)


def finish(relatives, place, kept, given, w_out, hidden):
    count = hidden.shape[0]
    number = len(relatives)
    any_space = pl.BlockSpec(memory_space=pl.ANY)
    vmem = pl.BlockSpec(memory_space=pltpu.VMEM)
    depth = 4 * HD
    return pl.pallas_call(
        functools.partial(finish_kernel, relatives, [len(parts) for parts in kept]),
        out_shape=jax.ShapeDtypeStruct((count, D), jnp.bfloat16),
        in_specs=[pl.BlockSpec(memory_space=pltpu.SMEM)]
        + [any_space] * (sum(map(len, kept)) + number + 1)
        + [vmem],
        out_specs=vmem,
        scratch_shapes=[
            pltpu.VMEM((number, count, depth), jnp.bfloat16),
            pltpu.VMEM((number, depth, D), jnp.bfloat16),
            pltpu.VMEM((count, D), jnp.float32),
            pltpu.SemaphoreType.DMA((number * 8,)),
            pltpu.SemaphoreType.DMA((number * 4,)),
            pltpu.SemaphoreType.DMA((number,)),
        ],
        compiler_params=pltpu.CompilerParams(vmem_limit_bytes=VMEM_LIMIT),
        cost_estimate=pl.CostEstimate(
            flops=2 * count * D * D, bytes_accessed=2 * D * D, transcendentals=0
        ),
        name="project_out",
    )(place, *[part for parts in kept for part in parts], *given, w_out, hidden)


def by_head(hidden_in, norm_gain, w_qkv, w_out, block_lists):
    section = lax.axis_index("section")
    device = lax.axis_index("head")
    chip, core = device // 2, device % 2
    blocks_here = block_lists.shape[0]
    tok = blocks_here * BLK
    rows = hidden_in.shape[0]
    half = rows // 2

    other_core = [(i, i ^ 1) for i in range(8)]
    along_x = [(i, i ^ 2) for i in range(8)]
    along_y = [(i, i ^ 4) for i in range(8)]

    def to_section(array, shift):
        return lax.ppermute(array, "section", [(i, (i + shift) % 4) for i in range(4)])

    place = jnp.stack([section, chip, core]).astype(jnp.int32)
    shifts = jnp.arange(4, dtype=jnp.int32)
    chosen = (section + shifts - 2 * core + 4) % 4

    own = jnp.transpose(w_qkv, (1, 0, 2))
    other = lax.ppermute(own, "head", other_core)
    hidden_in, own = lax.optimization_barrier((hidden_in, own))

    resid = hidden_in.astype(jnp.float32)
    normed = (
        resid * lax.rsqrt(jnp.mean(resid * resid, axis=-1, keepdims=True) + EPS) * norm_gain
    ).astype(jnp.bfloat16)
    y_rows = lax.ppermute(normed, "head", along_y)
    x_rows = lax.ppermute(normed, "head", along_x)

    frequency = THETA ** (-(2.0 * jnp.arange(HD // 2, dtype=jnp.float32)) / HD)

    def projected(relatives, pieces, note=None, unrolled=False, beside=None, base=None):
        starts = (section if base is None else base) * tok + (chip ^ jnp.array(relatives)) * (2 * rows) + core * rows
        positions = (starts[:, None] + jnp.arange(rows, dtype=jnp.int32)[None, :]).reshape(-1)
        angle = positions.astype(jnp.float32)[:, None] * frequency
        cosine, sine = jnp.cos(angle), jnp.sin(angle)
        cosine = jnp.concatenate([cosine, cosine], axis=-1)
        sine = jnp.concatenate([-sine, sine], axis=-1)
        return project(chosen, pieces, own, other, cosine, sine, note, unrolled, beside)

    def sent(outs):
        return [outs[0]] + [to_section(outs[shift], shift) for shift in range(1, 4)]

    def to_other(array):
        return lax.ppermute(array, "head", other_core)

    def after(first, second):
        joined = lax.optimization_barrier((*first, *second))
        return list(joined[: len(first)]), list(joined[len(first) :])

    note = jnp.pad(
        block_lists.astype(jnp.bfloat16),
        ((0, 16 - blocks_here), (0, 3 * HD - block_lists.shape[1])),
    )
    own_outs = projected([0], [normed], note, True)
    own_outs, (base,) = after(own_outs, [section])
    own_parts = sent(own_outs)
    *y_outs, y_low, x_high = projected([2], [y_rows], None, True, x_rows, base)
    own_parts, held = after(own_parts, [x_high, y_low, *y_outs])
    x_high, y_low, *y_outs = held
    d_low = lax.ppermute(y_low, "head", along_x)
    d_high = lax.ppermute(x_high, "head", along_y)
    y_parts = sent(y_outs)
    d_outs = projected([3], [d_low, d_high], base=base)
    y_parts, held = after(y_parts, [w_out, x_rows, *d_outs])
    w_out, x_rows, *d_outs = held
    lists = [block_lists] + [
        part[rows : rows + blocks_here, : block_lists.shape[1]].astype(jnp.int32)
        for part in own_parts[1:]
    ]
    w_out_all = lax.all_gather(w_out, "head", axis=0, tiled=True)
    d_parts = sent(d_outs)
    d_parts, x_outs = after(d_parts, projected([1], [x_rows], base=base))
    x_parts = sent(x_outs)

    here = {0: own_parts, 1: x_parts, 2: y_parts, 3: d_parts}
    there = {relative: [to_other(jnp.stack(here[relative]))] for relative in (0, 2, 3)}
    state = attend("early", place, lists, here, there)
    x_parts, state = after(x_parts, state)
    here[1], there[1] = x_parts, [to_other(part) for part in x_parts]

    def to_chip(array, relative, cross):
        flip = 2 * relative + (1 if cross else 0)
        return lax.ppermute(array, "head", [(i, i ^ flip) for i in range(8)])

    far = attend("late", place, lists, here, there, state)
    far = [far[0]] + [to_section(far[shift], shift) for shift in range(1, 4)]
    near = attend("near", place, lists, here, there)
    near, (place, *far) = after(near, [place, *far])
    y_part = to_chip(jnp.stack([part[0:3] for part in far]), 2, False)
    d_part = to_chip(jnp.stack([part[3:6] for part in far]), 3, False)
    near = [to_section(near[shift - 1], shift) for shift in range(1, 4)]
    near = [*attend("local", place, lists, here, there), *near]
    swapped = to_other(jnp.stack([y_part[:, 2:3], d_part[:, 2:3]]))
    x_kept = to_chip(jnp.stack([part[2:4] for part in near]), 1, False)
    x_given = to_chip(jnp.stack([part[5:6] for part in near]), 1, True)
    own_given = to_other(jnp.stack([part[4:5] for part in near]))
    kept = [near, [x_kept], [y_part], [d_part]]
    given = [own_given, x_given, swapped[0], swapped[1]]
    return finish((0, 1, 2, 3), place, kept, given, w_out_all, hidden_in)


def solution(mesh):
    placed = (
        P(("section", "head"), None),
        P(),
        P(None, None, "head"),
        P("head", None),
        P("section", None),
    )

    def local(hidden_in, norm_gain, w_qkv, w_out, block_lists):
        fits = (
            mesh.shape["section"] == 4
            and mesh.shape["head"] == 8
            and w_qkv.shape[2] == 2 * HD
            and block_lists.shape[0] == 6
            and hidden_in.shape[0] == 3 * TILE
        )
        form = by_head if fits else general
        return form(hidden_in, norm_gain, w_qkv, w_out, block_lists)

    return jax.shard_map(
        local, mesh=mesh, in_specs=placed, out_specs=P(("section", "head"), None), check_vma=False
    )
```

```python
import functools
import math

import jax
import jax.numpy as jnp
from jax import lax
from jax.experimental import pallas as pl
from jax.experimental.pallas import tpu as pltpu
from jax.sharding import PartitionSpec as P

D = 2048
HD = 128
BLK = 512
TILE = 128
STEPS = {"early": 4, "late": 8, "near": 12, "local": 3}


EPS = 1e-05
THETA = 10000.0
VMEM_LIMIT = 56 * 1024 * 1024
ATTEND_LIMIT = 32 * 1024 * 1024


def rotate(vectors, cosine, sine):
    half = vectors.shape[-1] // 2
    first = vectors[..., :half]
    second = vectors[..., half:]
    return jnp.concatenate(
        [first * cosine - second * sine, second * cosine + first * sine], axis=-1
    )


def general(hidden_in, norm_gain, w_qkv, w_out, block_lists):
    section_id = lax.axis_index("section")
    width = w_qkv.shape[2]
    heads_here = width // HD
    blocks_here = block_lists.shape[0]
    tok_dev = blocks_here * BLK
    scale = 1.0 / math.sqrt(HD)
    resid = hidden_in.astype(jnp.float32)
    normed = (
        resid * lax.rsqrt(jnp.mean(resid * resid, axis=-1, keepdims=True) + EPS) * norm_gain
    ).astype(jnp.bfloat16)
    flat_weight = w_qkv.reshape(D, 3 * width)
    frequency = THETA ** (-(2.0 * jnp.arange(HD // 2, dtype=jnp.float32)) / HD)
    piece = lax.all_gather(normed, "head", axis=0, tiled=True)
    count = piece.shape[0]
    mixed_rows = jnp.dot(piece, flat_weight, preferred_element_type=jnp.float32).reshape(
        count, 3, heads_here, HD
    )
    positions = (section_id * tok_dev + jnp.arange(count, dtype=jnp.int32)).astype(jnp.float32)
    angle = positions[:, None] * frequency[None, :]
    cosine = jnp.cos(angle)[:, None, :]
    sine = jnp.sin(angle)[:, None, :]
    query = rotate(mixed_rows[:, 0], cosine, sine).astype(jnp.bfloat16).reshape(count, width)
    keys = rotate(mixed_rows[:, 1], cosine, sine).astype(jnp.bfloat16).reshape(count, width)
    values = mixed_rows[:, 2].astype(jnp.bfloat16).reshape(count, width)
    keys_all, values_all = (
        lax.all_gather(keys, "section", axis=0, tiled=True),
        lax.all_gather(values, "section", axis=0, tiled=True),
    )
    count_blocks = block_lists.shape[0]
    query_blocks = query.reshape(count_blocks, BLK, heads_here, HD)
    block_ids = section_id * blocks_here + jnp.arange(count_blocks, dtype=jnp.int32)

    def one_block(carry, item):
        query_block, block_row, block_id = item
        live_slots = jnp.sum((block_row >= 0).astype(jnp.int32))
        query_positions = block_id * BLK + jnp.arange(BLK, dtype=jnp.int32)

        def one_slot(slot, state):
            highest, total, weighted = state
            source = block_row[slot]
            key_block = lax.dynamic_slice_in_dim(keys_all, source * BLK, BLK, 0).reshape(
                BLK, heads_here, HD
            )
            value_block = lax.dynamic_slice_in_dim(values_all, source * BLK, BLK, 0).reshape(
                BLK, heads_here, HD
            )
            scores = (
                jnp.einsum(
                    "qhd,khd->hqk", query_block, key_block, preferred_element_type=jnp.float32
                )
                * scale
            )
            key_positions = source * BLK + jnp.arange(BLK, dtype=jnp.int32)
            scores = jnp.where(
                key_positions[None, None, :] <= query_positions[None, :, None], scores, -jnp.inf
            )
            new_highest = jnp.maximum(highest, jnp.max(scores, axis=-1))
            factor = jnp.exp(highest - new_highest)
            weights = jnp.exp(scores - new_highest[..., None])
            total = total * factor + jnp.sum(weights, axis=-1)
            update = jnp.einsum(
                "hqk,khd->hqd",
                weights.astype(jnp.bfloat16),
                value_block,
                preferred_element_type=jnp.float32,
            )
            weighted = weighted * factor[..., None] + update
            return (new_highest, total, weighted)

        start_state = (
            jnp.full((heads_here, BLK), -jnp.inf, jnp.float32),
            jnp.zeros((heads_here, BLK), jnp.float32),
            jnp.zeros((heads_here, BLK, HD), jnp.float32),
        )
        highest, total, weighted = lax.fori_loop(0, live_slots, one_slot, start_state)
        result = (
            (weighted / total[..., None])
            .transpose(1, 0, 2)
            .reshape(BLK, width)
            .astype(jnp.bfloat16)
        )
        return (carry, result)

    _, results = lax.scan(
        one_block, jnp.zeros((), jnp.int32), (query_blocks, block_lists, block_ids)
    )
    attended = results.reshape(count_blocks * BLK, width)
    regrouped = lax.all_to_all(attended, "head", split_axis=0, concat_axis=1, tiled=True)
    summed = jnp.dot(
        regrouped,
        lax.all_gather(w_out, "head", axis=0, tiled=True),
        preferred_element_type=jnp.float32,
    )
    return (resid + summed).astype(jnp.bfloat16)


def project_kernel(number, noted, unrolled, halved, place, *rest):
    pieces, rest = rest[:number], rest[number:]
    if halved:
        beside, rest = rest[0], rest[1:]
    if noted:
        note, rest = rest[0], rest[1:]
    own, other, cosine, sine = rest[:4]
    outs, rest = rest[4:8], rest[8:]
    if halved:
        half = beside.shape[0] // 2
        (low, high), rest = rest[:2], rest[2:]
    rows, weights, results, row_sems, weight_sems, out_sems = rest[:6]
    count = rows.shape[0]
    half_copies, fetch_half = [], []
    if halved:
        staged = rest[6]
        fetch_half = [
            pltpu.make_async_copy(beside.at[pl.ds(half, half)], staged, row_sems.at[number])
        ]
        half_copies = [
            pltpu.make_async_copy(rows.at[pl.ds(0, half)], low, out_sems.at[4]),
            pltpu.make_async_copy(staged, high, out_sems.at[5]),
        ]
    row_copies, start = [], 0
    for i, ref in enumerate(pieces):
        size = ref.shape[0]
        row_copies.append(
            pltpu.make_async_copy(ref, rows.at[pl.ds(start, size)], row_sems.at[i])
        )
        start += size
    weight_copies = [
        pltpu.make_async_copy(
            ref.at[part],
            weights.at[w * 3 + part],
            weight_sems.at[w * 3 + part],
        )
        for w, ref in enumerate((own, other))
        for part in range(3)
    ]
    for copy in row_copies + weight_copies[:2] + fetch_half:
        copy.start()
    for copy in row_copies + fetch_half:
        copy.wait()
    for copy in half_copies:
        copy.start()
    query_scale = math.log2(math.e) / math.sqrt(HD)
    step = count // 2

    def out_copy(result, shift):
        return pltpu.make_async_copy(results.at[result], outs[shift], out_sems.at[shift])

    if noted:
        for result in range(4):
            results[result, count:, :] = note[...]

    for w in range(2):
        for part in range(3):
            weight_copies[w * 3 + part].wait()
            if w * 3 + part + 2 < 6:
                weight_copies[w * 3 + part + 2].start()

            def tile(i, carry, w=w, part=part):
                piece = pl.ds(pl.multiple_of(i * step, step), step)
                product = jnp.dot(
                    rows[piece], weights[w * 3 + part], preferred_element_type=jnp.float32
                )
                for h in range(2):
                    vector = product[:, h * HD : (h + 1) * HD]
                    if part < 2:
                        turned = pltpu.roll(vector, HD // 2, 1)
                        vector = vector * cosine[piece] + turned * sine[piece]
                    if part == 0:
                        vector = vector * query_scale
                    column = slice(part * HD, (part + 1) * HD)
                    results[w * 2 + h, piece, column] = vector.astype(jnp.bfloat16)
                return carry

            if unrolled:
                tile(0, 0)
                tile(1, 0)
            else:
                lax.fori_loop(0, 2, tile, 0)
        for h in range(2):
            for shift in range(4):

                @pl.when(place[shift] == w * 2 + h)
                def _(shift=shift, result=w * 2 + h):
                    out_copy(result, shift).start()

    for shift in range(4):
        out_copy(0, shift).wait()
    for copy in half_copies:
        copy.wait()


def project(place, pieces, own, other, cosine, sine, note, unrolled, beside):
    count = sum(piece.shape[0] for piece in pieces)
    number = len(pieces)
    width = own.shape[2]
    notes = [] if note is None else [note]
    extra = [] if beside is None else [beside]
    halves = [jax.ShapeDtypeStruct((count // 2, D), jnp.bfloat16)] * (2 * len(extra))
    full = count + sum(each.shape[0] for each in notes)
    any_space = pl.BlockSpec(memory_space=pl.ANY)
    vmem = pl.BlockSpec(memory_space=pltpu.VMEM)
    return pl.pallas_call(
        functools.partial(project_kernel, number, len(notes) > 0, unrolled, len(extra) > 0),
        out_shape=[jax.ShapeDtypeStruct((full, 3 * HD), jnp.bfloat16)] * 4 + halves,
        in_specs=[pl.BlockSpec(memory_space=pltpu.SMEM)]
        + [any_space] * (number + len(extra))
        + [vmem] * len(notes)
        + [any_space] * 2
        + [vmem] * 2,
        out_specs=[any_space] * (4 + len(halves)),
        scratch_shapes=[
            pltpu.VMEM((count, D), jnp.bfloat16),
            pltpu.VMEM((6, D, width), jnp.bfloat16),
            pltpu.VMEM((4, full, 3 * HD), jnp.bfloat16),
            pltpu.SemaphoreType.DMA((number + 1,)),
            pltpu.SemaphoreType.DMA((6,)),
            pltpu.SemaphoreType.DMA((6,)),
        ]
        + [pltpu.VMEM((count // 2, D), jnp.bfloat16)] * len(extra),
        compiler_params=pltpu.CompilerParams(vmem_limit_bytes=VMEM_LIMIT),
        cost_estimate=pl.CostEstimate(
            flops=2 * count * D * 6 * width, bytes_accessed=2 * 6 * D * width, transcendentals=0
        ),
        name="project_and_rotate",
    )(place, *pieces, *extra, *notes, own, other, cosine, sine)


def attend_kernel(mode, blocks_here, place, *refs):
    refs = list(refs)

    def take(number):
        taken = refs[:number]
        del refs[:number]
        return taken

    near, early, late = mode in ("near", "local"), mode == "early", mode == "late"
    steps = STEPS[mode]
    targets = {"near": (1, 2, 3), "local": (0,)}.get(mode, (0, 1, 2, 3))
    lists = take(4)
    have = (0, 2, 3) if early else (0, 1, 2, 3)
    here = {relative: take(4) for relative in have}
    there = {relative: take(4 if relative == 1 else 1) for relative in have}
    state = take(3) if late else []
    outs = take(3 if early else len(targets))
    if early:
        queries, tops, sums = outs
        rows, query_rows, values_t, item_q, item_k, table, sems = refs
    else:
        rows, query_rows, values_t, queries, tops, sums, item_q, item_k, table, sems = refs
    section, chip, core = place[0], place[1], place[2]
    rows_here = here[2][0].shape[0]
    tok = blocks_here * BLK
    slots = lists[0].shape[1]
    wide = 2 * TILE
    pair_blocks = blocks_here // 2
    total_blocks = 4 * pair_blocks
    own_pair = chip // 2
    pair = own_pair if near else 1 - own_pair
    parity = lax.rem(chip, 2)

    def fetches(relatives, with_queries, first):
        copies = []
        for shift in range(4):
            number, query_number = first + shift * 12, first + shift * 12 + 8
            for relative in relatives:
                owner = chip ^ relative
                source = lax.rem(section - shift + 4, 4)
                for far in range(2):
                    side = core if far == 0 else 1 - core
                    if far == 0:
                        ref = here[relative][shift]
                    elif relative == 1:
                        ref = there[relative][shift]
                    else:
                        ref = there[relative][0].at[shift]
                    start = source * tok + owner * (2 * rows_here) + side * rows_here
                    start = pl.multiple_of(start, rows_here)
                    copies.append(
                        pltpu.make_async_copy(
                            ref.at[pl.ds(0, rows_here), pl.ds(HD, 2 * HD)],
                            rows.at[pl.ds(start, rows_here)],
                            sems.at[number],
                        )
                    )
                    number += 1
                    if not with_queries or (relative < 2) != near:
                        continue
                    start = source * (tok // 2) + lax.rem(owner, 2) * (2 * rows_here)
                    start = pl.multiple_of(start + side * rows_here, rows_here)
                    copies.append(
                        pltpu.make_async_copy(
                            ref.at[pl.ds(0, rows_here), pl.ds(0, HD)],
                            query_rows.at[pl.ds(start, rows_here)],
                            sems.at[query_number],
                        )
                    )
                    query_number += 1
        return copies

    def key_block(block):
        return block // pair_blocks * blocks_here + pair * pair_blocks + lax.rem(block, pair_blocks)

    copies = fetches((0, 1) if late else have, not late, 0)
    state_copies = [
        pltpu.make_async_copy(ref, held, sems.at[48 + i])
        for i, (ref, held) in enumerate(zip(state, (queries, tops, sums)))
    ]
    for copy in copies + state_copies:
        copy.start()

    count = jnp.int32(0)
    for target in targets:
        block_list = lists[(4 - target) % 4]
        first_block = lax.rem(section + target, 4) * pair_blocks

        def note(local, count, block_list=block_list, first_block=first_block):
            def one(slot, count, local=local):
                source = block_list[pair * pair_blocks + local, slot]
                item_q[count] = first_block + local
                item_k[count] = source
                table[(first_block + local) * slots + slot] = source
                wanted = source >= 0
                if not near:
                    in_section = lax.rem(jnp.maximum(source, 0), blocks_here)
                    whole = (in_section // pair_blocks != own_pair) | (
                        lax.rem(in_section, pair_blocks) == parity * (pair_blocks - 1)
                    )
                    wanted = wanted & (whole if early else jnp.logical_not(whole))
                return count + wanted.astype(jnp.int32)

            if mode in ("early", "local"):
                return lax.fori_loop(1, slots, one, count)
            for slot in range(1, slots):
                count = one(slot, count)
            return count

        count = lax.fori_loop(0, pair_blocks, note, count)
    for extra in range(steps):
        item_q[count + extra] = total_blocks
        item_k[count + extra] = (own_pair if late else pair) * pair_blocks

    values_t[HD:, :] = jnp.ones((values_t.shape[0] - HD, values_t.shape[1]), jnp.bfloat16)
    if not late:
        queries[total_blocks] = jnp.zeros((wide, HD), jnp.bfloat16)
        tops[total_blocks] = jnp.zeros((8, wide), jnp.float32)
        sums[total_blocks] = jnp.zeros(sums.shape[1:], jnp.float32)

    lane = lax.broadcasted_iota(jnp.int32, (BLK, wide), 1)
    key_at = lax.broadcasted_iota(jnp.int32, (BLK, wide), 0)

    def query_place(local):
        middle = local == 1
        return jnp.where(middle, core * TILE, core * wide), jnp.where(middle, TILE, 0)

    def scores_of(source, query):
        at = pl.multiple_of(source * BLK, BLK)
        return lax.dot_general(
            rows[pl.ds(at, BLK), 0:HD],
            query,
            (((1,), (1,)), ((), ())),
            preferred_element_type=jnp.float32,
        )

    def weigh(source, weights):
        at = pl.multiple_of(source * BLK, BLK)
        return jnp.dot(
            values_t[:, pl.ds(at, BLK)],
            weights.astype(jnp.bfloat16),
            preferred_element_type=jnp.float32,
        )

    def masked(local, scores):
        offset, gap = query_place(local)
        query_at = offset + lane + jnp.where(lane >= TILE, gap, 0)
        return jnp.where(key_at <= query_at, scores, -jnp.inf)

    def diagonal(first):
        blocks = [first + local for local in range(pair_blocks)]
        scores = []
        for local, block in enumerate(blocks):
            offset, gap = query_place(local)
            start = pl.multiple_of(block * BLK + offset, TILE)
            later = pl.multiple_of(start + TILE + gap, TILE)
            query = jnp.concatenate(
                [query_rows[pl.ds(start, TILE)], query_rows[pl.ds(later, TILE)]], axis=0
            )
            queries[block] = query
            scores.append(scores_of(key_block(block), query))
        for local, (block, score) in enumerate(zip(blocks, scores)):
            score = masked(local, score)
            top = jnp.max(score, axis=0, keepdims=True)
            tops[block] = jnp.broadcast_to(top, (8, wide))
            sums[block] = weigh(key_block(block), jnp.exp2(score - top))

    def turn(first, number):
        for i in range(number):
            at = pl.multiple_of((first + i) * BLK, BLK)
            values_t[:HD, pl.ds(at, BLK)] = rows[pl.ds(at, BLK), HD : 2 * HD].T

    waits = 4 if late else 2 * len(have)

    def arrive(shift, carry):
        source = lax.rem(section - shift + 4, 4)
        for number in range(waits):
            pltpu.make_async_copy(
                rows.at[pl.ds(0, rows_here)],
                rows.at[pl.ds(0, rows_here)],
                sems.at[shift * 12 + number],
            ).wait()
        if late:
            turn(source * blocks_here + own_pair * pair_blocks, pair_blocks)
            return carry
        for number in range(4):
            pltpu.make_async_copy(
                query_rows.at[pl.ds(0, rows_here)],
                query_rows.at[pl.ds(0, rows_here)],
                sems.at[shift * 12 + 8 + number],
            ).wait()
        turn(source * blocks_here, blocks_here)
        if mode == "early":
            diagonal(source * pair_blocks)
        else:
            wanted = shift == 0 if mode == "local" else shift != 0
            pl.when(wanted)(lambda: diagonal(source * pair_blocks))
        return carry

    lax.fori_loop(0, 4, arrive, 0)
    for copy in state_copies:
        copy.wait()

    def below(step, carry):
        items = [step * steps + i for i in range(steps)]
        scores = scores_of(item_k[items[0]], queries[item_q[items[0]]])
        held = None
        for i, item in enumerate(items):
            if i + 1 < steps:
                ahead = scores_of(item_k[items[i + 1]], queries[item_q[items[i + 1]]])
            weights = jnp.exp2(scores - tops[item_q[item], 0:1]).astype(jnp.bfloat16)
            if held is not None:
                sums[item_q[items[i - 1]]] += weigh(item_k[items[i - 1]], held)
            held, scores = weights, ahead
        sums[item_q[items[-1]]] += weigh(item_k[items[-1]], held)
        return carry

    lax.fori_loop(0, (count + steps - 1) // steps, below, 0)
    if early:
        return

    def over_in(i, over):
        block = lax.rem(section * pair_blocks + targets[0] * pair_blocks + i, total_blocks)
        return jnp.maximum(over, jnp.where(sums[block, HD : HD + 1] < 2.0**100, 0.0, 1.0))

    number_blocks = len(targets) * pair_blocks
    over = lax.fori_loop(0, number_blocks, over_in, jnp.zeros((1, wide), jnp.float32))

    @pl.when(jnp.max(over) > 0)
    def _():
        if late:
            copies = fetches((2, 3), False, 0)
            for copy in copies:
                copy.start()
            for copy in copies:
                copy.wait()

            def turn_all(step, carry):
                turn(step * pair_blocks, pair_blocks)
                return carry

            lax.fori_loop(0, 8, turn_all, 0)

        def one_block(i, carry):
            block = lax.rem(section * pair_blocks + targets[0] * pair_blocks + i, total_blocks)
            home = key_block(block)
            query = queries[block]
            scores = masked(lax.rem(block, pair_blocks), scores_of(home, query))
            highest = jnp.max(scores, axis=0, keepdims=True)
            weighted = weigh(home, jnp.exp2(scores - highest))

            def one_slot(slot, state):
                highest, weighted = state
                source = table[block * slots + slot]
                scores = scores_of(jnp.maximum(source, 0), query)
                scores = jnp.where(source >= 0, scores, -jnp.inf)
                new_highest = jnp.maximum(highest, jnp.max(scores, axis=0, keepdims=True))
                weights = jnp.exp2(scores - new_highest)
                weighted = weighted * jnp.exp2(highest - new_highest)
                weighted = weighted + weigh(jnp.maximum(source, 0), weights)
                return (new_highest, weighted)

            _, sums[block] = lax.fori_loop(1, slots, one_slot, (highest, weighted))
            return carry

        lax.fori_loop(0, number_blocks, one_block, 0)

    for number, target in enumerate(targets):

        def leave(local, carry, number=number, target=target):
            block = lax.rem(section + target, 4) * pair_blocks + local
            result = (sums[block, 0:HD] / sums[block, HD : HD + 1]).T.astype(jnp.bfloat16)
            for part in range(2):
                tile = 2 * local + part
                upper = (tile >= 3).astype(jnp.int32)
                i = tile - 3 * upper
                which = upper ^ parity
                given = i == 2 - 2 * core
                if near:
                    where = jnp.where(given, 4 + which, which * 2 + i - core)
                else:
                    where = which * 3 + jnp.where(given, 2, i - core)
                outs[number][where] = result[part * TILE : (part + 1) * TILE]
            return carry

        lax.fori_loop(0, pair_blocks, leave, 0)


def attend(mode, place, lists, here, there, state=()):
    blocks_here, slots = lists[0].shape
    total_blocks = 2 * blocks_here
    tokens = 4 * blocks_here * BLK
    room = total_blocks * slots + STEPS[mode]
    pairs = total_blocks * slots // 4
    have = (0, 2, 3) if mode == "early" else (0, 1, 2, 3)
    pieces = [piece for relative in have for piece in here[relative]]
    pieces += [piece for relative in have for piece in there[relative]]
    sums = [
        jax.ShapeDtypeStruct((total_blocks + 1, 2 * TILE, HD), jnp.bfloat16),
        jax.ShapeDtypeStruct((total_blocks + 1, 8, 2 * TILE), jnp.float32),
        jax.ShapeDtypeStruct((total_blocks + 1, HD + 16, 2 * TILE), jnp.float32),
    ]
    if mode == "early":
        outs = sums
    else:
        number = {"late": 4, "near": 3, "local": 1}[mode]
        outs = [jax.ShapeDtypeStruct((blocks_here, TILE, HD), jnp.bfloat16)] * number
    held = [] if mode == "early" else [pltpu.VMEM(each.shape, each.dtype) for each in sums]
    return pl.pallas_call(
        functools.partial(attend_kernel, mode, blocks_here),
        out_shape=outs,
        in_specs=[pl.BlockSpec(memory_space=pltpu.SMEM)] * 5
        + [pl.BlockSpec(memory_space=pl.ANY)] * (len(pieces) + len(state)),
        out_specs=[pl.BlockSpec(memory_space=pltpu.VMEM)] * len(outs),
        scratch_shapes=[
            pltpu.VMEM((tokens, 2 * HD), jnp.bfloat16),
            pltpu.VMEM((tokens // 2, HD), jnp.bfloat16),
            pltpu.VMEM((HD + 16, tokens), jnp.bfloat16),
            *held,
            pltpu.SMEM((room,), jnp.int32),
            pltpu.SMEM((room,), jnp.int32),
            pltpu.SMEM((room,), jnp.int32),
            pltpu.SemaphoreType.DMA((51,)),
        ],
        compiler_params=pltpu.CompilerParams(vmem_limit_bytes=ATTEND_LIMIT),
        cost_estimate=pl.CostEstimate(
            flops=pairs * 4 * BLK * 2 * TILE * HD,
            bytes_accessed=tokens * 5 * HD,
            transcendentals=pairs * BLK * 2 * TILE,
        ),
        name="attend_" + mode,
    )(place, *lists, *pieces, *state)


def finish_kernel(relatives, kept_parts, place, *rest):
    number = len(relatives)
    kept = []
    for parts in kept_parts:
        kept.append(rest[:parts])
        rest = rest[parts:]
    given, rest = rest[:number], rest[number:]
    w_out, hidden, out, attended, weights, sums, sems, given_sems, weight_sems = rest
    section, chip, core = place[0], place[1], place[2]
    odd = lax.rem(chip, 2)
    depth = 4 * HD
    copies = []
    for r, relative in enumerate(relatives):
        start = pl.multiple_of((chip ^ relative) * depth, depth)
        group = [
            pltpu.make_async_copy(w_out.at[pl.ds(start, depth)], weights.at[r], weight_sems.at[r])
        ]
        for shift in range(4):
            head = lax.rem(section - shift + 4, 4)
            column = pl.ds(pl.multiple_of(head * HD, HD), HD)
            for slot in range(2):
                to = jnp.where(core == 0, slot * (1 + odd), odd if slot == 0 else 2)
                source = kept[r][0].at[shift] if kept_parts[r] == 1 else kept[r][shift]
                group.append(
                    pltpu.make_async_copy(
                        source.at[slot],
                        attended.at[r, pl.ds(pl.multiple_of(to * TILE, TILE), TILE), column],
                        sems.at[(r * 4 + shift) * 2 + slot],
                    )
                )
            to = jnp.where(core == 0, 2 - odd, 1 - odd)
            group.append(
                pltpu.make_async_copy(
                    given[r].at[shift, 0],
                    attended.at[r, pl.ds(pl.multiple_of(to * TILE, TILE), TILE), column],
                    given_sems.at[r * 4 + shift],
                )
            )
        copies.append(group)
    for copy in copies[0] + copies[1]:
        copy.start()
    half = out.shape[0] // 2
    step = 512
    for r in range(number):
        for copy in copies[r]:
            copy.wait()
        if r + 2 < number:
            for copy in copies[r + 2]:
                copy.start()

        def columns(i, carry, r=r):
            column = pl.ds(pl.multiple_of(i * step, step), step)
            for at in range(0, out.shape[0], half):
                piece = (slice(at, at + half), column)
                summed = jnp.dot(
                    attended[r, at : at + half],
                    weights[r, :, column],
                    preferred_element_type=jnp.float32,
                )
                summed = summed + (hidden[piece].astype(jnp.float32) if r == 0 else sums[piece])
                if r + 1 < number:
                    sums[piece] = summed
                else:
                    out[piece] = summed.astype(out.dtype)
            return carry

        for i in range(out.shape[1] // step):
            columns(i, 0)


def finish(relatives, place, kept, given, w_out, hidden):
    count = hidden.shape[0]
    number = len(relatives)
    any_space = pl.BlockSpec(memory_space=pl.ANY)
    vmem = pl.BlockSpec(memory_space=pltpu.VMEM)
    depth = 4 * HD
    return pl.pallas_call(
        functools.partial(finish_kernel, relatives, [len(parts) for parts in kept]),
        out_shape=jax.ShapeDtypeStruct((count, D), jnp.bfloat16),
        in_specs=[pl.BlockSpec(memory_space=pltpu.SMEM)]
        + [any_space] * (sum(map(len, kept)) + number + 1)
        + [vmem],
        out_specs=vmem,
        scratch_shapes=[
            pltpu.VMEM((number, count, depth), jnp.bfloat16),
            pltpu.VMEM((number, depth, D), jnp.bfloat16),
            pltpu.VMEM((count, D), jnp.float32),
            pltpu.SemaphoreType.DMA((number * 8,)),
            pltpu.SemaphoreType.DMA((number * 4,)),
            pltpu.SemaphoreType.DMA((number,)),
        ],
        compiler_params=pltpu.CompilerParams(vmem_limit_bytes=VMEM_LIMIT),
        cost_estimate=pl.CostEstimate(
            flops=2 * count * D * D, bytes_accessed=2 * D * D, transcendentals=0
        ),
        name="project_out",
    )(place, *[part for parts in kept for part in parts], *given, w_out, hidden)


def by_head(hidden_in, norm_gain, w_qkv, w_out, block_lists):
    section = lax.axis_index("section")
    device = lax.axis_index("head")
    chip, core = device // 2, device % 2
    blocks_here = block_lists.shape[0]
    tok = blocks_here * BLK
    rows = hidden_in.shape[0]
    half = rows // 2

    other_core = [(i, i ^ 1) for i in range(8)]
    along_x = [(i, i ^ 2) for i in range(8)]
    along_y = [(i, i ^ 4) for i in range(8)]

    def to_section(array, shift):
        return lax.ppermute(array, "section", [(i, (i + shift) % 4) for i in range(4)])

    place = jnp.stack([section, chip, core]).astype(jnp.int32)
    shifts = jnp.arange(4, dtype=jnp.int32)
    chosen = (section + shifts - 2 * core + 4) % 4

    own = jnp.transpose(w_qkv, (1, 0, 2))
    other = lax.ppermute(own, "head", other_core)
    hidden_in, own = lax.optimization_barrier((hidden_in, own))

    resid = hidden_in.astype(jnp.float32)
    normed = (
        resid * lax.rsqrt(jnp.mean(resid * resid, axis=-1, keepdims=True) + EPS) * norm_gain
    ).astype(jnp.bfloat16)
    y_rows = lax.ppermute(normed, "head", along_y)
    x_rows = lax.ppermute(normed, "head", along_x)

    frequency = THETA ** (-(2.0 * jnp.arange(HD // 2, dtype=jnp.float32)) / HD)

    def projected(relatives, pieces, note=None, unrolled=False, beside=None, base=None):
        starts = (section if base is None else base) * tok + (chip ^ jnp.array(relatives)) * (2 * rows) + core * rows
        positions = (starts[:, None] + jnp.arange(rows, dtype=jnp.int32)[None, :]).reshape(-1)
        angle = positions.astype(jnp.float32)[:, None] * frequency
        cosine, sine = jnp.cos(angle), jnp.sin(angle)
        cosine = jnp.concatenate([cosine, cosine], axis=-1)
        sine = jnp.concatenate([-sine, sine], axis=-1)
        return project(chosen, pieces, own, other, cosine, sine, note, unrolled, beside)

    def sent(outs):
        return [outs[0]] + [to_section(outs[shift], shift) for shift in range(1, 4)]

    def to_other(array):
        return lax.ppermute(array, "head", other_core)

    def after(first, second):
        joined = lax.optimization_barrier((*first, *second))
        return list(joined[: len(first)]), list(joined[len(first) :])

    note = jnp.pad(
        block_lists.astype(jnp.bfloat16),
        ((0, 16 - blocks_here), (0, 3 * HD - block_lists.shape[1])),
    )
    own_outs = projected([0], [normed], note, True)
    own_outs, (base,) = after(own_outs, [section])
    own_parts = sent(own_outs)
    *y_outs, y_low, x_high = projected([2], [y_rows], None, True, x_rows, base)
    own_parts, held = after(own_parts, [x_high, y_low, *y_outs])
    x_high, y_low, *y_outs = held
    d_low = lax.ppermute(y_low, "head", along_x)
    d_high = lax.ppermute(x_high, "head", along_y)
    y_parts = sent(y_outs)
    d_outs = projected([3], [d_low, d_high], base=base)
    y_parts, held = after(y_parts, [w_out, x_rows, *d_outs])
    w_out, x_rows, *d_outs = held
    lists = [block_lists] + [
        part[rows : rows + blocks_here, : block_lists.shape[1]].astype(jnp.int32)
        for part in own_parts[1:]
    ]
    w_out_all = lax.all_gather(w_out, "head", axis=0, tiled=True)
    d_parts = sent(d_outs)
    d_parts, x_outs = after(d_parts, projected([1], [x_rows], base=base))
    x_parts = sent(x_outs)

    here = {0: own_parts, 1: x_parts, 2: y_parts, 3: d_parts}
    there = {relative: [to_other(jnp.stack(here[relative]))] for relative in (0, 2, 3)}
    state = attend("early", place, lists, here, there)
    x_parts, state = after(x_parts, state)
    here[1], there[1] = x_parts, [to_other(part) for part in x_parts]

    def to_chip(array, relative, cross):
        flip = 2 * relative + (1 if cross else 0)
        return lax.ppermute(array, "head", [(i, i ^ flip) for i in range(8)])

    far = attend("late", place, lists, here, there, state)
    far = [far[0]] + [to_section(far[shift], shift) for shift in range(1, 4)]
    near = attend("near", place, lists, here, there)
    near, (place, *far) = after(near, [place, *far])
    y_part = to_chip(jnp.stack([part[0:3] for part in far]), 2, False)
    d_part = to_chip(jnp.stack([part[3:6] for part in far]), 3, False)
    near = [to_section(near[shift - 1], shift) for shift in range(1, 4)]
    near = [*attend("local", place, lists, here, there), *near]
    swapped = to_other(jnp.stack([y_part[:, 2:3], d_part[:, 2:3]]))
    x_kept = to_chip(jnp.stack([part[2:4] for part in near]), 1, False)
    x_given = to_chip(jnp.stack([part[5:6] for part in near]), 1, True)
    own_given = to_other(jnp.stack([part[4:5] for part in near]))
    kept = [near, [x_kept], [y_part], [d_part]]
    given = [own_given, x_given, swapped[0], swapped[1]]
    return finish((0, 1, 2, 3), place, kept, given, w_out_all, hidden_in)


def solution(mesh):
    placed = (
        P(("section", "head"), None),
        P(),
        P(None, None, "head"),
        P("head", None),
        P("section", None),
    )

    def local(hidden_in, norm_gain, w_qkv, w_out, block_lists):
        fits = (
            mesh.shape["section"] == 4
            and mesh.shape["head"] == 8
            and w_qkv.shape[2] == 2 * HD
            and block_lists.shape[0] == 6
            and hidden_in.shape[0] == 3 * TILE
        )
        form = by_head if fits else general
        return form(hidden_in, norm_gain, w_qkv, w_out, block_lists)

    return jax.shard_map(
        local, mesh=mesh, in_specs=placed, out_specs=P(("section", "head"), None), check_vma=False
    )
```
